32 devices in a mesh: dp: 2 (over x), seq: 4 (over z), chan: 4 (over y, core).
Axes of the slice: x: 2, y: 2, z: 4, core: 2. Of those that a mesh axis runs over, the one named last changes fastest.
Arguments:
- tokens: bfloat16 [2, 4096, 1536], P('dp', 'seq'), may hold values from -6 to 6
- segment_ids: int32 [2, 4096], P('dp'), may hold values from 0 to 4095, as said below
- first_gain: bfloat16 [1536], replicated, may hold values from 0.5 to 1.5
- input_proj: bfloat16 [1536, 3072], P(None, 'chan'), may hold values from -0.15625 to 0.15625
- gate_proj: bfloat16 [1536, 3072], P(None, 'chan'), may hold values from -0.15625 to 0.15625
- conv_weight: bfloat16 [3072, 4], P('chan'), may hold values from -3 to 3
- conv_bias: bfloat16 [3072], P('chan'), may hold values from -3 to 3
- state_proj: bfloat16 [3072, 128], P('chan'), may hold values from -0.109375 to 0.109375
- step_proj: bfloat16 [96, 3072], P(None, 'chan'), may hold values from -0.625 to 0.625
- step_bias: bfloat16 [3072], P('chan'), may hold values from -6 to -2
- decay_log: bfloat16 [3072, 16], P('chan'), may hold values from -6 to 1
- skip_gain: bfloat16 [3072], P('chan'), may hold values from 0.5 to 1.5
- output_proj: bfloat16 [3072, 1536], P('chan'), may hold values from -0.3125 to 0.3125
- second_gain: bfloat16 [1536], replicated, may hold values from 0.5 to 1.5
- hidden_gate: bfloat16 [1536, 4096], P(None, 'chan'), may hold values from -0.15625 to 0.15625
- hidden_up: bfloat16 [1536, 4096], P(None, 'chan'), may hold values from -0.15625 to 0.15625
- hidden_down: bfloat16 [4096, 1536], P('chan'), may hold values from -0.1875 to 0.1875
- upstream: bfloat16 [2, 4096, 1536], P('dp', 'seq'), may hold values from -6 to 6
Outputs:
- result: bfloat16 [2, 4096, 1536], P('dp', 'seq')
- tokens_grad: float32 [2, 4096, 1536], P('dp', 'seq')
- first_gain_grad: float32 [1536], P(('dp', 'seq'))
- input_proj_grad: float32 [1536, 3072], P(('dp', 'seq'), 'chan')
- gate_proj_grad: float32 [1536, 3072], P(('dp', 'seq'), 'chan')
- conv_weight_grad: float32 [3072, 4], P('chan')
- conv_bias_grad: float32 [3072], P('chan')
- state_proj_grad: float32 [3072, 96], P('chan', ('dp', 'seq'))
- state_io_grad: float32 [3072, 32], P('chan')
- step_proj_grad: float32 [96, 3072], P(('dp', 'seq'), 'chan')
- step_bias_grad: float32 [3072], P('chan')
- decay_log_grad: float32 [3072, 16], P('chan')
- skip_gain_grad: float32 [3072], P('chan')
- output_proj_grad: float32 [3072, 1536], P('chan', ('dp', 'seq'))
- second_gain_grad: float32 [1536], P(('dp', 'seq'))
- hidden_gate_grad: float32 [1536, 4096], P(('dp', 'seq'), 'chan')
- hidden_up_grad: float32 [1536, 4096], P(('dp', 'seq'), 'chan')
- hidden_down_grad: float32 [4096, 1536], P('chan', ('dp', 'seq'))
The draws below stay inside these ranges and needn't reach their ends.
Inputs may be any that keep to these rules, and one draw needn't show every extreme that they name: `segment_ids`: each token's id is the position, within its sequence, of the last token of its document, so ids never fall along a sequence; token 0 is a document by itself; in every sequence one document covers tokens 1024 - 1 through 4096 - 1024.
All inputs are finite; a program needn't handle non-finite values.
Results may differ from the reference program's by a relative error of at most 0.019.
Values may be sent and summed in bfloat16 or wider, within the bound.
No kernel may reach another device: no remote copies, remote signals or barrier semaphores. Data moves between devices by JAX's collectives and lax.ppermute only.
A program may use at most 256 MiB of HBM per device.

```python
import jax
import jax.numpy as jnp
from jax import lax

D = 1536
E = 3072
N = 16
K = 4
R = 96
FF = 4096
TOK_DEV = 1024
SEQS = 2
LEN = 4096


def draw_segment_ids(key, part):
    key = jax.random.fold_in(key, 11)
    keys = jax.random.split(key, 4)
    first = jax.random.randint(keys[0], (SEQS, 1), 1, TOK_DEV)
    last = jax.random.randint(keys[1], (SEQS, 1), LEN - TOK_DEV + 1, LEN)
    position = jnp.arange(LEN, dtype=jnp.int32)[None, :]
    picks = jax.random.randint(keys[2], (SEQS, LEN // 16), 0, 3)
    spacing = jnp.where(picks == 0, 4, jnp.where(picks == 1, 32, 256))
    spacing = jnp.repeat(spacing, 16, axis=1)
    coins = jax.random.randint(keys[3], (SEQS, LEN), 0, 1 << 20)
    starts = coins % spacing == 0
    inside = (position > first) & (position < last)
    starts = starts & jnp.logical_not(inside) | (position == first) | (position == last) | (position == 0) | (position == 1)
    marked = jnp.where(starts, position, LEN).astype(jnp.int32)
    following = lax.cummin(marked, axis=1, reverse=True)
    tail = jnp.full((SEQS, 1), LEN, jnp.int32)
    next_start = jnp.concatenate([following[:, 1:], tail], axis=1)
    return (next_start - 1).astype(jnp.int32)


def steps_of(rng, extent, pieces, smallest, top_value):
    level = 1.0
    for dim, shards_of in pieces:
        steps = jax.random.uniform(jax.random.fold_in(jax.random.fold_in(rng, 6), dim), (shards_of,), jnp.float32, smallest / len(pieces), top_value / len(pieces))
        level = level * jnp.repeat(jnp.exp(steps), extent[dim] // shards_of).reshape((-1,) + (1,) * (len(extent) - 1 - dim))
    return level


def normal_values(stream_key, extent, spread, most, cuts=(), held_as=jnp.bfloat16):
    array = spread * jax.random.normal(stream_key, extent, jnp.float32)
    if cuts:
        array = array * steps_of(stream_key, extent, cuts, -0.22, 0.18)
    return jnp.clip(array, -most, most).astype(held_as)


def setup_inputs(seed: int = 0) -> dict:
    streams_of = jax.random.split(jax.random.key(seed), 19)
    tokens = normal_values(streams_of[0], (SEQS, LEN, D), 1.0, 6.0, ((0, 2), (1, 4)))
    segment_ids = draw_segment_ids(jax.random.fold_in(streams_of[18], 71), 0)
    first_gain = jnp.clip(1.0 + 0.1 * jax.random.normal(streams_of[2], (D,), jnp.float32), 0.5, 1.5).astype(jnp.bfloat16)
    input_proj = normal_values(streams_of[3], (D, E), D ** -0.5, 0.15625, ((1, 4),))
    gate_proj = normal_values(streams_of[4], (D, E), D ** -0.5, 0.15625, ((1, 4),))
    conv_weight = normal_values(streams_of[5], (E, K), K ** -0.5, 3.0, ((0, 4),))
    conv_bias = normal_values(streams_of[6], (E,), 0.5, 3.0, ((0, 4),))
    state_proj = normal_values(streams_of[7], (E, R + 2 * N), E ** -0.5, 0.109375, ((0, 4),))
    step_proj = normal_values(streams_of[8], (R, E), R ** -0.5, 0.625, ((1, 4),))
    step_bias = jnp.clip(-6.0 + 4.0 * jax.random.uniform(streams_of[9], (E,), jnp.float32) ** steps_of(streams_of[9], (E,), ((0, 4),), -0.2, 0.2), -6.0, -2.0).astype(jnp.bfloat16)
    decay_log = jnp.clip(-6.0 + 7.0 * jax.random.uniform(streams_of[10], (E, N), jnp.float32) ** steps_of(streams_of[10], (E, N), ((0, 4),), -0.2, 0.2), -6.0, 1.0).astype(jnp.bfloat16)
    skip_gain = jnp.clip(0.5 + 1.0 * jax.random.uniform(streams_of[11], (E,), jnp.float32) ** steps_of(streams_of[11], (E,), ((0, 4),), -0.2, 0.2), 0.5, 1.5).astype(jnp.bfloat16)
    output_proj = normal_values(streams_of[12], (E, D), (E // 8) ** -0.5, 0.3125, ((0, 4),))
    second_gain = jnp.clip(1.0 + 0.1 * jax.random.normal(streams_of[13], (D,), jnp.float32), 0.5, 1.5).astype(jnp.bfloat16)
    hidden_gate = normal_values(streams_of[14], (D, FF), D ** -0.5, 0.15625, ((1, 4),))
    hidden_up = normal_values(streams_of[15], (D, FF), D ** -0.5, 0.15625, ((1, 4),))
    hidden_down = normal_values(streams_of[16], (FF, D), (FF // 4) ** -0.5, 0.1875, ((0, 4),))
    upstream = normal_values(streams_of[17], (SEQS, LEN, D), 1.0, 6.0, ((0, 2), (1, 4)))
    return dict(tokens=tokens, segment_ids=segment_ids, first_gain=first_gain, input_proj=input_proj, gate_proj=gate_proj, conv_weight=conv_weight, conv_bias=conv_bias, state_proj=state_proj, step_proj=step_proj, step_bias=step_bias, decay_log=decay_log, skip_gain=skip_gain, output_proj=output_proj, second_gain=second_gain, hidden_gate=hidden_gate, hidden_up=hidden_up, hidden_down=hidden_down, upstream=upstream)


epsilon = 1e-05
highest = lax.Precision.HIGHEST
block_span = 16

@jax.custom_vjp
def low(v):
    return lax.optimization_barrier(v.astype(jnp.bfloat16)).astype(jnp.float32)

@jax.custom_vjp
def low_back(v):
    return v

def low_keep(v):
    return (low(v), None)

def low_pass(kept, grad):
    return (grad,)

def back_keep(v):
    return (v, None)

def back_low(kept, grad):
    return (low(grad),)
low.defvjp(low_keep, low_pass)
low_back.defvjp(back_keep, back_low)

def matmul(left, right):
    return jnp.dot(left, right, precision=highest, preferred_element_type=jnp.float32)

def rms_norm(values, gain):
    scale = lax.rsqrt(lax.optimization_barrier(jnp.mean(values * values, axis=-1, keepdims=True)) + epsilon)
    return values * scale * gain

def causal_conv(inner, taps, offset_bias, segment):
    length = inner.shape[0]
    padded = jnp.concatenate([jnp.zeros((K - 1, inner.shape[1]), jnp.float32), inner], axis=0)
    padded_ids = jnp.concatenate([jnp.full((K - 1,), -1, jnp.int32), segment], axis=0)
    total = jnp.zeros_like(inner) + offset_bias
    for offset in range(K):
        same = (padded_ids[offset:offset + length] == segment).astype(jnp.float32)
        total = total + padded[offset:offset + length] * taps[:, offset] * same[:, None]
    return total

def selective_scan(decay, rates, mixed, entry, readout, keep):

    def token_step(state, items):
        rate_row, mixed_row, entry_row, readout_row, keep_row = items
        factor = jnp.exp(rate_row[None, :] * decay) * keep_row
        state = factor * state + (rate_row * mixed_row)[None, :] * entry_row[:, None]
        return (state, lax.optimization_barrier(jnp.sum(readout_row[:, None] * state, axis=0)))

    def block_step(state, block):
        return lax.scan(token_step, state, block)
    blocks = tuple((item.reshape((item.shape[0] // block_span, block_span) + item.shape[1:]) for item in (rates, mixed, entry, readout, keep)))
    initial = jnp.zeros(decay.shape, jnp.float32)
    unused, outputs = lax.scan(jax.checkpoint(block_step), initial, blocks)
    return outputs.reshape(rates.shape)

def block_forward(weights, rows, segment):
    first_gain, input_proj, gate_proj, conv_weight, conv_bias, state_proj, step_proj, step_bias, decay_log, skip_gain, output_proj, second_gain, hidden_gate, hidden_up, hidden_down = weights
    normed = low(rms_norm(rows, first_gain))
    inner = low(low_back(matmul(normed, input_proj)))
    gate_in = low_back(matmul(normed, gate_proj))
    mixed = low(jax.nn.silu(causal_conv(inner, conv_weight, conv_bias, segment)))
    projected = low_back(matmul(mixed, state_proj))
    step_low = low(projected[:, :R])
    entry = projected[:, R:R + N]
    readout = projected[:, R + N:]
    rates = jax.nn.softplus(low_back(matmul(step_low, step_proj)) + step_bias)
    previous = jnp.concatenate([jnp.full((1,), -1, jnp.int32), segment[:-1]], axis=0)
    keep = (previous == segment).astype(jnp.float32)
    decay = -jnp.exp(decay_log).T
    scanned = selective_scan(decay, rates, mixed, entry, readout, keep)
    gated = low((scanned + skip_gain * mixed) * jax.nn.silu(gate_in))
    hidden_one = rows + low_back(matmul(gated, output_proj))
    normed_two = low(rms_norm(hidden_one, second_gain))
    gate_ffn = low_back(matmul(normed_two, hidden_gate))
    up_ffn = low_back(matmul(normed_two, hidden_up))
    active = low(jax.nn.silu(gate_ffn) * up_ffn)
    return hidden_one + low_back(matmul(active, hidden_down))

def reference(tokens, segment_ids, first_gain, input_proj, gate_proj, conv_weight, conv_bias, state_proj, step_proj, step_bias, decay_log, skip_gain, output_proj, second_gain, hidden_gate, hidden_up, hidden_down, upstream):
    weights = tuple((item.astype(jnp.float32) for item in (first_gain, input_proj, gate_proj, conv_weight, conv_bias, state_proj, step_proj, step_bias, decay_log, skip_gain, output_proj, second_gain, hidden_gate, hidden_up, hidden_down)))

    def per_sequence(totals, items):
        rows, segment, cotangent = items

        def forward(inputs, params):
            return block_forward(params, inputs, segment)
        output, pullback = jax.vjp(forward, rows.astype(jnp.float32), weights)
        rows_grad, weight_grads = pullback(cotangent.astype(jnp.float32))
        totals = tuple((total + update for total, update in zip(totals, weight_grads)))
        return (totals, (output.astype(jnp.bfloat16), rows_grad))
    zeros = tuple((jnp.zeros_like(item) for item in weights))
    totals, (results, rows_grads) = lax.scan(per_sequence, zeros, (tokens, segment_ids, upstream))
    return (results, rows_grads, totals[0], totals[1], totals[2], totals[3], totals[4], totals[5][:, :R], totals[5][:, R:], totals[6], totals[7], totals[8], totals[9], totals[10], totals[11], totals[12], totals[13], totals[14])
```

```python
import functools

import jax
import jax.numpy as jnp
from jax import lax
from jax.experimental import pallas as pl
from jax.experimental.pallas import tpu as pltpu
from jax.sharding import PartitionSpec as P

epsilon = 1e-05
pieces = 8
lanes = 128
far = 1e6
log2e = 1.4426950408889634
ln2 = 0.6931471805599453
vmem_bytes = 52 * 1024 * 1024
bf16 = jnp.bfloat16
f32 = jnp.float32


def silu_slope(values):
    sigma = jax.nn.sigmoid(values)
    return sigma * (1.0 + values * (1.0 - sigma))


def matmul(left, right):
    return jnp.dot(left, right, preferred_element_type=f32)


def transposed_left(left, right):
    return lax.dot_general(left, right, (((0,), (0,)), ((), ())), preferred_element_type=f32)


def transposed_right(left, right):
    return lax.dot_general(left, right, (((1,), (1,)), ((), ())), preferred_element_type=f32)


def swap(value, axis, mask):
    return lax.ppermute(value, axis, [(i, i ^ mask) for i in range(lax.axis_size(axis))])


def shifted(value, axis, by):
    size = lax.axis_size(axis)
    return lax.ppermute(value, axis, [(i, i + by) for i in range(size) if 0 <= i + by < size])


def bits_of(axis):
    return [1 << k for k in reversed(range(lax.axis_size(axis).bit_length() - 1))]


def bit_is_set(axis, mask):
    return ((lax.axis_index(axis) & mask) != 0).astype(jnp.int32)


def sum_all(value, axes):
    for axis, mask in axes:
        value = (value.astype(f32) + swap(value, axis, mask).astype(f32)).astype(bf16)
    return value


def sum_scatter(value, order, whole):
    value = value.reshape((2,) * len(whole) + (-1,) + value.shape[1:])
    left = list(whole)
    for axis, mask in order:
        at = left.index((axis, mask))
        left.pop(at)
        mine = bit_is_set(axis, mask)
        keep = lax.dynamic_index_in_dim(value, mine, at, keepdims=False)
        away = lax.dynamic_index_in_dim(value, 1 - mine, at, keepdims=False)
        total = keep.astype(f32) + swap(away, axis, mask).astype(f32)
        value = total.astype(bf16) if left else total
    return value


def chan_scatter(part):
    third = swap(part(3), "chan", 1)
    second = swap((part(2).astype(f32) + third.astype(f32)).astype(bf16), "chan", 2)
    first = swap(part(1), "chan", 1)
    return part(0).astype(f32) + first.astype(f32) + second.astype(f32)


def chan_gather(own):
    across = swap(own, "chan", 2)
    beside = swap(own, "chan", 1)
    return [own, beside, across, swap(across, "chan", 1)]


def chan_total(value):
    value = value + swap(value, "chan", 1)
    value = value.astype(bf16)
    return value.astype(f32) + swap(value, "chan", 2).astype(f32)


def spread(proj, out, first, count, steps):
    def fill(i, unused):
        rows = pl.ds(pl.multiple_of(i * pieces, pieces), pieces)
        tile = proj[rows, :]
        for n in range(count):
            out[n, rows, :] = jnp.broadcast_to(tile[:, first + n : first + n + 1], (pieces, lanes))
        return unused

    lax.fori_loop(0, steps, fill, 0)


def decay_rows(dec, count):
    return [jnp.broadcast_to(dec[n : n + 1, :], (pieces, lanes)) for n in range(count)]


def ends_kernel(size, rank, reff, drive, proj, dec, ends, sums, end_total, product_total, eb):
    steps = reff.shape[0] // pieces

    @pl.when(pl.program_id(0) == 0)
    def _():
        spread(proj, eb, rank, size, steps)

    decays = decay_rows(dec, size)

    def body(i, carry):
        states, total = carry
        rows = pl.ds(pl.multiple_of(i * pieces, pieces), pieces)
        rate = reff[rows, :]
        push = drive[rows, :]
        out = []
        for n in range(size):
            out.append(jnp.exp2(rate * decays[n]) * states[n] + push * eb[n, rows, :])
        return tuple(out), total + rate

    zero = jnp.zeros((pieces, lanes), f32)
    states, total = lax.fori_loop(0, steps, body, ((zero,) * size, zero), unroll=2)
    for n in range(size):
        ends[n] = states[n]
    sums[...] = total
    reached = ends[:, 0, :]
    for s in range(1, pieces):
        reached = ends[:, s, :] + jnp.exp2(dec[...] * sums[s : s + 1, :]) * reached
    end_total[...] = reached
    product_total[...] = jnp.exp2(dec[...] * jnp.sum(total, axis=0, keepdims=True))


def forward_kernel(
    size, rank, reff, drive, proj, dec, ends, sums, arriving, scanned, before, eb, rb, start
):
    steps = reff.shape[0] // pieces

    @pl.when(pl.program_id(0) == 0)
    def _():
        spread(proj, eb, rank, size, steps)
        spread(proj, rb, rank + size, size, steps)

    decays = decay_rows(dec, size)
    reached = arriving[...]
    for s in range(pieces):
        start[:, s, :] = reached
        reached = ends[:, s, :] + jnp.exp2(dec[...] * sums[s : s + 1, :]) * reached

    def body(i, states):
        rows = pl.ds(pl.multiple_of(i * 2 * pieces, 2 * pieces), 2 * pieces)
        rate = reff[rows, :]
        push = drive[rows, :]
        low = jnp.zeros((pieces, lanes), f32)
        high = low
        out = []
        for n in range(size):
            entry = eb[n, rows, :]
            readout = rb[n, rows, :]
            at_zero = states[n]
            at_one = jnp.exp2(rate[:pieces] * decays[n]) * at_zero + push[:pieces] * entry[:pieces]
            at_two = jnp.exp2(rate[pieces:] * decays[n]) * at_one + push[pieces:] * entry[pieces:]
            low = low + readout[:pieces] * at_one
            high = high + readout[pieces:] * at_two
            before[n, rows, :] = jnp.concatenate([at_zero, at_one], axis=0).astype(bf16)
            out.append(at_two)
        scanned[rows, :] = jnp.concatenate([low, high], axis=0)
        return tuple(out)

    states = lax.fori_loop(0, steps // 2, body, tuple(start[n] for n in range(size)))
    for n in range(size):
        last = jnp.concatenate([states[n], states[n]], axis=0).astype(bf16)
        before[n, pl.ds(steps * pieces, 2 * pieces), :] = last


def heads_kernel(size, rank, reff, slope, proj, dec, sums, heads, head_total, rb):
    steps = reff.shape[0] // pieces

    @pl.when(pl.program_id(0) == 0)
    def _():
        spread(proj, rb, rank + size, size, steps)

    decays = decay_rows(dec, size)

    def body(i, carried):
        rows = pl.ds(pl.multiple_of((steps - 1 - i) * pieces, pieces), pieces)
        rate = reff[rows, :]
        grad = slope[rows, :]
        return tuple(
            (carried[n] + rb[n, rows, :] * grad) * jnp.exp2(rate * decays[n]) for n in range(size)
        )

    zero = jnp.zeros((pieces, lanes), f32)
    carried = lax.fori_loop(0, steps, body, (zero,) * size, unroll=2)
    for n in range(size):
        heads[n] = carried[n]
    reached = heads[:, pieces - 1, :]
    for s in reversed(range(pieces - 1)):
        reached = heads[:, s, :] + jnp.exp2(dec[...] * sums[s : s + 1, :]) * reached
    head_total[...] = reached


def backward_kernel(
    size,
    rank,
    reff,
    drive,
    slope,
    proj,
    dec,
    heads,
    sums,
    leaving,
    before,
    rate_grad,
    drive_grad,
    proj_grad,
    decay_grad,
    eb,
    rb,
    stop,
    decay_sum,
    entry_terms,
    readout_terms,
):
    steps = reff.shape[0] // pieces
    pair = 2 * pieces

    @pl.when(pl.program_id(0) == 0)
    def _():
        spread(proj, eb, rank, size, steps)
        spread(proj, rb, rank + size, size, steps)
        proj_grad[...] = jnp.zeros_like(proj_grad)

    decays = decay_rows(dec, size)
    reached = leaving[...]
    for s in reversed(range(pieces)):
        stop[:, s, :] = reached
        reached = heads[:, s, :] + jnp.exp2(dec[...] * sums[s : s + 1, :]) * reached
    decay_sum[...] = jnp.zeros_like(decay_sum)

    def body(i, carried):
        at = pl.multiple_of((steps // 2 - 1 - i) * pair, pair)
        rows = pl.ds(at, pair)
        following = pl.ds(at + pair, pair)
        rate = reff[rows, :]
        push = drive[rows, :]
        grad = slope[rows, :]
        rate0, rate1 = rate[:pieces], rate[pieces:]
        push0, push1 = push[:pieces], push[pieces:]
        grad0, grad1 = grad[:pieces], grad[pieces:]
        zero = jnp.zeros((pieces, lanes), f32)
        rates0 = rates1 = drives0 = drives1 = zero
        out = []
        for n in range(size):
            entry = eb[n, rows, :]
            readout = rb[n, rows, :]
            state = before[n, rows, :].astype(f32)
            later = before[n, following, :].astype(f32)[:pieces]
            held1 = carried[n] + readout[pieces:] * grad1
            passed1 = held1 * jnp.exp2(rate1 * decays[n])
            scaled1 = passed1 * state[pieces:]
            held0 = passed1 + readout[:pieces] * grad0
            passed0 = held0 * jnp.exp2(rate0 * decays[n])
            scaled0 = passed0 * state[:pieces]
            rates1 = rates1 + scaled1 * decays[n]
            rates0 = rates0 + scaled0 * decays[n]
            drives1 = drives1 + held1 * entry[pieces:]
            drives0 = drives0 + held0 * entry[:pieces]
            decay_sum[n] += scaled1 * rate1 + scaled0 * rate0
            half = pl.ds((n % 2) * lanes, lanes)
            entry_terms[n // 2, rows, half] = jnp.concatenate(
                [held0 * push0, held1 * push1], axis=0
            ).astype(bf16)
            readout_terms[n // 2, rows, half] = jnp.concatenate(
                [grad0 * state[pieces:], grad1 * later], axis=0
            ).astype(bf16)
            out.append(passed0)
        rate_grad[rows, :] = jnp.concatenate([rates0, rates1], axis=0) * ln2
        drive_grad[rows, :] = jnp.concatenate([drives0, drives1], axis=0)
        return tuple(out)

    lax.fori_loop(0, steps // 2, body, tuple(stop[n] for n in range(size)))
    decay_grad[...] = jnp.sum(decay_sum[...], axis=1)

    source = lax.broadcasted_iota(jnp.int32, (2 * lanes, lanes), 0) // lanes
    target = lax.broadcasted_iota(jnp.int32, (2 * lanes, lanes), 1)
    tall = 256

    def gather(i, unused):
        rows = pl.ds(pl.multiple_of(i * tall, tall), tall)
        total = proj_grad[rows, :]
        for j in range(size // 2):
            pick = (target == source + (rank + 2 * j)).astype(f32).astype(bf16)
            total = total + jnp.dot(entry_terms[j, rows, :], pick, preferred_element_type=f32)
            pick = (target == source + (rank + size + 2 * j)).astype(f32).astype(bf16)
            total = total + jnp.dot(readout_terms[j, rows, :], pick, preferred_element_type=f32)
        proj_grad[rows, :] = total
        return unused

    lax.fori_loop(0, steps * pieces // tall, gather, 0)


def scan_calls(count, channels, size, rank):
    groups = channels // lanes
    steps = count // pieces
    tall = pl.BlockSpec((count, lanes), lambda g: (0, g))
    fixed = pl.BlockSpec((count, lanes), lambda g: (0, 0))
    small = pl.BlockSpec((size, lanes), lambda g: (0, g))
    ends = pl.BlockSpec((size, pieces, lanes), lambda g: (0, 0, g))
    sums = pl.BlockSpec((pieces, lanes), lambda g: (0, g))
    states = pl.BlockSpec((size, count + 2 * pieces, lanes), lambda g: (0, 0, g))
    wide = pltpu.VMEM((size, count, lanes), f32)
    tall_out = jax.ShapeDtypeStruct((count, channels), f32)
    small_out = jax.ShapeDtypeStruct((size, channels), f32)
    ends_out = jax.ShapeDtypeStruct((size, pieces, channels), f32)
    sums_out = jax.ShapeDtypeStruct((pieces, channels), f32)
    states_out = jax.ShapeDtypeStruct((size, count + 2 * pieces, channels), bf16)
    fixed_out = jax.ShapeDtypeStruct((count, lanes), f32)
    terms = pltpu.VMEM((size // 2, count, 2 * lanes), bf16)
    edge = pltpu.VMEM((size, pieces, lanes), f32)
    work = count * channels * size

    def call(kernel, name, ins, outs, out_shape, scratch, cost):
        return pl.pallas_call(
            functools.partial(kernel, size, rank),
            grid=(groups,),
            in_specs=ins,
            out_specs=outs,
            out_shape=out_shape,
            scratch_shapes=scratch,
            compiler_params=pltpu.CompilerParams(
                dimension_semantics=("arbitrary",), vmem_limit_bytes=vmem_bytes
            ),
            cost_estimate=pl.CostEstimate(
                flops=cost * work, bytes_accessed=20_000_000, transcendentals=work
            ),
            name=name,
        )

    return (
        call(
            ends_kernel,
            "scan_ends",
            [tall, tall, fixed, small],
            [ends, sums, small, small],
            [ends_out, sums_out, small_out, small_out],
            [wide],
            4,
        ),
        call(
            forward_kernel,
            "scan_forward",
            [tall, tall, fixed, small, ends, sums, small],
            [tall, states],
            [tall_out, states_out],
            [wide, wide, edge],
            6,
        ),
        call(
            heads_kernel,
            "scan_heads",
            [tall, tall, fixed, small, sums],
            [ends, small],
            [ends_out, small_out],
            [wide],
            4,
        ),
        call(
            backward_kernel,
            "scan_backward",
            [tall, tall, tall, fixed, small, ends, sums, small, states],
            [tall, tall, fixed, small],
            [tall_out, tall_out, fixed_out, small_out],
            [wide, wide, edge, edge, terms, terms],
            16,
        ),
    )


def chained(product, end, by):
    pair = jnp.stack([product, end])
    total = jnp.zeros_like(end)
    for distance in reversed(range(1, lax.axis_size("seq"))):
        got = shifted(pair, "seq", by * distance)
        total = got[1] + got[0] * total
    return total


def per_device(
    tokens,
    segment_ids,
    first_gain,
    input_proj,
    gate_proj,
    conv_weight,
    conv_bias,
    state_proj,
    step_proj,
    step_bias,
    decay_log,
    skip_gain,
    output_proj,
    second_gain,
    hidden_gate,
    hidden_up,
    hidden_down,
    upstream,
):
    count, features = tokens.shape[1:]
    width = conv_weight.shape[1]
    rank = step_proj.shape[0]
    size = decay_log.shape[1]
    channels = input_proj.shape[1]
    steps = count // pieces
    quarter = count // lax.axis_size("chan")
    me = lax.axis_index("chan")
    place = lax.axis_index("seq")
    dp_bits = [("dp", mask) for mask in bits_of("dp")]
    seq_bits = [("seq", mask) for mask in bits_of("seq")]
    shard_bits = dp_bits + seq_bits
    scan_ends, scan_forward, scan_heads, scan_backward = scan_calls(count, channels, size, rank)

    def mixed_order(values):
        return (
            values.reshape((pieces, steps) + values.shape[1:])
            .swapaxes(0, 1)
            .reshape(values.shape)
        )

    def block(values, r):
        return lax.dynamic_slice_in_dim(values, (me ^ r) * quarter, quarter)

    padded_ids = jnp.concatenate([jnp.full((width - 1,), -1, jnp.int32), segment_ids[0]], axis=0)
    window_ids = lax.dynamic_slice_in_dim(padded_ids, place * count, count + width - 1)
    own_ids = window_ids[width - 1 :]
    masks = [
        mixed_order((window_ids[offset : offset + count] == own_ids).astype(f32)[:, None])
        for offset in range(width)
    ]
    keep = masks[width - 2]

    rows = mixed_order(tokens[0])
    upper = mixed_order(upstream[0])

    def unit_of(values):
        scale = lax.rsqrt(jnp.mean(values * values, axis=-1, keepdims=True) + epsilon)
        return scale, values * scale

    gain_one = first_gain.astype(f32)
    gain_two = second_gain.astype(f32)
    normed = (unit_of(rows.astype(f32))[1] * gain_one).astype(bf16)
    inner = matmul(normed, input_proj).astype(bf16)

    reach = (width - 1) * pieces
    tail = inner[count - reach :].reshape(width - 1, pieces, channels)
    brought = shifted(tail[:, pieces - 1, :], "seq", 1)
    rim = jnp.concatenate([brought[:, None, :], tail[:, : pieces - 1, :]], axis=1)
    extended = jnp.concatenate([rim.reshape(reach, channels), inner], axis=0)
    taps = conv_weight.astype(f32).T

    def window(offset):
        return extended[offset * pieces : offset * pieces + count].astype(f32)

    convolved = conv_bias.astype(f32) + sum(
        window(offset) * taps[offset] * masks[offset] for offset in range(width)
    )
    mixed = jax.nn.silu(convolved).astype(bf16)
    mixed_wide = mixed.astype(f32)
    projected = chan_total(matmul(mixed, state_proj))
    gate_in = matmul(normed, gate_proj)
    step_low = projected[:, :rank].astype(bf16)
    step_pre = matmul(step_low, step_proj) + step_bias.astype(f32)
    rates = jax.nn.softplus(step_pre)
    decay = -jnp.exp(decay_log.astype(f32)).T
    decay_two = decay * log2e
    drive = rates * mixed_wide
    effective = jnp.where(keep > 0.0, rates, far)

    ends, sums, end_total, product_total = scan_ends(effective, drive, projected, decay_two)
    arriving = chained(product_total, end_total, 1)
    scanned, before = scan_forward(effective, drive, projected, decay_two, ends, sums, arriving)

    skip = skip_gain.astype(f32)
    gate_act = jax.nn.silu(gate_in)
    ssm_sum = scanned + skip * mixed_wide
    gated = (ssm_sum * gate_act).astype(bf16)

    hidden_sum = chan_scatter(lambda r: matmul(block(gated, r), output_proj).astype(bf16))
    rows_own = block(rows, 0).astype(f32)
    upper_own = block(upper, 0).astype(f32)
    hidden_one = rows_own + hidden_sum
    scale_two, unit_two = unit_of(hidden_one)
    normed_blocks = chan_gather((unit_two * gain_two).astype(bf16))
    upper_blocks = [block(upper, r) for r in range(4)]

    def feed_forward(normed_part, upper_part):
        gate_ffn = matmul(normed_part, hidden_gate)
        up_ffn = matmul(normed_part, hidden_up)
        gate_act_ffn = jax.nn.silu(gate_ffn)
        active = (gate_act_ffn * up_ffn).astype(bf16)
        grad_active = transposed_right(upper_part, hidden_down)
        grad_gate_ffn = (grad_active * up_ffn * silu_slope(gate_ffn)).astype(bf16)
        grad_up_ffn = (grad_active * gate_act_ffn).astype(bf16)
        grad_normed = (
            transposed_right(grad_gate_ffn, hidden_gate) + transposed_right(grad_up_ffn, hidden_up)
        ).astype(bf16)
        return active, grad_gate_ffn, grad_up_ffn, grad_normed

    halves = []
    for first in (0, 2):
        normed_half = jnp.concatenate(normed_blocks[first : first + 2], axis=0)
        upper_half = jnp.concatenate(upper_blocks[first : first + 2], axis=0)
        halves.append((normed_half, upper_half) + feed_forward(normed_half, upper_half))

    def quarter_of(items, r):
        return items[r // 2][(r % 2) * quarter : (r % 2 + 1) * quarter]

    grad_normed_two = chan_scatter(lambda r: quarter_of([half[5] for half in halves], r))
    normed_two, upper_two, active, grad_gate_ffn, grad_up_ffn = (
        jnp.concatenate([half[k] for half in halves], axis=0) for k in range(5)
    )

    def grad_scatter(value, order):
        return sum_scatter(value.astype(bf16), order, shard_bits)

    usual = dp_bits + seq_bits[::-1]
    other = seq_bits[-1:] + dp_bits + seq_bits[:-1]
    up_grad = grad_scatter(transposed_left(normed_two, grad_up_ffn), usual)
    gate_ffn_grad = grad_scatter(transposed_left(normed_two, grad_gate_ffn), usual)
    down_grad = grad_scatter(transposed_left(upper_two, active), usual)

    gain_two_grad = jnp.sum(grad_normed_two * unit_two, axis=0)
    grad_unit_two = grad_normed_two * gain_two
    grad_hidden = upper_own + scale_two * (
        grad_unit_two - unit_two * jnp.mean(grad_unit_two * unit_two, axis=-1, keepdims=True)
    )
    hidden_blocks = chan_gather(grad_hidden.astype(bf16))

    def placed(blocks):
        whole = jnp.zeros((count, blocks[0].shape[1]), blocks[0].dtype)
        for r, item in enumerate(blocks):
            whole = lax.dynamic_update_slice_in_dim(whole, item, (me ^ r) * quarter, 0)
        return whole

    def natural(own, dtype):
        item = own.reshape(steps // 4, pieces, features).swapaxes(0, 1)
        whole = jnp.zeros((pieces, steps, features), dtype)
        for r, got in enumerate(chan_gather(item)):
            whole = lax.dynamic_update_slice_in_dim(
                whole, got.astype(dtype), (me ^ r) * (steps // 4), 1
            )
        return whole.reshape(1, count, features)

    hidden_low = placed(hidden_blocks)
    grad_gated = transposed_right(hidden_low, output_proj)
    grad_scanned = grad_gated * gate_act
    grad_gate_in = (grad_gated * ssm_sum * silu_slope(gate_in)).astype(bf16)
    skip_grad = jnp.sum(grad_scanned * mixed_wide, axis=0)
    heads, head_total = scan_heads(effective, grad_scanned, projected, decay_two, sums)
    leaving = chained(product_total, head_total, -1)
    output_grad = grad_scatter(transposed_left(hidden_low, gated), usual)
    gate_grad = grad_scatter(transposed_left(normed, grad_gate_in), other)
    result_sum = chan_scatter(
        lambda r: matmul(quarter_of([half[2] for half in halves], r), hidden_down).astype(bf16)
    )
    result = natural((hidden_one + result_sum).astype(bf16), bf16)

    rate_grad, drive_grad, proj_terms, decay_grad = scan_backward(
        effective, drive, grad_scanned, projected, decay_two, heads, sums, leaving, before
    )
    rates_grad = rate_grad + drive_grad * mixed_wide
    pre_grad = rates_grad * jax.nn.sigmoid(step_pre)
    step_bias_grad = jnp.sum(pre_grad, axis=0)
    pre_low = pre_grad.astype(bf16)
    step_padded = jnp.pad(step_proj, ((0, 2 * size), (0, 0)))
    grad_projected = chan_total(transposed_right(pre_low, step_padded) + proj_terms).astype(bf16)
    step_weight_grad = transposed_left(step_low, pre_low)
    grad_mixed = (
        transposed_right(grad_projected, state_proj) + drive_grad * rates + skip * grad_scanned
    )
    grad_conv = grad_mixed * silu_slope(convolved)
    conv_bias_grad = jnp.sum(grad_conv, axis=0)
    conv_taps_grad = jnp.stack(
        [
            jnp.sum(grad_conv * window(offset) * masks[offset], axis=0)
            for offset in range(width)
        ],
        axis=0,
    )
    grad_extended = sum(
        jnp.pad(
            grad_conv * taps[offset] * masks[offset],
            ((offset * pieces, reach - offset * pieces), (0, 0)),
        )
        for offset in range(width)
    )
    spill = grad_extended[:reach].reshape(width - 1, pieces, channels)
    returned = shifted(spill[:, 0, :], "seq", -1)
    spill = jnp.concatenate([spill[:, 1:, :], returned[:, None, :]], axis=1)
    inner_low = (
        grad_extended[reach:]
        + jnp.pad(spill.reshape(reach, channels), ((count - reach, 0), (0, 0)))
    ).astype(bf16)

    def token_part(r):
        return (
            transposed_right(block(inner_low, r), input_proj)
            + transposed_right(block(grad_gate_in, r), gate_proj)
        ).astype(bf16)

    grad_normed = chan_scatter(token_part)
    input_grad = grad_scatter(transposed_left(normed, inner_low), usual)
    scale_one, unit_one = unit_of(rows_own)
    gain_one_grad = jnp.sum(grad_normed * unit_one, axis=0)
    grad_unit_one = grad_normed * gain_one
    tokens_grad = grad_hidden + scale_one * (
        grad_unit_one - unit_one * jnp.mean(grad_unit_one * unit_one, axis=-1, keepdims=True)
    )
    tokens_out = natural(tokens_grad.astype(bf16), f32)

    state_grad = transposed_left(grad_projected, mixed)
    chan_bits = [("chan", 1), ("chan", 2)]
    gain_two_sum = sum_all(gain_two_grad.astype(bf16), chan_bits + shard_bits).astype(f32)
    gain_one_sum = sum_all(gain_one_grad.astype(bf16), chan_bits + shard_bits).astype(f32)
    shards = lax.axis_size("dp") * lax.axis_size("seq")
    shard = lax.axis_index("dp") * lax.axis_size("seq") + place
    share = features // shards
    gain_one_out = lax.dynamic_slice_in_dim(gain_one_sum, shard * share, share)
    gain_two_out = lax.dynamic_slice_in_dim(gain_two_sum, shard * share, share)
    small = rank // shards
    low_parts = jnp.concatenate(
        [
            state_grad[:rank].reshape(shards, small, channels),
            step_weight_grad.reshape(shards, small, channels),
        ],
        axis=1,
    ).astype(bf16)
    low_sum = sum_scatter(low_parts, shard_bits, shard_bits).reshape(2 * small, channels)
    vectors = jnp.concatenate(
        [
            conv_taps_grad,
            conv_bias_grad[None],
            step_bias_grad[None],
            decay_grad * decay,
            skip_grad[None],
            state_grad[rank:],
        ],
        axis=0,
    ).astype(bf16)
    vectors = sum_all(vectors, shard_bits).astype(f32)
    at = width + 2
    return (
        result,
        tokens_out,
        gain_one_out,
        input_grad,
        gate_grad,
        vectors[:width].T,
        vectors[width],
        low_sum[:small].T,
        vectors[at + size + 1 :].T,
        low_sum[small:],
        vectors[width + 1],
        vectors[at : at + size].T,
        vectors[at + size],
        output_grad.T,
        gain_two_out,
        gate_ffn_grad,
        up_grad,
        down_grad.T,
    )


def solution(mesh):
    return jax.shard_map(
        per_device,
        mesh=mesh,
        in_specs=(
            P("dp", "seq", None),
            P("dp", None),
            P(),
            P(None, "chan"),
            P(None, "chan"),
            P("chan", None),
            P("chan"),
            P("chan", None),
            P(None, "chan"),
            P("chan"),
            P("chan", None),
            P("chan"),
            P("chan", None),
            P(),
            P(None, "chan"),
            P(None, "chan"),
            P("chan", None),
            P("dp", "seq", None),
        ),
        out_specs=(
            P("dp", "seq", None),
            P("dp", "seq", None),
            P(("dp", "seq")),
            P(("dp", "seq"), "chan"),
            P(("dp", "seq"), "chan"),
            P("chan", None),
            P("chan"),
            P("chan", ("dp", "seq")),
            P("chan", None),
            P(("dp", "seq"), "chan"),
            P("chan"),
            P("chan", None),
            P("chan"),
            P("chan", ("dp", "seq")),
            P(("dp", "seq")),
            P(("dp", "seq"), "chan"),
            P(("dp", "seq"), "chan"),
            P("chan", ("dp", "seq")),
        ),
        check_vma=False,
    )
```

```python
import functools

import jax
import jax.numpy as jnp
from jax import lax
from jax.experimental import pallas as pl
from jax.experimental.pallas import tpu as pltpu
from jax.sharding import PartitionSpec as P

epsilon = 1e-05
pieces = 8
lanes = 128
far = 1e6
log2e = 1.4426950408889634
ln2 = 0.6931471805599453
vmem_bytes = 58 * 1024 * 1024
bf16 = jnp.bfloat16
f32 = jnp.float32


def silu_slope(values):
    sigma = jax.nn.sigmoid(values)
    return sigma * (1.0 + values * (1.0 - sigma))


def matmul(left, right):
    return jnp.dot(left, right, preferred_element_type=f32)


def transposed_left(left, right):
    return lax.dot_general(left, right, (((0,), (0,)), ((), ())), preferred_element_type=f32)


def transposed_right(left, right):
    return lax.dot_general(left, right, (((1,), (1,)), ((), ())), preferred_element_type=f32)


def swap(value, axis, mask):
    return lax.ppermute(value, axis, [(i, i ^ mask) for i in range(lax.axis_size(axis))])


def shifted(value, axis, by):
    size = lax.axis_size(axis)
    return lax.ppermute(value, axis, [(i, i + by) for i in range(size) if 0 <= i + by < size])


def bits_of(axis):
    return [1 << k for k in reversed(range(lax.axis_size(axis).bit_length() - 1))]


def bit_is_set(axis, mask):
    return ((lax.axis_index(axis) & mask) != 0).astype(jnp.int32)


def after(value, *others):
    if not others:
        return value
    return lax.optimization_barrier((value, others))[0]


def sum_all(value, axes):
    for axis, mask in axes:
        value = (value.astype(f32) + swap(value, axis, mask).astype(f32)).astype(bf16)
    return value


class Scatter:
    def __init__(self, value, order, whole):
        value = value.astype(bf16)
        self.terms = [value.reshape((2,) * len(whole) + (-1,) + value.shape[1:])]
        self.order = list(order)
        self.left = list(whole)

    def send(self, *others):
        axis, mask = self.order.pop(0)
        at = self.left.index((axis, mask))
        self.left.pop(at)
        mine = bit_is_set(axis, mask)
        if others:
            self.terms[-1] = after(self.terms[-1], *others)
        away = [lax.dynamic_index_in_dim(t, 1 - mine, at, keepdims=False) for t in self.terms]
        away = sum(t.astype(f32) for t in away).astype(bf16)
        self.terms = [
            lax.dynamic_index_in_dim(t, mine, at, keepdims=False) for t in self.terms
        ]
        self.terms.append(swap(away, axis, mask))
        return away

    def total(self, *others):
        while self.order:
            self.send(*others)
        if others:
            self.terms[-1] = after(self.terms[-1], *others)
        return sum(t.astype(f32) for t in self.terms)


def chan_scatter(part, fill=lambda begun: ()):
    third = swap(part(3), "chan", 1)
    middle = (part(2).astype(f32) + third.astype(f32)).astype(bf16)
    second = swap(middle, "chan", 2)
    first = swap(part(1), "chan", 1)
    own = part(0)
    second = after(second, own, *fill(middle))
    return own.astype(f32) + first.astype(f32) + second.astype(f32)


def chan_gather(own, fill=lambda begun: ()):
    across = swap(own, "chan", 2)
    beside = swap(own, "chan", 1)
    across = after(across, *fill(beside))
    return [own, beside, across, swap(across, "chan", 1)]


def in_order(own, beside):
    upper = bit_is_set("chan", 1) == 1
    return jnp.concatenate(
        [jnp.where(upper, beside, own), jnp.where(upper, own, beside)], axis=0
    )


def chan_total(value, near=lambda: (), distant=lambda begun: ()):
    got = swap(value, "chan", 1)
    value = (value + after(got, *near())).astype(bf16)
    got = swap(value, "chan", 2)
    got = after(got, *distant(value))
    return value.astype(f32) + got.astype(f32)


def step_rows(step, steps):
    return pl.ds(step, pieces, stride=steps)


def split_proj(proj, both, steps):
    def body(i, unused):
        tile = jnp.concatenate(
            [proj[step_rows(2 * i, steps), :], proj[step_rows(2 * i + 1, steps), :]], axis=0
        )
        high = tile.astype(bf16)
        rows = pl.ds(pl.multiple_of(i * 2 * pieces, 2 * pieces), 2 * pieces)
        both[rows, :lanes] = high
        both[rows, lanes:] = (tile - high.astype(f32)).astype(bf16)
        return unused

    lax.fori_loop(0, steps // 2, body, 0)


def spread(both, out, first, count):
    tall = min(256, both.shape[0])
    source = lax.broadcasted_iota(jnp.int32, (2 * lanes, 2 * lanes), 0) % lanes
    target = lax.broadcasted_iota(jnp.int32, (2 * lanes, 2 * lanes), 1) // lanes
    for n in range(0, count, 2):
        pick = (source == target + (first + n)).astype(f32).astype(bf16)
        for k in range(both.shape[0] // tall):
            rows = pl.ds(k * tall, tall)
            wide = jnp.dot(both[rows, :], pick, preferred_element_type=f32)
            out[n, rows, :] = wide[:, :lanes]
            if n + 1 < count:
                out[n + 1, rows, :] = wide[:, lanes:]


def decay_rows(dec, count):
    return [jnp.broadcast_to(dec[n : n + 1, :], (pieces, lanes)) for n in range(count)]


def ends_kernel(size, rank, rates, mixed, proj, dec, ends, sums, end_total, product_total, *scratch):
    both, eb, fb = scratch
    steps = rates.shape[0] // pieces

    @pl.when(pl.program_id(0) == 0)
    def _():
        split_proj(proj, both, steps)
        spread(both, eb, rank, size)
        spread(both, fb, 0, 1)

    decays = decay_rows(dec, size)

    def body(i, carry):
        states, total = carry
        rows = pl.ds(pl.multiple_of(i * pieces, pieces), pieces)
        rate = rates[step_rows(i, steps), :]
        push = rate * mixed[step_rows(i, steps), :]
        rate = rate + fb[0, rows, :]
        out = []
        for n in range(size):
            out.append(jnp.exp2(rate * decays[n]) * states[n] + push * eb[n, rows, :])
        return tuple(out), total + rate

    zero = jnp.zeros((pieces, lanes), f32)
    states, total = lax.fori_loop(0, steps, body, ((zero,) * size, zero), unroll=4)
    for n in range(size):
        ends[n] = states[n]
    sums[...] = total
    reached = ends[:, 0, :]
    for s in range(1, pieces):
        reached = ends[:, s, :] + jnp.exp2(dec[...] * sums[s : s + 1, :]) * reached
    end_total[...] = reached
    product_total[...] = jnp.exp2(dec[...] * jnp.sum(total, axis=0, keepdims=True))


def forward_kernel(
    size, rank, rates, mixed, proj, dec, ends, sums, arriving, gate_in, skip, *rest
):
    gated, summed, before, both, eb, rb, fb, start, scanned = rest
    steps = rates.shape[0] // pieces

    @pl.when(pl.program_id(0) == 0)
    def _():
        split_proj(proj, both, steps)
        spread(both, eb, rank, size)
        spread(both, rb, rank + size, size)
        spread(both, fb, 0, 1)

    decays = decay_rows(dec, size)
    reached = arriving[...]
    for s in range(pieces):
        start[:, s, :] = reached
        reached = ends[:, s, :] + jnp.exp2(dec[...] * sums[s : s + 1, :]) * reached

    def body(i, states):
        rows = pl.ds(pl.multiple_of(i * 2 * pieces, 2 * pieces), 2 * pieces)
        first, second = step_rows(2 * i, steps), step_rows(2 * i + 1, steps)
        rate0, rate1 = rates[first, :], rates[second, :]
        push0, push1 = rate0 * mixed[first, :], rate1 * mixed[second, :]
        apart = fb[0, rows, :]
        rate0, rate1 = rate0 + apart[:pieces], rate1 + apart[pieces:]
        low = jnp.zeros((pieces, lanes), f32)
        high = low
        out = []
        for n in range(size):
            entry = eb[n, rows, :]
            readout = rb[n, rows, :]
            at_zero = states[n]
            at_one = jnp.exp2(rate0 * decays[n]) * at_zero + push0 * entry[:pieces]
            at_two = jnp.exp2(rate1 * decays[n]) * at_one + push1 * entry[pieces:]
            low = low + readout[:pieces] * at_one
            high = high + readout[pieces:] * at_two
            before[n, rows, :] = jnp.concatenate([at_zero, at_one], axis=0).astype(bf16)
            out.append(at_two)
        scanned[first, :] = low
        scanned[second, :] = high
        return tuple(out)

    states = lax.fori_loop(0, steps // 2, body, tuple(start[n] for n in range(size)))
    for n in range(size):
        last = jnp.concatenate([states[n], states[n]], axis=0).astype(bf16)
        before[n, pl.ds(steps * pieces, 2 * pieces), :] = last

    def finish(i, unused):
        rows = pl.ds(pl.multiple_of(i * 64, 64), 64)
        total = scanned[rows, :] + skip[...] * mixed[rows, :]
        gate = gate_in[rows, :]
        gated[rows, :] = (total * (gate * jax.nn.sigmoid(gate))).astype(bf16)
        summed[rows, :] = total.astype(bf16)
        return unused

    lax.fori_loop(0, steps * pieces // 64, finish, 0)


def heads_kernel(size, rank, rates, slope, proj, dec, sums, heads, head_total, *scratch):
    both, rb, fb = scratch
    steps = rates.shape[0] // pieces

    @pl.when(pl.program_id(0) == 0)
    def _():
        split_proj(proj, both, steps)
        spread(both, rb, rank + size, size)
        spread(both, fb, 0, 1)

    decays = decay_rows(dec, size)

    def body(i, carried):
        step = steps - 1 - i
        rows = pl.ds(pl.multiple_of(step * pieces, pieces), pieces)
        rate = rates[step_rows(step, steps), :] + fb[0, rows, :]
        grad = slope[step_rows(step, steps), :]
        return tuple(
            (carried[n] + rb[n, rows, :] * grad) * jnp.exp2(rate * decays[n]) for n in range(size)
        )

    zero = jnp.zeros((pieces, lanes), f32)
    carried = lax.fori_loop(0, steps, body, (zero,) * size, unroll=4)
    for n in range(size):
        heads[n] = carried[n]
    reached = heads[:, pieces - 1, :]
    for s in reversed(range(pieces - 1)):
        reached = heads[:, s, :] + jnp.exp2(dec[...] * sums[s : s + 1, :]) * reached
    head_total[...] = reached


def backward_kernel(
    size,
    rank,
    rates,
    mixed,
    slope,
    proj,
    dec,
    heads,
    sums,
    leaving,
    before,
    skip,
    step_proj,
    *rest,
):
    pre_low, direct, proj_grad, decay_grad, bias_grad = rest[:5]
    both, eb, rb, fb, stop, decay_sum, entry_terms, readout_terms = rest[5:13]
    picks, rate_grad, drive_grad, terms_grad = rest[13:]
    steps = rates.shape[0] // pieces
    count = steps * pieces
    pair = 2 * pieces
    group = pl.program_id(0)

    @pl.when(group == 0)
    def _():
        split_proj(proj, both, steps)
        spread(both, eb, rank, size)
        spread(both, rb, rank + size, size)
        spread(both, fb, 0, 1)
        proj_grad[...] = jnp.zeros_like(proj_grad)
        target = lax.broadcasted_iota(jnp.int32, (lanes, lanes), 1)
        for n in range(2 * size):
            picks[pl.ds(n * lanes, lanes), :] = (target == rank + n).astype(f32).astype(bf16)

    decays = decay_rows(dec, size)
    reached = leaving[...]
    for s in reversed(range(pieces)):
        stop[:, s, :] = reached
        reached = heads[:, s, :] + jnp.exp2(dec[...] * sums[s : s + 1, :]) * reached
    decay_sum[...] = jnp.zeros_like(decay_sum)

    def body(fresh, i, carried):
        half = steps // 2 - 1 - i
        at = pl.multiple_of(half * pair, pair)
        rows = pl.ds(at, pair)
        following = pl.ds(at + pair, pair)
        first, second = step_rows(2 * half, steps), step_rows(2 * half + 1, steps)
        rate0, rate1 = rates[first, :], rates[second, :]
        push0, push1 = rate0 * mixed[first, :], rate1 * mixed[second, :]
        grad0, grad1 = slope[first, :], slope[second, :]
        apart = fb[0, rows, :]
        far0, far1 = rate0 + apart[:pieces], rate1 + apart[pieces:]
        zero = jnp.zeros((pieces, lanes), f32)
        rates0 = rates1 = drives0 = drives1 = zero
        out = []
        for n in range(size):
            entry = eb[n, rows, :]
            readout = rb[n, rows, :]
            state = before[n, rows, :].astype(f32)
            later = before[n, following, :].astype(f32)[:pieces]
            held1 = carried[n] + readout[pieces:] * grad1
            passed1 = held1 * jnp.exp2(far1 * decays[n])
            scaled1 = passed1 * state[pieces:]
            held0 = passed1 + readout[:pieces] * grad0
            passed0 = held0 * jnp.exp2(far0 * decays[n])
            scaled0 = passed0 * state[:pieces]
            rates1 = rates1 + scaled1 * decays[n]
            rates0 = rates0 + scaled0 * decays[n]
            drives1 = drives1 + held1 * entry[pieces:]
            drives0 = drives0 + held0 * entry[:pieces]
            decay_sum[n] += scaled1 * rate1 + scaled0 * rate0
            here = pl.ds(n * lanes, lanes)
            entries = jnp.concatenate([held0 * push0, held1 * push1], axis=0)
            readouts = jnp.concatenate([grad0 * state[pieces:], grad1 * later], axis=0)
            entry_terms[rows, here] = entries if fresh else entry_terms[rows, here] + entries
            readout_terms[rows, here] = (
                readouts if fresh else readout_terms[rows, here] + readouts
            )
            out.append(passed0)
        rate_grad[first, :] = rates0
        rate_grad[second, :] = rates1
        drive_grad[first, :] = drives0
        drive_grad[second, :] = drives1
        return tuple(out)

    def sweep(fresh):
        edges = tuple(stop[n] for n in range(size))
        lax.fori_loop(0, steps // 2, functools.partial(body, fresh), edges)

    pl.when(group == 0)(lambda: sweep(True))
    pl.when(group > 0)(lambda: sweep(False))
    decay_grad[...] = jnp.sum(decay_sum[...], axis=1)

    tall = min(256, count)
    bias_total = jnp.zeros((1, lanes), f32)
    for k in range(count // tall):
        rows = pl.ds(k * tall, tall)
        rate, drives = rates[rows, :], drive_grad[rows, :]
        pre = (rate_grad[rows, :] * ln2 + drives * mixed[rows, :]) * (1.0 - jnp.exp(-rate))
        bias_total = bias_total + jnp.sum(pre, axis=0, keepdims=True)
        low = pre.astype(bf16)
        pre_low[rows, :] = low
        direct[rows, :] = drives * rate + skip[...] * slope[rows, :]
        proj_grad[rows, :] += lax.dot_general(
            low, step_proj[...], (((1,), (1,)), ((), ())), preferred_element_type=f32
        )
    bias_grad[...] = bias_total

    @pl.when(group == pl.num_programs(0) - 1)
    def _():
        for k in range(count // tall):
            rows = pl.ds(k * tall, tall)
            terms_grad[rows, :] = jnp.dot(
                entry_terms[rows, :].astype(bf16),
                picks[: size * lanes, :],
                preferred_element_type=f32,
            ) + jnp.dot(
                readout_terms[rows, :].astype(bf16),
                picks[size * lanes :, :],
                preferred_element_type=f32,
            )

        def finish(i, unused):
            rows = pl.ds(pl.multiple_of(i * pieces, pieces), pieces)
            proj_grad[step_rows(i, steps), :] += terms_grad[rows, :]
            return unused

        lax.fori_loop(0, steps, finish, 0)


def scan_calls(count, channels, size, rank):
    groups = channels // lanes
    tall = pl.BlockSpec((count, lanes), lambda g: (0, g))
    fixed = pl.BlockSpec((count, lanes), lambda g: (0, 0))
    small = pl.BlockSpec((size, lanes), lambda g: (0, g))
    ends = pl.BlockSpec((size, pieces, lanes), lambda g: (0, 0, g))
    sums = pl.BlockSpec((pieces, lanes), lambda g: (0, g))
    line = pl.BlockSpec((1, lanes), lambda g: (0, g))
    square = pl.BlockSpec((lanes, lanes), lambda g: (0, g))
    states = pl.BlockSpec((size, count + 2 * pieces, lanes), lambda g: (0, 0, g))
    shape = jax.ShapeDtypeStruct
    tall_out = shape((count, channels), f32)
    tall_low = shape((count, channels), bf16)
    small_out = shape((size, channels), f32)
    ends_out = shape((size, pieces, channels), f32)
    sums_out = shape((pieces, channels), f32)
    states_out = shape((size, count + 2 * pieces, channels), bf16)
    fixed_out = shape((count, lanes), f32)
    line_out = shape((1, channels), f32)
    both = pltpu.VMEM((count, 2 * lanes), bf16)
    wide = pltpu.VMEM((size, count, lanes), f32)
    thin = pltpu.VMEM((1, count, lanes), f32)
    terms = pltpu.VMEM((count, size * lanes), f32)
    edge = pltpu.VMEM((size, pieces, lanes), f32)
    own = pltpu.VMEM((count, lanes), f32)
    picks = pltpu.VMEM((2 * size * lanes, lanes), bf16)
    work = count * channels * size

    def call(kernel, name, ins, outs, out_shape, scratch, span=groups, aliases={}):
        return pl.pallas_call(
            functools.partial(kernel, size, rank),
            grid=(span,),
            in_specs=ins,
            out_specs=outs,
            out_shape=out_shape,
            scratch_shapes=scratch,
            compiler_params=pltpu.CompilerParams(
                dimension_semantics=("arbitrary",), vmem_limit_bytes=vmem_bytes
            ),
            cost_estimate=pl.CostEstimate(flops=work, bytes_accessed=0, transcendentals=0),
            input_output_aliases=aliases,
            name=name,
        )

    def backward_call(first, span):
        def moved(spec):
            return pl.BlockSpec(spec.block_shape, lambda g: spec.index_map(g + first))

        ins = [tall, tall, tall, fixed, small, ends, sums, small, states, line, square]
        outs = [tall, tall, fixed, small, line]
        kept = [0, 1, 3, 4] if first else []
        aliases = {len(ins) + i: out for i, out in enumerate(kept)}
        held = [pl.BlockSpec(memory_space=pl.ANY)] * len(kept)

        def kernel(size, rank, *refs):
            refs = refs[: len(ins)] + refs[len(ins) + len(kept) :]
            backward_kernel(size, rank, *refs)

        return call(
            kernel,
            "scan_backward",
            [moved(spec) for spec in ins] + held,
            [moved(spec) for spec in outs],
            [tall_low, tall_out, fixed_out, small_out, line_out],
            [both, wide, wide, thin, edge, edge, terms, terms, picks, own, own, own],
            span,
            aliases,
        )

    part = groups // 2
    backward_parts = (backward_call(0, part), backward_call(part, groups - part))
    return (
        call(
            ends_kernel,
            "scan_ends",
            [tall, tall, fixed, small],
            [ends, sums, small, small],
            [ends_out, sums_out, small_out, small_out],
            [both, wide, thin],
        ),
        call(
            forward_kernel,
            "scan_forward",
            [tall, tall, fixed, small, ends, sums, small, tall, line],
            [tall, tall, states],
            [tall_low, tall_low, states_out],
            [both, wide, wide, thin, edge, own],
        ),
        call(
            heads_kernel,
            "scan_heads",
            [tall, tall, fixed, small, sums],
            [ends, small],
            [ends_out, small_out],
            [both, wide, thin],
        ),
        backward_parts,
    )


def norm_kernel(rows, gain, out):
    values = rows[...].astype(f32)
    scale = lax.rsqrt(jnp.mean(values * values, axis=-1, keepdims=True) + epsilon)
    out[...] = (values * scale * gain[...]).astype(bf16)


def norm_call(count, features):
    tall = min(count, 128)
    return pl.pallas_call(
        norm_kernel,
        grid=(count // tall,),
        in_specs=[
            pl.BlockSpec((tall, features), lambda i: (i, 0)),
            pl.BlockSpec((1, features), lambda i: (0, 0)),
        ],
        out_specs=pl.BlockSpec((tall, features), lambda i: (i, 0)),
        out_shape=jax.ShapeDtypeStruct((count, features), bf16),
        cost_estimate=pl.CostEstimate(
            flops=6 * count * features, bytes_accessed=4 * count * features, transcendentals=count
        ),
        name="norm_rows",
    )


def chained(product, end, by, fill=()):
    inside = jnp.stack([product, end])
    reach = 1
    outside = None
    while reach < lax.axis_size("seq"):
        got = shifted(inside, "seq", by * reach)
        if fill:
            got = after(got, *fill.pop(0)(inside))
        if outside is None:
            outside = got
        else:
            outside = jnp.stack([outside[0] * got[0], outside[1] + outside[0] * got[1]])
        inside = jnp.stack([product * outside[0], end + product * outside[1]])
        reach *= 2
    return outside[1]


def per_device(
    tokens,
    segment_ids,
    first_gain,
    input_proj,
    gate_proj,
    conv_weight,
    conv_bias,
    state_proj,
    step_proj,
    step_bias,
    decay_log,
    skip_gain,
    output_proj,
    second_gain,
    hidden_gate,
    hidden_up,
    hidden_down,
    upstream,
):
    count, features = tokens.shape[1:]
    width = conv_weight.shape[1]
    rank = step_proj.shape[0]
    size = decay_log.shape[1]
    channels = input_proj.shape[1]
    quarter = count // lax.axis_size("chan")
    half = count // 2
    me = lax.axis_index("chan")
    place = lax.axis_index("seq")
    dp_bits = [("dp", mask) for mask in bits_of("dp")]
    seq_bits = [("seq", mask) for mask in bits_of("seq")]
    shard_bits = dp_bits + seq_bits
    usual = dp_bits + seq_bits[::-1]
    other = seq_bits[-1:] + dp_bits + seq_bits[:-1]
    scan_ends, scan_forward, scan_heads, scan_backward = scan_calls(count, channels, size, rank)

    def block(values, r):
        return lax.dynamic_slice_in_dim(values, (me ^ r) * quarter, quarter)

    def own_half(values, r):
        return lax.dynamic_slice_in_dim(values, ((me >> 1) ^ r) * half, half)

    def scatter(value, order):
        return Scatter(value, order, shard_bits)

    padded_ids = jnp.concatenate([jnp.full((width - 1,), -1, jnp.int32), segment_ids[0]], axis=0)
    window_ids = lax.dynamic_slice_in_dim(padded_ids, place * count, count + width - 1)
    own_ids = window_ids[width - 1 :]
    masks = [
        (window_ids[offset : offset + count] == own_ids).astype(f32)[:, None]
        for offset in range(width)
    ]
    keep = masks[width - 2]

    rows = tokens[0]
    upper = upstream[0]

    def unit_of(values):
        scale = lax.rsqrt(jnp.mean(values * values, axis=-1, keepdims=True) + epsilon)
        return scale, values * scale

    gain_one = first_gain.astype(f32)
    gain_two = second_gain.astype(f32)
    normed = norm_call(count, features)(rows, gain_one[None])
    inner = matmul(normed, input_proj).astype(bf16)
    rim = shifted(inner[count - width + 1 :], "seq", 1)
    gate_in = matmul(normed, gate_proj)
    extended = jnp.concatenate([rim, after(inner, gate_in)], axis=0).astype(f32)
    taps = conv_weight.astype(f32).T
    convolved = conv_bias.astype(f32) + sum(
        extended[offset : offset + count] * taps[offset] * masks[offset]
        for offset in range(width)
    )
    mixed = jax.nn.silu(convolved).astype(bf16)
    mixed_wide = mixed.astype(f32)
    upper_halves = [own_half(upper, r) for r in range(2)]
    grad_actives = []

    def upstream_parts(begun):
        grad_actives.extend(
            transposed_right(after(item, begun), hidden_down) for item in upper_halves
        )
        return grad_actives

    projected = chan_total(matmul(mixed, state_proj), distant=upstream_parts)
    step_low = projected[:, :rank].astype(bf16)
    step_pre = matmul(step_low, step_proj) + step_bias.astype(f32)
    rates = jax.nn.softplus(step_pre)
    decay = -jnp.exp(decay_log.astype(f32)).T
    decay_two = decay * log2e
    column = lax.broadcasted_iota(jnp.int32, projected.shape, 1)
    scan_proj = jnp.where(column == 0, (1.0 - keep) * far, projected)

    ends, sums, end_total, product_total = scan_ends(rates, mixed_wide, scan_proj, decay_two)
    arriving = chained(product_total, end_total, 1)
    skip = skip_gain.astype(f32)[None]
    gated, ssm_sum, before = scan_forward(
        rates, mixed_wide, scan_proj, decay_two, ends, sums, arriving, gate_in, skip
    )

    hidden_sum = chan_scatter(lambda r: matmul(block(gated, r), output_proj).astype(bf16))
    rows_own = block(rows, 0).astype(f32)
    upper_own = block(upper, 0).astype(f32)
    hidden_one = rows_own + hidden_sum
    scale_two, unit_two = unit_of(hidden_one)

    def feed_forward(normed_part, grad_active):
        gate_ffn = matmul(normed_part, hidden_gate)
        up_ffn = matmul(normed_part, hidden_up)
        gate_act_ffn = jax.nn.silu(gate_ffn)
        active = (gate_act_ffn * up_ffn).astype(bf16)
        grad_gate_ffn = (grad_active * up_ffn * silu_slope(gate_ffn)).astype(bf16)
        grad_up_ffn = (grad_active * gate_act_ffn).astype(bf16)
        grad_normed = (
            transposed_right(grad_gate_ffn, hidden_gate) + transposed_right(grad_up_ffn, hidden_up)
        ).astype(bf16)
        return active, grad_gate_ffn, grad_up_ffn, grad_normed

    halves = []

    def half_forward(own, beside, r):
        normed_half = lax.optimization_barrier(in_order(own, beside))
        halves.append((normed_half,) + feed_forward(normed_half, grad_actives[r]))
        return halves[-1]

    normed_own = (unit_two * gain_two).astype(bf16)
    normed_blocks = chan_gather(normed_own, lambda beside: half_forward(normed_own, beside, 0))
    half_forward(*normed_blocks[2:], 1)

    def quarter_of(items, r):
        return lax.dynamic_slice_in_dim(items[r // 2], ((me ^ r) & 1) * quarter, quarter)

    normed_two, active, grad_gate_ffn, grad_up_ffn = (
        jnp.concatenate([item[k] for item in halves], axis=0) for k in range(4)
    )
    upper_two = jnp.concatenate(upper_halves, axis=0)
    ffn_sums = []

    def ffn_weights(begun):
        left, right = after((normed_two, upper_two), begun)
        sent = []
        for value, order in (
            (transposed_left(left, grad_up_ffn), usual),
            (transposed_left(left, grad_gate_ffn), usual),
            (transposed_left(right, active), other),
        ):
            ffn_sums.append(scatter(value, order))
            sent.append(ffn_sums[-1].send())
        return sent

    grad_normed_two = chan_scatter(
        lambda r: quarter_of([item[4] for item in halves], r), ffn_weights
    )
    grad_unit_two = grad_normed_two * gain_two
    grad_hidden = upper_own + scale_two * (
        grad_unit_two - unit_two * jnp.mean(grad_unit_two * unit_two, axis=-1, keepdims=True)
    )

    def placed(blocks, dtype):
        whole = jnp.zeros((count, features), dtype)
        for r, item in enumerate(blocks):
            whole = lax.dynamic_update_slice_in_dim(
                whole, item.astype(dtype), (me ^ r) * quarter, 0
            )
        return whole

    results = []

    def result_parts(begun):
        for item in halves:
            results.append(matmul(after(item[1], begun), hidden_down).astype(bf16))
        results.append(swap(quarter_of(results, 3), "chan", 1))
        results.append(swap(quarter_of(results, 1), "chan", 1))
        return results[:2]

    hidden_low = placed(chan_gather(grad_hidden.astype(bf16), result_parts), bf16)
    result_middle = (
        quarter_of(results, 2).astype(f32) + after(results[2], hidden_low).astype(f32)
    ).astype(bf16)
    result_far = swap(result_middle, "chan", 2)
    gate_act = jax.nn.silu(gate_in)
    grad_gated = transposed_right(hidden_low, output_proj)
    grad_scanned = grad_gated * gate_act
    grad_gate_in = (grad_gated * ssm_sum.astype(f32) * silu_slope(gate_in)).astype(bf16)
    skip_grad = jnp.sum(grad_scanned * mixed_wide, axis=0)
    heads, head_total = scan_heads(
        rates, after(grad_scanned, result_middle), scan_proj, decay_two, sums
    )

    mixer_sums = []

    def output_weights(begun):
        value = transposed_left(after(hidden_low, begun), gated)
        mixer_sums.append(scatter(value, usual))
        return [mixer_sums[0].send()]

    def gate_weights(begun):
        value = transposed_left(normed, after(grad_gate_in, begun))
        mixer_sums.append(scatter(value, other))
        return [mixer_sums[1].send()]

    leaving = chained(product_total, head_total, -1, [output_weights, gate_weights])
    sent = [item.send(leaving) for item in ffn_sums]
    result_sum = (
        quarter_of(results, 0).astype(f32)
        + results[3].astype(f32)
        + after(result_far, leaving).astype(f32)
    )
    result_own = (hidden_one + result_sum).astype(bf16)
    result_across = swap(result_own, "chan", 2)
    result_beside = swap(result_own, "chan", 1)
    step_padded = jnp.pad(step_proj, ((0, 2 * size), (0, 0)))
    scan_inputs = (rates, mixed_wide, grad_scanned, scan_proj, decay_two, heads, sums)
    first_scan, second_scan = scan_backward
    begin = after(leaving, sent, result_own)
    parts = first_scan(*scan_inputs, begin, before, skip, step_padded)
    terms = parts[2]
    sent = [item.send(terms) for item in ffn_sums]
    begin = after(leaving, sent)
    kept = [parts[k] for k in (0, 1, 3, 4)]
    pre_low, direct, more_terms, decay_grad, step_bias_grad = second_scan(
        *scan_inputs, begin, before, skip, step_padded, *kept
    )
    arrived = [item.terms[-1] for item in ffn_sums[:2] + mixer_sums]
    more_terms = after(more_terms, arrived, result_across)
    proj_terms = terms + more_terms

    step_weight_grad = []

    def step_weights():
        step_weight_grad.append(transposed_left(step_low, pre_low).astype(bf16))
        return step_weight_grad

    results_whole = []

    def result_place(begun):
        sent = [item.send(begun) for item in mixer_sums]
        across = after(result_across, begun, *sent)
        blocks = [result_own, result_beside, across, swap(across, "chan", 1)]
        results_whole.append(placed(blocks, bf16))
        return results_whole + [ffn_sums[2].terms[-1]]

    grad_projected = chan_total(proj_terms, step_weights, result_place).astype(bf16)
    grad_mixed = transposed_right(grad_projected, state_proj) + direct
    grad_conv = grad_mixed * silu_slope(convolved)
    conv_bias_grad = jnp.sum(grad_conv, axis=0)
    conv_taps_grad = jnp.stack(
        [
            jnp.sum(grad_conv * extended[offset : offset + count] * masks[offset], axis=0)
            for offset in range(width)
        ],
        axis=0,
    )
    grad_extended = sum(
        jnp.pad(
            grad_conv * taps[offset] * masks[offset], ((offset, width - 1 - offset), (0, 0))
        )
        for offset in range(width)
    )
    spill = grad_extended[: width - 1]
    returned = shifted(spill, "seq", -1)
    state_grad = transposed_left(after(grad_projected, spill), mixed).astype(bf16)
    few = jnp.concatenate(
        [
            conv_taps_grad,
            conv_bias_grad[None],
            step_bias_grad,
            decay_grad * decay,
            skip_grad[None],
        ],
        axis=0,
    )
    shards = lax.axis_size("dp") * lax.axis_size("seq")
    shard = lax.axis_index("dp") * lax.axis_size("seq") + place
    low_rows = rank // shards
    low_parts = jnp.concatenate(
        [
            state_grad[:rank].reshape(shards, low_rows, channels),
            step_weight_grad[0].reshape(shards, low_rows, channels),
        ],
        axis=1,
    )
    inner_low = (
        grad_extended[width - 1 :]
        + jnp.pad(after(returned, low_parts), ((count - width + 1, 0), (0, 0)))
    ).astype(bf16)

    def token_part(r):
        return (
            transposed_right(block(inner_low, r), input_proj)
            + transposed_right(block(grad_gate_in, r), gate_proj)
        ).astype(bf16)

    input_sums = []

    def third_round(begun):
        value = transposed_left(normed, after(inner_low, begun)).astype(bf16)
        sent = []
        value = jnp.concatenate([value.reshape(shards, -1, channels), low_parts], axis=1)
        for k, order in ((0, usual), (1, other)):
            part = value[:, :, k * (channels // 2) : (k + 1) * (channels // 2)]
            input_sums.append(scatter(part.reshape(-1, channels // 2), order))
            sent.append(input_sums[-1].send())
        return (
            sent
            + [item.send(*sent) for item in mixer_sums]
            + [item.total(*sent) for item in ffn_sums]
        )

    grad_normed = chan_scatter(token_part, third_round)
    scale_one, unit_one = unit_of(rows_own)
    gain_one_grad = jnp.sum(grad_normed * unit_one, axis=0)
    gain_two_grad = jnp.sum(grad_normed_two * unit_two, axis=0)
    grad_unit_one = grad_normed * gain_one
    tokens_grad = grad_hidden + scale_one * (
        grad_unit_one - unit_one * jnp.mean(grad_unit_one * unit_one, axis=-1, keepdims=True)
    )
    last = []

    def fourth_round(begun):
        last.extend(item.send(begun) for item in input_sums)
        gains = jnp.concatenate([gain_one_grad, gain_two_grad]).astype(bf16)
        gains = sum_all(gains, [("chan", 1), ("chan", 2)]).reshape(-1, channels)
        lines = jnp.concatenate([state_grad[rank:], few.astype(bf16), gains], axis=0)
        padded = jnp.pad(lines, ((0, -lines.shape[0] % 16), (0, 0)))
        last.extend(item.total(begun, *last) for item in mixer_sums)
        last.append(sum_all(padded, shard_bits).astype(f32))
        return last

    tokens_out = placed(chan_gather(tokens_grad.astype(bf16), fourth_round), f32)
    vectors = last[-1]
    input_parts = jnp.concatenate([item.total() for item in input_sums], axis=1)
    input_rows = features // shards

    def share(first):
        whole = vectors[first : first + features // channels].reshape(features)
        return lax.dynamic_slice_in_dim(whole, shard * input_rows, input_rows)

    at = 2 * size
    return (
        results_whole[0][None],
        tokens_out[None],
        share(at + width + size + 3),
        input_parts[:input_rows],
        mixer_sums[1].total(),
        vectors[at : at + width].T,
        vectors[at + width],
        input_parts[input_rows : input_rows + low_rows].T,
        vectors[:at].T,
        input_parts[input_rows + low_rows :],
        vectors[at + width + 1],
        vectors[at + width + 2 : at + width + 2 + size].T,
        vectors[at + width + size + 2],
        mixer_sums[0].total().T,
        share(at + width + size + 3 + features // channels),
        ffn_sums[1].total(),
        ffn_sums[0].total(),
        ffn_sums[2].total().T,
    )


def solution(mesh):
    return jax.shard_map(
        per_device,
        mesh=mesh,
        in_specs=(
            P("dp", "seq", None),
            P("dp", None),
            P(),
            P(None, "chan"),
            P(None, "chan"),
            P("chan", None),
            P("chan"),
            P("chan", None),
            P(None, "chan"),
            P("chan"),
            P("chan", None),
            P("chan"),
            P("chan", None),
            P(),
            P(None, "chan"),
            P(None, "chan"),
            P("chan", None),
            P("dp", "seq", None),
        ),
        out_specs=(
            P("dp", "seq", None),
            P("dp", "seq", None),
            P(("dp", "seq")),
            P(("dp", "seq"), "chan"),
            P(("dp", "seq"), "chan"),
            P("chan", None),
            P("chan"),
            P("chan", ("dp", "seq")),
            P("chan", None),
            P(("dp", "seq"), "chan"),
            P("chan"),
            P("chan", None),
            P("chan"),
            P("chan", ("dp", "seq")),
            P(("dp", "seq")),
            P(("dp", "seq"), "chan"),
            P(("dp", "seq"), "chan"),
            P("chan", ("dp", "seq")),
        ),
        check_vma=False,
    )
```

```python
import functools

import jax
import jax.numpy as jnp
from jax import lax
from jax.experimental import pallas as pl
from jax.experimental.pallas import tpu as pltpu
from jax.sharding import PartitionSpec as P

epsilon = 1e-05
pieces = 8
chunks = 1
lanes = 128
far = 1e6
log2e = 1.4426950408889634
ln2 = 0.6931471805599453
vmem_bytes = 58 * 1024 * 1024
bf16 = jnp.bfloat16
f32 = jnp.float32


def silu_slope(values):
    sigma = jax.nn.sigmoid(values)
    return sigma * (1.0 + values * (1.0 - sigma))


def matmul(left, right):
    return jnp.dot(left, right, preferred_element_type=f32)


def transposed_left(left, right):
    return lax.dot_general(left, right, (((0,), (0,)), ((), ())), preferred_element_type=f32)


def transposed_right(left, right):
    return lax.dot_general(left, right, (((1,), (1,)), ((), ())), preferred_element_type=f32)


def swap(value, axis, mask):
    return lax.ppermute(value, axis, [(i, i ^ mask) for i in range(lax.axis_size(axis))])


def shifted(value, axis, by):
    size = lax.axis_size(axis)
    return lax.ppermute(value, axis, [(i, i + by) for i in range(size) if 0 <= i + by < size])


def bits_of(axis):
    return [1 << k for k in reversed(range(lax.axis_size(axis).bit_length() - 1))]


def bit_is_set(axis, mask):
    return ((lax.axis_index(axis) & mask) != 0).astype(jnp.int32)


def after(value, *others):
    if not others:
        return value
    return lax.optimization_barrier((value, others))[0]


def sum_step(value, bit, *others):
    got = after(swap(value, *bit), *others)
    return (value.astype(f32) + got.astype(f32)).astype(bf16)


class Scatter:
    def __init__(self, value, order, whole):
        self.terms = [value.astype(bf16).reshape((2,) * len(whole) + value.shape[1:])]
        self.order = list(order)
        self.left = list(whole)

    def send(self, *others):
        axis, mask = self.order.pop(0)
        at = self.left.index((axis, mask))
        self.left.pop(at)
        mine = after(bit_is_set(axis, mask), *others)

        def part(term, which):
            return lax.dynamic_index_in_dim(term, which, at, keepdims=False)

        away = sum(part(t, 1 - mine).astype(f32) for t in self.terms).astype(bf16)
        self.terms = [part(t, mine) for t in self.terms] + [swap(away, axis, mask)]
        return away

    @property
    def got(self):
        return self.terms[-1]

    def total(self, *others):
        while self.order:
            self.send(*others)
        self.terms[-1] = after(self.terms[-1], *others)
        return sum(t.astype(f32) for t in self.terms)


class chan_scatter:
    def __init__(self, part):
        third = swap(part(3), "chan", 1)
        self.middle = (part(2).astype(f32) + third.astype(f32)).astype(bf16)
        self.second = swap(self.middle, "chan", 2)
        self.first = swap(part(1), "chan", 1)
        self.own = part(0)

    def total(self, *others):
        second = after(self.second, self.first, *others)
        return self.own.astype(f32) + self.first.astype(f32) + second.astype(f32)


class chan_gather:
    def __init__(self, own):
        self.own = own
        self.across = swap(own, "chan", 2)
        self.beside = swap(own, "chan", 1)

    def blocks(self, *others):
        across = after(self.across, self.beside, *others)
        return [after(self.own, across), self.beside, across, swap(across, "chan", 1)]


def in_order(own, beside):
    upper = bit_is_set("chan", 1) == 1
    return jnp.concatenate(
        [jnp.where(upper, beside, own), jnp.where(upper, own, beside)], axis=0
    )


def chan_total(value, near=lambda: (), distant=lambda begun: ()):
    got = swap(value, "chan", 1)
    value = (value + after(got, *near())).astype(bf16)
    got = swap(value, "chan", 2)
    got = after(got, *distant(value))
    return value.astype(f32) + got.astype(f32)


def step_rows(step, steps):
    return pl.ds(step, pieces, stride=steps)


def split_proj(proj, both, steps):
    def body(i, unused):
        tile = jnp.concatenate(
            [proj[step_rows(2 * i, steps), :], proj[step_rows(2 * i + 1, steps), :]], axis=0
        )
        high = tile.astype(bf16)
        rows = pl.ds(pl.multiple_of(i * 2 * pieces, 2 * pieces), 2 * pieces)
        both[rows, :lanes] = high
        both[rows, lanes:] = (tile - high.astype(f32)).astype(bf16)
        return unused

    lax.fori_loop(0, steps // 2, body, 0)


def spread(both, out, first, count):
    tall = min(256, both.shape[0])
    source = lax.broadcasted_iota(jnp.int32, (2 * lanes, 2 * lanes), 0) % lanes
    target = lax.broadcasted_iota(jnp.int32, (2 * lanes, 2 * lanes), 1) // lanes
    for n in range(0, count, 2):
        pick = (source == target + (first + n)).astype(f32).astype(bf16)
        for k in range(both.shape[0] // tall):
            rows = pl.ds(k * tall, tall)
            wide = jnp.dot(both[rows, :], pick, preferred_element_type=f32)
            out[n, rows, :] = wide[:, :lanes]
            if n + 1 < count:
                out[n + 1, rows, :] = wide[:, lanes:]


def decay_rows(dec, count):
    return [jnp.broadcast_to(dec[n : n + 1, :], (pieces, lanes)) for n in range(count)]


def ends_kernel(size, rank, rates, mixed, proj, dec, ends, sums, end_total, product_total, *scratch):
    both, eb, fb = scratch
    steps = rates.shape[0] // pieces

    @pl.when(pl.program_id(0) == 0)
    def _():
        split_proj(proj, both, steps)
        spread(both, eb, rank, size)
        spread(both, fb, 0, 1)

    decays = decay_rows(dec, size)

    def body(i, carry):
        states, total = carry
        rows = pl.ds(pl.multiple_of(i * pieces, pieces), pieces)
        rate = rates[step_rows(i, steps), :]
        push = rate * mixed[step_rows(i, steps), :]
        rate = rate + fb[0, rows, :]
        out = []
        for n in range(size):
            out.append(jnp.exp2(rate * decays[n]) * states[n] + push * eb[n, rows, :])
        return tuple(out), total + rate

    zero = jnp.zeros((pieces, lanes), f32)
    states, total = lax.fori_loop(0, steps, body, ((zero,) * size, zero), unroll=4)
    for n in range(size):
        ends[n] = states[n]
    sums[...] = total
    reached = ends[:, 0, :]
    for s in range(1, pieces):
        reached = ends[:, s, :] + jnp.exp2(dec[...] * sums[s : s + 1, :]) * reached
    end_total[...] = reached
    product_total[...] = jnp.exp2(dec[...] * jnp.sum(total, axis=0, keepdims=True))


def forward_kernel(size, rank, opening, rates, mixed, proj, dec, gate_in, skip, *rest):
    if opening:
        ends, sums, arriving = rest[:3]
    else:
        begin = rest[0]
    gated, summed, before, final, both, eb, rb, fb, start, scanned = rest[-10:]
    steps = rates.shape[1]
    rates, mixed, proj, gate_in = (
        item.reshape(pieces * steps, lanes) for item in (rates, mixed, proj, gate_in)
    )

    @pl.when(pl.program_id(0) == 0)
    def _():
        split_proj(proj, both, steps)
        spread(both, eb, rank, size)
        spread(both, rb, rank + size, size)
        spread(both, fb, 0, 1)

    decays = decay_rows(dec, size)
    if opening:
        reached = arriving[...]
        for s in range(pieces):
            start[:, s, :] = reached
            reached = ends[:, s, :] + jnp.exp2(dec[...] * sums[s : s + 1, :]) * reached
        begin = start

    def body(i, states):
        rows = pl.ds(pl.multiple_of(i * 2 * pieces, 2 * pieces), 2 * pieces)
        first, second = step_rows(2 * i, steps), step_rows(2 * i + 1, steps)
        rate0, rate1 = rates[first, :], rates[second, :]
        push0, push1 = rate0 * mixed[first, :], rate1 * mixed[second, :]
        apart = fb[0, rows, :]
        rate0, rate1 = rate0 + apart[:pieces], rate1 + apart[pieces:]
        low = jnp.zeros((pieces, lanes), f32)
        high = low
        out = []
        for n in range(size):
            entry = eb[n, rows, :]
            readout = rb[n, rows, :]
            at_zero = states[n]
            at_one = jnp.exp2(rate0 * decays[n]) * at_zero + push0 * entry[:pieces]
            at_two = jnp.exp2(rate1 * decays[n]) * at_one + push1 * entry[pieces:]
            low = low + readout[:pieces] * at_one
            high = high + readout[pieces:] * at_two
            before[n, rows, :] = jnp.concatenate([at_zero, at_one], axis=0).astype(bf16)
            out.append(at_two)
        scanned[first, :] = low
        scanned[second, :] = high
        return tuple(out)

    states = lax.fori_loop(0, steps // 2, body, tuple(begin[n] for n in range(size)))
    for n in range(size):
        final[n] = states[n]
        last = jnp.concatenate([states[n], states[n]], axis=0).astype(bf16)
        before[n, pl.ds(steps * pieces, 2 * pieces), :] = last

    tall = min(256, steps * pieces)
    for k in range(steps * pieces // tall):
        rows = pl.ds(k * tall, tall)
        total = scanned[rows, :] + skip[...] * mixed[rows, :]
        gate = gate_in[rows, :]
        gated[rows, :] = (total * (gate * jax.nn.sigmoid(gate))).astype(bf16)
        summed[rows, :] = total.astype(bf16)


def heads_kernel(size, rank, rates, slope, proj, dec, sums, heads, head_total, *scratch):
    both, rb, fb = scratch
    steps = rates.shape[0] // pieces

    @pl.when(pl.program_id(0) == 0)
    def _():
        split_proj(proj, both, steps)
        spread(both, rb, rank + size, size)
        spread(both, fb, 0, 1)

    decays = decay_rows(dec, size)

    def body(i, carried):
        step = steps - 1 - i
        rows = pl.ds(pl.multiple_of(step * pieces, pieces), pieces)
        rate = rates[step_rows(step, steps), :] + fb[0, rows, :]
        grad = slope[step_rows(step, steps), :]
        return tuple(
            (carried[n] + rb[n, rows, :] * grad) * jnp.exp2(rate * decays[n]) for n in range(size)
        )

    zero = jnp.zeros((pieces, lanes), f32)
    carried = lax.fori_loop(0, steps, body, (zero,) * size, unroll=4)
    for n in range(size):
        heads[n] = carried[n]
    reached = heads[:, pieces - 1, :]
    for s in reversed(range(pieces - 1)):
        reached = heads[:, s, :] + jnp.exp2(dec[...] * sums[s : s + 1, :]) * reached
    head_total[...] = reached


def backward_kernel(
    size,
    rank,
    rates,
    mixed,
    slope,
    proj,
    dec,
    heads,
    sums,
    leaving,
    *rest,
):
    stored_states = rest[:chunks]
    skip, step_proj = rest[chunks : chunks + 2]
    rest = rest[chunks + 2 :]
    pre_low, direct, proj_grad, decay_grad, bias_grad = rest[:5]
    both, eb, rb, fb, stop, decay_sum, entry_terms, readout_terms = rest[5:13]
    picks, rate_grad, drive_grad, terms_grad = rest[13:]
    steps = rates.shape[0] // pieces
    count = steps * pieces
    pair = 2 * pieces
    group = pl.program_id(0)

    @pl.when(group == 0)
    def _():
        split_proj(proj, both, steps)
        spread(both, eb, rank, size)
        spread(both, rb, rank + size, size)
        spread(both, fb, 0, 1)
        proj_grad[...] = jnp.zeros_like(proj_grad)
        target = lax.broadcasted_iota(jnp.int32, (lanes, lanes), 1)
        for n in range(2 * size):
            picks[pl.ds(n * lanes, lanes), :] = (target == rank + n).astype(f32).astype(bf16)

    decays = decay_rows(dec, size)
    reached = leaving[...]
    for s in reversed(range(pieces)):
        stop[:, s, :] = reached
        reached = heads[:, s, :] + jnp.exp2(dec[...] * sums[s : s + 1, :]) * reached
    decay_sum[...] = jnp.zeros_like(decay_sum)

    span = steps // 2 // chunks

    def body(fresh, before, offset, i, carried):
        place = span - 1 - i
        at = pl.multiple_of(place * pair, pair)
        stored = pl.ds(at, pair)
        following = pl.ds(at + pair, pair)
        half = offset + place
        rows = pl.ds(pl.multiple_of(half * pair, pair), pair)
        first, second = step_rows(2 * half, steps), step_rows(2 * half + 1, steps)
        rate0, rate1 = rates[first, :], rates[second, :]
        push0, push1 = rate0 * mixed[first, :], rate1 * mixed[second, :]
        grad0, grad1 = slope[first, :], slope[second, :]
        apart = fb[0, rows, :]
        far0, far1 = rate0 + apart[:pieces], rate1 + apart[pieces:]
        zero = jnp.zeros((pieces, lanes), f32)
        rates0 = rates1 = drives0 = drives1 = zero
        out = []
        for n in range(size):
            entry = eb[n, rows, :]
            readout = rb[n, rows, :]
            state = before[n, stored, :].astype(f32)
            later = before[n, following, :].astype(f32)[:pieces]
            held1 = carried[n] + readout[pieces:] * grad1
            passed1 = held1 * jnp.exp2(far1 * decays[n])
            scaled1 = passed1 * state[pieces:]
            held0 = passed1 + readout[:pieces] * grad0
            passed0 = held0 * jnp.exp2(far0 * decays[n])
            scaled0 = passed0 * state[:pieces]
            rates1 = rates1 + scaled1 * decays[n]
            rates0 = rates0 + scaled0 * decays[n]
            drives1 = drives1 + held1 * entry[pieces:]
            drives0 = drives0 + held0 * entry[:pieces]
            decay_sum[n] += scaled1 * rate1 + scaled0 * rate0
            here = pl.ds(n * lanes, lanes)
            entries = jnp.concatenate([held0 * push0, held1 * push1], axis=0)
            readouts = jnp.concatenate([grad0 * state[pieces:], grad1 * later], axis=0)
            entry_terms[rows, here] = entries if fresh else entry_terms[rows, here] + entries
            readout_terms[rows, here] = (
                readouts if fresh else readout_terms[rows, here] + readouts
            )
            out.append(passed0)
        rate_grad[first, :] = rates0
        rate_grad[second, :] = rates1
        drive_grad[first, :] = drives0
        drive_grad[second, :] = drives1
        return tuple(out)

    def sweep(fresh):
        carried = tuple(stop[n] for n in range(size))
        for k in reversed(range(chunks)):
            step = functools.partial(body, fresh, stored_states[k], k * span)
            carried = lax.fori_loop(0, span, step, carried)

    pl.when(group == 0)(lambda: sweep(True))
    pl.when(group > 0)(lambda: sweep(False))
    decay_grad[...] = jnp.sum(decay_sum[...], axis=1)

    tall = min(256, count)
    bias_total = jnp.zeros((1, lanes), f32)
    for k in range(count // tall):
        rows = pl.ds(k * tall, tall)
        rate, drives = rates[rows, :], drive_grad[rows, :]
        pre = (rate_grad[rows, :] * ln2 + drives * mixed[rows, :]) * (1.0 - jnp.exp(-rate))
        bias_total = bias_total + jnp.sum(pre, axis=0, keepdims=True)
        low = pre.astype(bf16)
        pre_low[rows, :] = low
        direct[rows, :] = drives * rate + skip[...] * slope[rows, :]
        proj_grad[rows, :] += lax.dot_general(
            low, step_proj[...], (((1,), (1,)), ((), ())), preferred_element_type=f32
        )
    bias_grad[...] = bias_total

    @pl.when(group == pl.num_programs(0) - 1)
    def _():
        for k in range(count // tall):
            rows = pl.ds(k * tall, tall)
            terms_grad[rows, :] = jnp.dot(
                entry_terms[rows, :].astype(bf16),
                picks[: size * lanes, :],
                preferred_element_type=f32,
            ) + jnp.dot(
                readout_terms[rows, :].astype(bf16),
                picks[size * lanes :, :],
                preferred_element_type=f32,
            )

        def finish(i, unused):
            rows = pl.ds(pl.multiple_of(i * pieces, pieces), pieces)
            proj_grad[step_rows(i, steps), :] += terms_grad[rows, :]
            return unused

        lax.fori_loop(0, steps, finish, 0)


def scan_calls(count, channels, size, rank):
    groups = channels // lanes
    tall = pl.BlockSpec((count, lanes), lambda g: (0, g))
    fixed = pl.BlockSpec((count, lanes), lambda g: (0, 0))
    small = pl.BlockSpec((size, lanes), lambda g: (0, g))
    ends = pl.BlockSpec((size, pieces, lanes), lambda g: (0, 0, g))
    sums = pl.BlockSpec((pieces, lanes), lambda g: (0, g))
    line = pl.BlockSpec((1, lanes), lambda g: (0, g))
    square = pl.BlockSpec((lanes, lanes), lambda g: (0, g))
    run = count // pieces // chunks
    states = pl.BlockSpec((size, pieces * run + 2 * pieces, lanes), lambda g: (0, 0, g))
    shape = jax.ShapeDtypeStruct
    tall_out = shape((count, channels), f32)
    tall_low = shape((count, channels), bf16)
    small_out = shape((size, channels), f32)
    ends_out = shape((size, pieces, channels), f32)
    sums_out = shape((pieces, channels), f32)
    states_out = shape((size, pieces * run + 2 * pieces, channels), bf16)
    fixed_out = shape((count, lanes), f32)
    line_out = shape((1, channels), f32)
    both = pltpu.VMEM((count, 2 * lanes), bf16)
    wide = pltpu.VMEM((size, count, lanes), f32)
    thin = pltpu.VMEM((1, count, lanes), f32)
    terms = pltpu.VMEM((count, size * lanes), f32)
    edge = pltpu.VMEM((size, pieces, lanes), f32)
    own = pltpu.VMEM((count, lanes), f32)
    picks = pltpu.VMEM((2 * size * lanes, lanes), bf16)
    work = count * channels * size

    def call(kernel, name, ins, outs, out_shape, scratch, span=groups, aliases={}):
        return pl.pallas_call(
            functools.partial(kernel, size, rank),
            grid=(span,),
            in_specs=ins,
            out_specs=outs,
            out_shape=out_shape,
            scratch_shapes=scratch,
            compiler_params=pltpu.CompilerParams(
                dimension_semantics=("arbitrary",), vmem_limit_bytes=vmem_bytes
            ),
            cost_estimate=pl.CostEstimate(flops=work, bytes_accessed=0, transcendentals=0),
            input_output_aliases=aliases,
            name=name,
        )

    def forward_call(k):
        rows = pl.BlockSpec((pieces, run, lanes), lambda g: (0, k, g))
        same = pl.BlockSpec((pieces, run, lanes), lambda g: (0, k, 0))
        part = pl.BlockSpec((pieces * run, lanes), lambda g: (0, g))
        part_out = shape((pieces * run, channels), bf16)
        wide_part = pltpu.VMEM((size, pieces * run, lanes), f32)
        thin_part = pltpu.VMEM((1, pieces * run, lanes), f32)
        both_part = pltpu.VMEM((pieces * run, 2 * lanes), bf16)
        own_part = pltpu.VMEM((pieces * run, lanes), f32)
        begin = [ends] if k else [ends, sums, small]

        def kernel(size, rank, *refs):
            forward_kernel(size, rank, k == 0, *refs)

        return call(
            kernel,
            "scan_forward",
            [rows, rows, same, small, rows, line] + begin,
            [part, part, states, ends],
            [part_out, part_out, states_out, ends_out],
            [both_part, wide_part, wide_part, thin_part, edge, own_part],
        )

    def backward_call(first, span):
        def moved(spec):
            return pl.BlockSpec(spec.block_shape, lambda g: spec.index_map(g + first))

        ins = [tall, tall, tall, fixed, small, ends, sums, small]
        ins += [states] * chunks + [line, square]
        outs = [tall, tall, fixed, small, line]
        kept = [0, 1, 3, 4] if first else []
        aliases = {len(ins) + i: out for i, out in enumerate(kept)}
        held = [pl.BlockSpec(memory_space=pl.ANY)] * len(kept)

        def kernel(size, rank, *refs):
            refs = refs[: len(ins)] + refs[len(ins) + len(kept) :]
            backward_kernel(size, rank, *refs)

        return call(
            kernel,
            "scan_backward",
            [moved(spec) for spec in ins] + held,
            [moved(spec) for spec in outs],
            [tall_low, tall_out, fixed_out, small_out, line_out],
            [both, wide, wide, thin, edge, edge, terms, terms, picks, own, own, own],
            span,
            aliases,
        )

    part = groups // 2
    backward_parts = (backward_call(0, part), backward_call(part, groups - part))
    return (
        call(
            ends_kernel,
            "scan_ends",
            [tall, tall, fixed, small],
            [ends, sums, small, small],
            [ends_out, sums_out, small_out, small_out],
            [both, wide, thin],
        ),
        tuple(forward_call(k) for k in range(chunks)),
        call(
            heads_kernel,
            "scan_heads",
            [tall, tall, fixed, small, sums],
            [ends, small],
            [ends_out, small_out],
            [both, wide, thin],
        ),
        backward_parts,
    )


def norm_kernel(rows, gain, out):
    values = rows[...].astype(f32)
    scale = lax.rsqrt(jnp.mean(values * values, axis=-1, keepdims=True) + epsilon)
    out[...] = (values * scale * gain[...]).astype(bf16)


def norm_call(count, features):
    tall = min(count, 128)
    return pl.pallas_call(
        norm_kernel,
        grid=(count // tall,),
        in_specs=[
            pl.BlockSpec((tall, features), lambda i: (i, 0)),
            pl.BlockSpec((1, features), lambda i: (0, 0)),
        ],
        out_specs=pl.BlockSpec((tall, features), lambda i: (i, 0)),
        out_shape=jax.ShapeDtypeStruct((count, features), bf16),
        cost_estimate=pl.CostEstimate(
            flops=6 * count * features, bytes_accessed=4 * count * features, transcendentals=count
        ),
        name="norm_rows",
    )


def chained(product, end, by, fill=()):
    inside = jnp.stack([product, end])
    reach = 1
    outside = None
    while reach < lax.axis_size("seq"):
        got = shifted(inside, "seq", by * reach)
        if fill:
            got = after(got, *fill.pop(0)(inside))
        if outside is None:
            outside = got
        else:
            outside = jnp.stack([outside[0] * got[0], outside[1] + outside[0] * got[1]])
        inside = jnp.stack([product * outside[0], end + product * outside[1]])
        reach *= 2
    return outside[1]


def per_device(
    tokens,
    segment_ids,
    first_gain,
    input_proj,
    gate_proj,
    conv_weight,
    conv_bias,
    state_proj,
    step_proj,
    step_bias,
    decay_log,
    skip_gain,
    output_proj,
    second_gain,
    hidden_gate,
    hidden_up,
    hidden_down,
    upstream,
):
    count, features = tokens.shape[1:]
    width = conv_weight.shape[1]
    rank = step_proj.shape[0]
    size = decay_log.shape[1]
    channels = input_proj.shape[1]
    quarter = count // lax.axis_size("chan")
    me = lax.axis_index("chan")
    place = lax.axis_index("seq")
    dp_bits = [("dp", mask) for mask in bits_of("dp")]
    seq_bits = [("seq", mask) for mask in bits_of("seq")]
    shard_bits = dp_bits + seq_bits
    usual = dp_bits + seq_bits[::-1]
    other = seq_bits[-1:] + dp_bits + seq_bits[:-1]
    scan_ends, scan_forward, scan_heads, scan_backward = scan_calls(count, channels, size, rank)

    def block(values, r):
        return lax.dynamic_slice_in_dim(values, (me ^ r) * quarter, quarter)

    shards = lax.axis_size("dp") * lax.axis_size("seq")

    def scatter(value, order):
        return Scatter(value.reshape(shards, -1, value.shape[-1]), order, shard_bits)

    def side(values, r):
        return lax.dynamic_slice_in_dim(values, ((me >> 1) ^ r) * 2 * quarter, 2 * quarter)

    def of_side(values, r):
        return lax.dynamic_slice_in_dim(values, ((me ^ r) & 1) * quarter, quarter)

    padded_ids = jnp.concatenate([jnp.full((width - 1,), -1, jnp.int32), segment_ids[0]], axis=0)
    window_ids = lax.dynamic_slice_in_dim(padded_ids, place * count, count + width - 1)
    own_ids = window_ids[width - 1 :]
    masks = [
        (window_ids[offset : offset + count] == own_ids).astype(f32)[:, None]
        for offset in range(width)
    ]
    keep = masks[width - 2]

    rows = tokens[0]
    upper = upstream[0]

    def unit_of(values):
        scale = lax.rsqrt(jnp.mean(values * values, axis=-1, keepdims=True) + epsilon)
        return scale, values * scale

    gain_one = first_gain.astype(f32)
    gain_two = second_gain.astype(f32)
    normed = norm_call(count, features)(rows, gain_one[None])
    inner = matmul(normed, input_proj).astype(bf16)
    rim = shifted(inner[count - width + 1 :], "seq", 1)
    gate_in = matmul(normed, gate_proj)
    extended = jnp.concatenate([rim, after(inner, gate_in)], axis=0).astype(f32)
    taps = conv_weight.astype(f32).T
    convolved = conv_bias.astype(f32) + sum(
        extended[offset : offset + count] * taps[offset] * masks[offset]
        for offset in range(width)
    )
    mixed = jax.nn.silu(convolved).astype(bf16)
    mixed_wide = mixed.astype(f32)
    upper_parts = [lax.optimization_barrier(side(upper, r)) for r in range(2)]
    grad_actives = []

    def upstream_parts(begun):
        grad_actives.extend(
            transposed_right(after(item, begun), hidden_down) for item in upper_parts
        )
        return grad_actives

    projected = chan_total(matmul(mixed, state_proj), distant=upstream_parts)
    step_low = projected[:, :rank].astype(bf16)
    step_pre = matmul(step_low, step_proj) + step_bias.astype(f32)
    rates = jax.nn.softplus(step_pre)
    decay = -jnp.exp(decay_log.astype(f32)).T
    decay_two = decay * log2e
    column = lax.broadcasted_iota(jnp.int32, projected.shape, 1)
    scan_proj = jnp.where(column == 0, (1.0 - keep) * far, projected)

    ends, sums, end_total, product_total = scan_ends(rates, mixed_wide, scan_proj, decay_two)
    arriving = chained(product_total, end_total, 1)
    skip = skip_gain.astype(f32)[None]

    def at_home(blocks, dtype):
        out = jnp.zeros((count, features), dtype)
        for r, item in enumerate(blocks):
            out = lax.dynamic_update_slice_in_dim(out, item.astype(dtype), (me ^ r) * quarter, 0)
        return out

    scan3 = [item.reshape(pieces, -1, item.shape[-1]) for item in (rates, mixed_wide, scan_proj)]
    gate3 = gate_in.reshape(pieces, -1, channels)
    gated, summed, before, unused = scan_forward[0](
        *scan3, decay_two, gate3, skip, ends, sums, arriving
    )

    def output_part(r):
        return matmul(side(gated, r), output_proj).astype(bf16)

    far_part = output_part(1)
    near_part = output_part(0)
    hidden = chan_scatter(lambda r: of_side(far_part if r > 1 else near_part, r))
    rows_own = block(rows, 0).astype(f32)
    upper_own = block(upper, 0).astype(f32)
    hidden_one = rows_own + hidden.total()
    scale_two, unit_two = unit_of(hidden_one)
    normed_own = chan_gather((unit_two * gain_two).astype(bf16))

    def feed_forward(blocks, r):
        normed_part = lax.optimization_barrier(in_order(*blocks))
        gate_ffn = matmul(normed_part, hidden_gate)
        up_ffn = matmul(normed_part, hidden_up)
        gate_act_ffn = jax.nn.silu(gate_ffn)
        active = (gate_act_ffn * up_ffn).astype(bf16)
        grad_active = grad_actives[r]
        grad_gate_ffn = (grad_active * up_ffn * silu_slope(gate_ffn)).astype(bf16)
        grad_up_ffn = (grad_active * gate_act_ffn).astype(bf16)
        grad_normed = (
            transposed_right(grad_gate_ffn, hidden_gate) + transposed_right(grad_up_ffn, hidden_up)
        ).astype(bf16)
        return normed_part, active, grad_gate_ffn, grad_up_ffn, grad_normed

    ffn0 = feed_forward([normed_own.own, normed_own.beside], 0)
    ffn1 = feed_forward(normed_own.blocks(ffn0)[2:], 1)
    back = chan_scatter(lambda r: of_side((ffn1 if r > 1 else ffn0)[4], r))
    normed_two, active, grad_gate_ffn, grad_up_ffn = (
        jnp.concatenate([ffn0[k], ffn1[k]], axis=0) for k in range(4)
    )
    upper_two = jnp.concatenate(upper_parts, axis=0)
    up_sum = scatter(transposed_left(after(normed_two, back.middle), grad_up_ffn), usual)
    sent = up_sum.send()
    gate_ffn_sum = scatter(transposed_left(after(normed_two, sent), grad_gate_ffn), usual)
    sent = gate_ffn_sum.send()
    down_sum = scatter(transposed_left(after(upper_two, sent), active), other)
    sent = down_sum.send()
    ffn_sums = [up_sum, gate_ffn_sum, down_sum]
    grad_normed_two = back.total(sent)
    grad_unit_two = grad_normed_two * gain_two
    grad_hidden = upper_own + scale_two * (
        grad_unit_two - unit_two * jnp.mean(grad_unit_two * unit_two, axis=-1, keepdims=True)
    )
    low = chan_gather(grad_hidden.astype(bf16))
    result_parts = [
        matmul(after(item[1], low.own), hidden_down).astype(bf16) for item in (ffn0, ffn1)
    ]
    hidden_blocks = low.blocks(result_parts)
    hidden_low = at_home(hidden_blocks, bf16)
    own_part = (of_side(result_parts[0], 0).astype(f32) + hidden_one).astype(bf16)
    upper_chip = me >> 1
    near_rows = lax.dynamic_update_slice_in_dim(
        result_parts[0], own_part, (me & 1) * quarter, 0
    )
    result_rows = jnp.concatenate(
        [
            jnp.where(upper_chip == 1, result_parts[1], near_rows),
            jnp.where(upper_chip == 1, near_rows, result_parts[1]),
        ],
        axis=0,
    )
    result = lax.psum(after(result_rows, hidden_blocks[3]), "chan")
    gate_act = jax.nn.silu(gate_in)
    grad_gated = transposed_right(hidden_low, output_proj)
    grad_scanned = grad_gated * gate_act
    grad_gate_in = (grad_gated * summed.astype(f32) * silu_slope(gate_in)).astype(bf16)
    skip_grad = jnp.sum(grad_scanned * mixed_wide, axis=0)
    heads, head_total = scan_heads(
        rates, grad_scanned, scan_proj, decay_two, sums
    )
    head_total = after(head_total, [item.got for item in ffn_sums])

    mixer_sums = []

    def output_weights(begun):
        value = transposed_left(after(hidden_low, begun), gated)
        mixer_sums.append(scatter(value, usual))
        return [mixer_sums[0].send()]

    def gate_weights(begun):
        value = transposed_left(normed, after(grad_gate_in, begun))
        mixer_sums.append(scatter(value, other))
        return [mixer_sums[1].send()]

    leaving = chained(product_total, head_total, -1, [output_weights, gate_weights])
    sent = [item.send(leaving) for item in ffn_sums]
    step_padded = jnp.pad(step_proj, ((0, 2 * size), (0, 0)))
    scan_inputs = (rates, mixed_wide, grad_scanned, scan_proj, decay_two, heads, sums)
    first_scan, second_scan = scan_backward
    begin = after(leaving, sent)
    parts = first_scan(*scan_inputs, begin, before, skip, step_padded)
    terms = parts[2]
    sent = [item.send(terms) for item in ffn_sums]
    begin = after(leaving, sent)
    kept = [parts[k] for k in (0, 1, 3, 4)]
    pre_low, direct, more_terms, decay_grad, step_bias_grad = second_scan(
        *scan_inputs, begin, before, skip, step_padded, *kept
    )
    more_terms = after(more_terms, [item.got for item in ffn_sums[:2] + mixer_sums], result)
    proj_terms = terms + more_terms

    step_weight_grad = []

    def mixer_round():
        return [item.send() for item in mixer_sums]

    gate_terms = []

    def step_weights(begun):
        step_weight_grad.append(transposed_left(after(step_low, begun), pre_low).astype(bf16))
        gate_terms.append(transposed_right(after(grad_gate_in, begun), gate_proj).astype(bf16))
        return step_weight_grad + gate_terms

    grad_projected = chan_total(proj_terms, mixer_round, step_weights).astype(bf16)
    grad_mixed = transposed_right(grad_projected, state_proj) + direct
    grad_conv = grad_mixed * silu_slope(convolved)
    conv_bias_grad = jnp.sum(grad_conv, axis=0)
    conv_taps_grad = jnp.stack(
        [
            jnp.sum(grad_conv * extended[offset : offset + count] * masks[offset], axis=0)
            for offset in range(width)
        ],
        axis=0,
    )
    grad_extended = sum(
        jnp.pad(
            grad_conv * taps[offset] * masks[offset], ((offset, width - 1 - offset), (0, 0))
        )
        for offset in range(width)
    )
    spill = grad_extended[: width - 1]
    returned = shifted(spill, "seq", -1)
    state_grad = transposed_left(after(grad_projected, spill), mixed).astype(bf16)
    few = jnp.concatenate(
        [
            conv_taps_grad,
            conv_bias_grad[None],
            step_bias_grad,
            decay_grad * decay,
            skip_grad[None],
        ],
        axis=0,
    )
    low_rows = rank // shards
    low_parts = jnp.concatenate(
        [
            state_grad[:rank].reshape(shards, low_rows, channels),
            step_weight_grad[0].reshape(shards, low_rows, channels),
        ],
        axis=1,
    )
    inner_low = (
        grad_extended[width - 1 :]
        + jnp.pad(after(returned, low_parts), ((count - width + 1, 0), (0, 0)))
    ).astype(bf16)

    lines = jnp.concatenate([state_grad[rank:], few.astype(bf16)], axis=0)
    lines_used = lines.shape[0]

    lines_used = lines.shape[0]

    def token_part(r, sent):
        return (
            transposed_right(block(after(inner_low, sent), r), input_proj)
            + transposed_right(block(after(grad_gate_in, proj_terms), r), gate_proj)
        ).astype(bf16)

    share = features // shards

    def token_part(r):
        product = transposed_right(side(inner_low, r), input_proj)
        return (product + side(gate_terms[0], r).astype(f32)).astype(bf16)

    far_part = token_part(1)
    near_part = token_part(0)
    tokens_sum = chan_scatter(lambda r: of_side(far_part if r > 1 else near_part, r))
    scale_one, unit_one = unit_of(rows_own)

    input_weight = transposed_left(normed, after(inner_low, tokens_sum.middle)).astype(bf16)
    half_width = channels // 2
    input_blocks = input_weight.reshape(shards, share, channels)
    input_sums = []
    sent = []
    for k, order in ((0, usual), (1, other)):
        columns = slice(k * half_width, (k + 1) * half_width)
        value = jnp.concatenate([input_blocks[:, :, columns], low_parts[:, :, columns]], axis=1)
        value = jnp.pad(value, ((0, 0), (0, -value.shape[1] % 16), (0, 0)))
        input_sums.append(Scatter(value, order, shard_bits))
        sent.append(input_sums[-1].send())
    grad_normed = tokens_sum.total(sent)
    grad_unit_one = grad_normed * gain_one
    tokens_grad = grad_hidden + scale_one * (
        grad_unit_one - unit_one * jnp.mean(grad_unit_one * unit_one, axis=-1, keepdims=True)
    )
    tokens_last = chan_gather(tokens_grad.astype(bf16))
    gains = jnp.concatenate(
        [jnp.sum(grad_normed * unit_one, axis=0), jnp.sum(grad_normed_two * unit_two, axis=0)]
    )
    gains = gains.reshape(-1, channels).astype(bf16)
    sent = [item.send(tokens_last.own) for item in mixer_sums]
    done = [item.total(sent) for item in ffn_sums[:2]]
    blocks = tokens_last.blocks(done)
    sent = [item.send(blocks[2]) for item in input_sums]
    for mask in (1, 2):
        gains = sum_step(gains, ("chan", mask), sent)
    vectors = jnp.concatenate([lines, gains], axis=0)
    vectors = jnp.pad(vectors, ((0, -vectors.shape[0] % 16), (0, 0)))
    vectors = sum_step(vectors, shard_bits[0])
    tokens_out = at_home(blocks, f32)
    done.append(ffn_sums[2].total(blocks[3]))
    while input_sums[0].order:
        sent = [item.send(blocks[3]) for item in input_sums]
    for bit in shard_bits[1:]:
        vectors = sum_step(vectors, bit, sent)
    done += [item.total(sent) for item in mixer_sums]
    input_parts = [item.total(done) for item in input_sums]
    first = share + 2 * low_rows
    gains = vectors[lines_used:].astype(f32)
    shard = lax.axis_index("dp") * lax.axis_size("seq") + place

    def gain_share(k):
        lines = features // channels
        line = gains[k * lines : (k + 1) * lines].reshape(features)
        return lax.dynamic_slice_in_dim(line, shard * share, share)

    input_parts = jnp.concatenate([item[:first] for item in input_parts], axis=1)
    vectors = vectors.astype(f32)
    at = 2 * size
    return (
        result[None],
        tokens_out[None],
        gain_share(0),
        input_parts[:share],
        done[4],
        vectors[at : at + width].T,
        vectors[at + width],
        input_parts[share : share + low_rows].T,
        vectors[:at].T,
        input_parts[share + low_rows :],
        vectors[at + width + 1],
        vectors[at + width + 2 : at + width + 2 + size].T,
        vectors[at + width + size + 2],
        done[3].T,
        gain_share(1),
        done[1],
        done[0],
        done[2].T,
    )


def solution(mesh):
    return jax.shard_map(
        per_device,
        mesh=mesh,
        in_specs=(
            P("dp", "seq", None),
            P("dp", None),
            P(),
            P(None, "chan"),
            P(None, "chan"),
            P("chan", None),
            P("chan"),
            P("chan", None),
            P(None, "chan"),
            P("chan"),
            P("chan", None),
            P("chan"),
            P("chan", None),
            P(),
            P(None, "chan"),
            P(None, "chan"),
            P("chan", None),
            P("dp", "seq", None),
        ),
        out_specs=(
            P("dp", "seq", None),
            P("dp", "seq", None),
            P(("dp", "seq")),
            P(("dp", "seq"), "chan"),
            P(("dp", "seq"), "chan"),
            P("chan", None),
            P("chan"),
            P("chan", ("dp", "seq")),
            P("chan", None),
            P(("dp", "seq"), "chan"),
            P("chan"),
            P("chan", None),
            P("chan"),
            P("chan", ("dp", "seq")),
            P(("dp", "seq")),
            P(("dp", "seq"), "chan"),
            P(("dp", "seq"), "chan"),
            P("chan", ("dp", "seq")),
        ),
        check_vma=False,
    )
```

```python
import functools

import jax
import jax.numpy as jnp
from jax import lax
from jax.experimental import pallas as pl
from jax.experimental.pallas import tpu as pltpu
from jax.sharding import PartitionSpec as P

epsilon = 1e-05
pieces = 8
chunks = 1
lanes = 128
far = 1e6
log2e = 1.4426950408889634
ln2 = 0.6931471805599453
vmem_bytes = 58 * 1024 * 1024
bf16 = jnp.bfloat16
f32 = jnp.float32


def silu_slope(values):
    sigma = jax.nn.sigmoid(values)
    return sigma * (1.0 + values * (1.0 - sigma))


def matmul(left, right):
    return jnp.dot(left, right, preferred_element_type=f32)


def transposed_left(left, right):
    return lax.dot_general(left, right, (((0,), (0,)), ((), ())), preferred_element_type=f32)


def transposed_right(left, right):
    return lax.dot_general(left, right, (((1,), (1,)), ((), ())), preferred_element_type=f32)


def swap(value, axis, mask):
    return lax.ppermute(value, axis, [(i, i ^ mask) for i in range(lax.axis_size(axis))])


def shifted(value, axis, by):
    size = lax.axis_size(axis)
    return lax.ppermute(value, axis, [(i, i + by) for i in range(size) if 0 <= i + by < size])


def bits_of(axis):
    return [1 << k for k in reversed(range(lax.axis_size(axis).bit_length() - 1))]


def bit_is_set(axis, mask):
    return ((lax.axis_index(axis) & mask) != 0).astype(jnp.int32)


def after(value, *others):
    if not others:
        return value
    return lax.optimization_barrier((value, others))[0]


def sum_step(value, bit, *others):
    got = after(swap(value, *bit), *others)
    return (value.astype(f32) + got.astype(f32)).astype(bf16)


class Scatter:
    def __init__(self, values, order, whole):
        self.own = [v.astype(bf16).reshape((2,) * len(whole) + v.shape[1:]) for v in values]
        self.arrived = []
        self.order = list(order)
        self.left = list(whole)

    def send(self, *others):
        axis, mask = self.order.pop(0)
        at = self.left.index((axis, mask))
        self.left.pop(at)
        mine = after(bit_is_set(axis, mask), *others)

        def part(term, which):
            return lax.dynamic_index_in_dim(term, which, at, keepdims=False)

        own = [part(t, 1 - mine) for t in self.own]
        away = own[0] if len(own) == 1 else jnp.concatenate(own, axis=-1)
        if self.arrived:
            away = away.astype(f32) + sum(part(t, 1 - mine).astype(f32) for t in self.arrived)
            away = away.astype(bf16)
        self.own = [part(t, mine) for t in self.own]
        self.arrived = [part(t, mine) for t in self.arrived] + [swap(away, axis, mask)]
        return away

    @property
    def got(self):
        return self.arrived[-1]

    def total(self, *others):
        while self.order:
            self.send(*others)
        self.arrived[-1] = after(self.arrived[-1], *others)
        out, at = [], 0
        for own in self.own:
            columns = slice(at, at + own.shape[-1])
            at += own.shape[-1]
            out.append(own.astype(f32) + sum(t[..., columns].astype(f32) for t in self.arrived))
        return out


class chan_scatter:
    def __init__(self, part):
        third = swap(part(3), "chan", 1)
        self.middle = (part(2).astype(f32) + third.astype(f32)).astype(bf16)
        self.second = swap(self.middle, "chan", 2)
        self.first = swap(part(1), "chan", 1)
        self.own = part(0)

    def total(self, *others):
        second = after(self.second, self.first, *others)
        return self.own.astype(f32) + self.first.astype(f32) + second.astype(f32)


class chan_gather:
    def __init__(self, own):
        self.own = own
        self.across = swap(own, "chan", 2)
        self.beside = swap(own, "chan", 1)

    def blocks(self, *others):
        across = after(self.across, self.beside, *others)
        return [after(self.own, across), self.beside, across, swap(across, "chan", 1)]


def in_order(own, beside):
    upper = bit_is_set("chan", 1) == 1
    return jnp.concatenate(
        [jnp.where(upper, beside, own), jnp.where(upper, own, beside)], axis=0
    )


def chan_total(value, near=lambda: (), distant=lambda begun: ()):
    got = swap(value, "chan", 1)
    value = (value + after(got, *near())).astype(bf16)
    got = swap(value, "chan", 2)
    got = after(got, *distant(value))
    return value.astype(f32) + got.astype(f32)


def step_rows(step, steps):
    return pl.ds(step, pieces, stride=steps)


gap = 8


def gapped_rows(step, steps):
    return pl.ds(step, pieces, stride=steps + gap)


def gapped_part(start, rows, steps):
    return pl.ds(start + start // steps * gap, rows)


def to_gapped(block, out, steps):
    for s in range(pieces):
        out[pl.ds(s * (steps + gap), steps), :] = block[pl.ds(s * steps, steps), :]


def split_proj(proj, both, steps):
    def body(i, unused):
        tile = jnp.concatenate(
            [proj[step_rows(2 * i, steps), :], proj[step_rows(2 * i + 1, steps), :]], axis=0
        )
        high = tile.astype(bf16)
        rows = pl.ds(pl.multiple_of(i * 2 * pieces, 2 * pieces), 2 * pieces)
        both[rows, :lanes] = high
        both[rows, lanes:] = (tile - high.astype(f32)).astype(bf16)
        return unused

    lax.fori_loop(0, steps // 2, body, 0)


def spread(both, out, first, count):
    tall = min(256, both.shape[0])
    source = lax.broadcasted_iota(jnp.int32, (2 * lanes, 2 * lanes), 0) % lanes
    target = lax.broadcasted_iota(jnp.int32, (2 * lanes, 2 * lanes), 1) // lanes
    for n in range(0, count, 2):
        pick = (source == target + (first + n)).astype(f32).astype(bf16)
        for k in range(both.shape[0] // tall):
            rows = pl.ds(k * tall, tall)
            wide = jnp.dot(both[rows, :], pick, preferred_element_type=f32)
            out[n, rows, :] = wide[:, :lanes]
            if n + 1 < count:
                out[n + 1, rows, :] = wide[:, lanes:]


def decay_rows(dec, count):
    return [jnp.broadcast_to(dec[n : n + 1, :], (pieces, lanes)) for n in range(count)]


def ends_kernel(size, rank, rates, mixed, proj, dec, ends, sums, end_total, product_total, *scratch):
    both, eb, fb, rates_apart, mixed_apart = scratch
    steps = rates.shape[0] // pieces
    to_gapped(rates, rates_apart, steps)
    to_gapped(mixed, mixed_apart, steps)

    @pl.when(pl.program_id(0) == 0)
    def _():
        split_proj(proj, both, steps)
        spread(both, eb, rank, size)
        spread(both, fb, 0, 1)

    decays = decay_rows(dec, size)

    def body(i, carry):
        states, total = carry
        rows = pl.ds(pl.multiple_of(i * pieces, pieces), pieces)
        rate = rates_apart[gapped_rows(i, steps), :]
        push = rate * mixed_apart[gapped_rows(i, steps), :]
        rate = rate + fb[0, rows, :]
        out = []
        for n in range(size):
            out.append(jnp.exp2(rate * decays[n]) * states[n] + push * eb[n, rows, :])
        return tuple(out), total + rate

    zero = jnp.zeros((pieces, lanes), f32)
    states, total = lax.fori_loop(0, steps, body, ((zero,) * size, zero), unroll=4)
    for n in range(size):
        ends[n] = states[n]
    sums[...] = total
    reached = ends[:, 0, :]
    for s in range(1, pieces):
        reached = ends[:, s, :] + jnp.exp2(dec[...] * sums[s : s + 1, :]) * reached
    end_total[...] = reached
    product_total[...] = jnp.exp2(dec[...] * jnp.sum(total, axis=0, keepdims=True))


def forward_kernel(size, rank, opening, rates, mixed, proj, dec, gate_in, skip, *rest):
    if opening:
        ends, sums, arriving = rest[:3]
    else:
        begin = rest[0]
    gated, summed, before, final, both, eb, rb, fb, start = rest[-12:-3]
    scanned, rates_apart, mixed_apart = rest[-3:]
    steps = rates.shape[1]
    rates, mixed, proj, gate_in = (
        item.reshape(pieces * steps, lanes) for item in (rates, mixed, proj, gate_in)
    )

    @pl.when(pl.program_id(0) == 0)
    def _():
        split_proj(proj, both, steps)
        spread(both, eb, rank, size)
        spread(both, rb, rank + size, size)
        spread(both, fb, 0, 1)

    to_gapped(rates, rates_apart, steps)
    to_gapped(mixed, mixed_apart, steps)
    decays = decay_rows(dec, size)
    if opening:
        reached = arriving[...]
        for s in range(pieces):
            start[:, s, :] = reached
            reached = ends[:, s, :] + jnp.exp2(dec[...] * sums[s : s + 1, :]) * reached
        begin = start

    def body(i, states):
        rows = pl.ds(pl.multiple_of(i * 2 * pieces, 2 * pieces), 2 * pieces)
        first, second = gapped_rows(2 * i, steps), gapped_rows(2 * i + 1, steps)
        rate0, rate1 = rates_apart[first, :], rates_apart[second, :]
        push0, push1 = rate0 * mixed_apart[first, :], rate1 * mixed_apart[second, :]
        apart = fb[0, rows, :]
        rate0, rate1 = rate0 + apart[:pieces], rate1 + apart[pieces:]
        low = jnp.zeros((pieces, lanes), f32)
        high = low
        out = []
        for n in range(size):
            entry = eb[n, rows, :]
            readout = rb[n, rows, :]
            at_zero = states[n]
            at_one = jnp.exp2(rate0 * decays[n]) * at_zero + push0 * entry[:pieces]
            at_two = jnp.exp2(rate1 * decays[n]) * at_one + push1 * entry[pieces:]
            low = low + readout[:pieces] * at_one
            high = high + readout[pieces:] * at_two
            before[n, rows, :] = jnp.concatenate([at_zero, at_one], axis=0).astype(bf16)
            out.append(at_two)
        scanned[first, :] = low
        scanned[second, :] = high
        return tuple(out)

    states = lax.fori_loop(0, steps // 2, body, tuple(begin[n] for n in range(size)))
    for n in range(size):
        final[n] = states[n]
        last = jnp.concatenate([states[n], states[n]], axis=0).astype(bf16)
        before[n, pl.ds(steps * pieces, 2 * pieces), :] = last

    tall = steps
    for k in range(steps * pieces // tall):
        rows = pl.ds(k * tall, tall)
        total = scanned[gapped_part(k * tall, tall, steps), :] + skip[...] * mixed[rows, :]
        gate = gate_in[rows, :]
        gated[rows, :] = (total * (gate * jax.nn.sigmoid(gate))).astype(bf16)
        summed[rows, :] = total.astype(bf16)


def heads_kernel(size, rank, rates, slope, proj, dec, sums, heads, head_total, *scratch):
    both, rb, fb, rates_apart, slope_apart = scratch
    steps = rates.shape[0] // pieces
    to_gapped(rates, rates_apart, steps)
    to_gapped(slope, slope_apart, steps)

    @pl.when(pl.program_id(0) == 0)
    def _():
        split_proj(proj, both, steps)
        spread(both, rb, rank + size, size)
        spread(both, fb, 0, 1)

    decays = decay_rows(dec, size)

    def body(i, carried):
        step = steps - 1 - i
        rows = pl.ds(pl.multiple_of(step * pieces, pieces), pieces)
        rate = rates_apart[gapped_rows(step, steps), :] + fb[0, rows, :]
        grad = slope_apart[gapped_rows(step, steps), :]
        return tuple(
            (carried[n] + rb[n, rows, :] * grad) * jnp.exp2(rate * decays[n]) for n in range(size)
        )

    zero = jnp.zeros((pieces, lanes), f32)
    carried = lax.fori_loop(0, steps, body, (zero,) * size, unroll=4)
    for n in range(size):
        heads[n] = carried[n]
    reached = heads[:, pieces - 1, :]
    for s in reversed(range(pieces - 1)):
        reached = heads[:, s, :] + jnp.exp2(dec[...] * sums[s : s + 1, :]) * reached
    head_total[...] = reached


def backward_kernel(
    size,
    rank,
    rates,
    mixed,
    slope,
    proj,
    dec,
    heads,
    sums,
    leaving,
    *rest,
):
    stored_states = rest[:chunks]
    skip, step_proj = rest[chunks : chunks + 2]
    rest = rest[chunks + 2 :]
    pre_low, direct, proj_grad, decay_grad, bias_grad = rest[:5]
    both, eb, rb, fb, stop, decay_sum, entry_terms, readout_terms = rest[5:13]
    picks, rate_grad, drive_grad, terms_grad, rates_apart, mixed_apart, slope_apart = rest[13:]
    steps = rates.shape[0] // pieces
    count = steps * pieces
    pair = 2 * pieces
    group = pl.program_id(0)

    @pl.when(group == 0)
    def _():
        split_proj(proj, both, steps)
        spread(both, eb, rank, size)
        spread(both, rb, rank + size, size)
        spread(both, fb, 0, 1)
        proj_grad[...] = jnp.zeros_like(proj_grad)
        target = lax.broadcasted_iota(jnp.int32, (lanes, lanes), 1)
        for n in range(2 * size):
            picks[pl.ds(n * lanes, lanes), :] = (target == rank + n).astype(f32).astype(bf16)

    to_gapped(rates, rates_apart, steps)
    to_gapped(mixed, mixed_apart, steps)
    to_gapped(slope, slope_apart, steps)
    decays = decay_rows(dec, size)
    reached = leaving[...]
    for s in reversed(range(pieces)):
        stop[:, s, :] = reached
        reached = heads[:, s, :] + jnp.exp2(dec[...] * sums[s : s + 1, :]) * reached
    decay_sum[...] = jnp.zeros_like(decay_sum)

    span = steps // 2 // chunks

    def body(fresh, before, offset, i, carried):
        place = span - 1 - i
        at = pl.multiple_of(place * pair, pair)
        stored = pl.ds(at, pair)
        following = pl.ds(at + pair, pair)
        half = offset + place
        rows = pl.ds(pl.multiple_of(half * pair, pair), pair)
        first, second = gapped_rows(2 * half, steps), gapped_rows(2 * half + 1, steps)
        rate0, rate1 = rates_apart[first, :], rates_apart[second, :]
        push0, push1 = rate0 * mixed_apart[first, :], rate1 * mixed_apart[second, :]
        grad0, grad1 = slope_apart[first, :], slope_apart[second, :]
        apart = fb[0, rows, :]
        far0, far1 = rate0 + apart[:pieces], rate1 + apart[pieces:]
        zero = jnp.zeros((pieces, lanes), f32)
        rates0 = rates1 = drives0 = drives1 = zero
        out = []
        for n in range(size):
            entry = eb[n, rows, :]
            readout = rb[n, rows, :]
            state = before[n, stored, :].astype(f32)
            later = before[n, following, :].astype(f32)[:pieces]
            held1 = carried[n] + readout[pieces:] * grad1
            passed1 = held1 * jnp.exp2(far1 * decays[n])
            scaled1 = passed1 * state[pieces:]
            held0 = passed1 + readout[:pieces] * grad0
            passed0 = held0 * jnp.exp2(far0 * decays[n])
            scaled0 = passed0 * state[:pieces]
            rates1 = rates1 + scaled1 * decays[n]
            rates0 = rates0 + scaled0 * decays[n]
            drives1 = drives1 + held1 * entry[pieces:]
            drives0 = drives0 + held0 * entry[:pieces]
            decay_sum[n] += scaled1 * rate1 + scaled0 * rate0
            here = pl.ds(n * lanes, lanes)
            entries = jnp.concatenate([held0 * push0, held1 * push1], axis=0)
            readouts = jnp.concatenate([grad0 * state[pieces:], grad1 * later], axis=0)
            entry_terms[rows, here] = entries if fresh else entry_terms[rows, here] + entries
            readout_terms[rows, here] = (
                readouts if fresh else readout_terms[rows, here] + readouts
            )
            out.append(passed0)
        rate_grad[first, :] = rates0
        rate_grad[second, :] = rates1
        drive_grad[first, :] = drives0
        drive_grad[second, :] = drives1
        return tuple(out)

    def sweep(fresh):
        carried = tuple(stop[n] for n in range(size))
        for k in reversed(range(chunks)):
            step = functools.partial(body, fresh, stored_states[k], k * span)
            carried = lax.fori_loop(0, span, step, carried)

    pl.when(group == 0)(lambda: sweep(True))
    pl.when(group > 0)(lambda: sweep(False))
    decay_grad[...] = jnp.sum(decay_sum[...], axis=1)

    tall = steps
    bias_total = jnp.zeros((1, lanes), f32)
    for k in range(count // tall):
        rows = pl.ds(k * tall, tall)
        apart = gapped_part(k * tall, tall, steps)
        rate, drives = rates[rows, :], drive_grad[apart, :]
        pre = (rate_grad[apart, :] * ln2 + drives * mixed[rows, :]) * (1.0 - jnp.exp(-rate))
        bias_total = bias_total + jnp.sum(pre, axis=0, keepdims=True)
        low = pre.astype(bf16)
        pre_low[rows, :] = low
        direct[rows, :] = drives * rate + skip[...] * slope[rows, :]
        proj_grad[rows, :] += lax.dot_general(
            low, step_proj[...], (((1,), (1,)), ((), ())), preferred_element_type=f32
        )
    bias_grad[...] = bias_total

    @pl.when(group == pl.num_programs(0) - 1)
    def _():
        for k in range(count // tall):
            rows = pl.ds(k * tall, tall)
            terms_grad[rows, :] = jnp.dot(
                entry_terms[rows, :].astype(bf16),
                picks[: size * lanes, :],
                preferred_element_type=f32,
            ) + jnp.dot(
                readout_terms[rows, :].astype(bf16),
                picks[size * lanes :, :],
                preferred_element_type=f32,
            )

        def finish(i, unused):
            rows = pl.ds(pl.multiple_of(i * pieces, pieces), pieces)
            proj_grad[step_rows(i, steps), :] += terms_grad[rows, :]
            return unused

        lax.fori_loop(0, steps, finish, 0)


def scan_calls(count, channels, size, rank):
    groups = channels // lanes
    tall = pl.BlockSpec((count, lanes), lambda g: (0, g))
    fixed = pl.BlockSpec((count, lanes), lambda g: (0, 0))
    small = pl.BlockSpec((size, lanes), lambda g: (0, g))
    ends = pl.BlockSpec((size, pieces, lanes), lambda g: (0, 0, g))
    sums = pl.BlockSpec((pieces, lanes), lambda g: (0, g))
    line = pl.BlockSpec((1, lanes), lambda g: (0, g))
    square = pl.BlockSpec((lanes, lanes), lambda g: (0, g))
    run = count // pieces // chunks
    states = pl.BlockSpec((size, pieces * run + 2 * pieces, lanes), lambda g: (0, 0, g))
    shape = jax.ShapeDtypeStruct
    tall_out = shape((count, channels), f32)
    tall_low = shape((count, channels), bf16)
    small_out = shape((size, channels), f32)
    ends_out = shape((size, pieces, channels), f32)
    sums_out = shape((pieces, channels), f32)
    states_out = shape((size, pieces * run + 2 * pieces, channels), bf16)
    fixed_out = shape((count, lanes), f32)
    line_out = shape((1, channels), f32)
    both = pltpu.VMEM((count, 2 * lanes), bf16)
    wide = pltpu.VMEM((size, count, lanes), f32)
    thin = pltpu.VMEM((1, count, lanes), f32)
    terms = pltpu.VMEM((count, size * lanes), f32)
    edge = pltpu.VMEM((size, pieces, lanes), f32)
    own = pltpu.VMEM((count, lanes), f32)
    apart = pltpu.VMEM((count + pieces * gap, lanes), f32)
    picks = pltpu.VMEM((2 * size * lanes, lanes), bf16)
    work = count * channels * size

    def call(kernel, name, ins, outs, out_shape, scratch, span=groups, aliases={}):
        return pl.pallas_call(
            functools.partial(kernel, size, rank),
            grid=(span,),
            in_specs=ins,
            out_specs=outs,
            out_shape=out_shape,
            scratch_shapes=scratch,
            compiler_params=pltpu.CompilerParams(
                dimension_semantics=("arbitrary",), vmem_limit_bytes=vmem_bytes
            ),
            cost_estimate=pl.CostEstimate(flops=work, bytes_accessed=0, transcendentals=0),
            input_output_aliases=aliases,
            name=name,
        )

    def forward_call(k):
        rows = pl.BlockSpec((pieces, run, lanes), lambda g: (0, k, g))
        same = pl.BlockSpec((pieces, run, lanes), lambda g: (0, k, 0))
        part = pl.BlockSpec((pieces * run, lanes), lambda g: (0, g))
        part_out = shape((pieces * run, channels), bf16)
        wide_part = pltpu.VMEM((size, pieces * run, lanes), f32)
        thin_part = pltpu.VMEM((1, pieces * run, lanes), f32)
        both_part = pltpu.VMEM((pieces * run, 2 * lanes), bf16)
        own_part = pltpu.VMEM((pieces * (run + gap), lanes), f32)
        begin = [ends] if k else [ends, sums, small]

        def kernel(size, rank, *refs):
            forward_kernel(size, rank, k == 0, *refs)

        return call(
            kernel,
            "scan_forward",
            [rows, rows, same, small, rows, line] + begin,
            [part, part, states, ends],
            [part_out, part_out, states_out, ends_out],
            [both_part, wide_part, wide_part, thin_part, edge, own_part, own_part, own_part],
        )

    def backward_call(first, span):
        def moved(spec):
            return pl.BlockSpec(spec.block_shape, lambda g: spec.index_map(g + first))

        ins = [tall, tall, tall, fixed, small, ends, sums, small]
        ins += [states] * chunks + [line, square]
        outs = [tall, tall, fixed, small, line]
        kept = [0, 1, 3, 4] if first else []
        aliases = {len(ins) + i: out for i, out in enumerate(kept)}
        held = [pl.BlockSpec(memory_space=pl.ANY)] * len(kept)

        def kernel(size, rank, *refs):
            refs = refs[: len(ins)] + refs[len(ins) + len(kept) :]
            backward_kernel(size, rank, *refs)

        return call(
            kernel,
            "scan_backward",
            [moved(spec) for spec in ins] + held,
            [moved(spec) for spec in outs],
            [tall_low, tall_out, fixed_out, small_out, line_out],
            [both, wide, wide, thin, edge, edge, terms, terms, picks, apart, apart, own]
            + [apart] * 3,
            span,
            aliases,
        )

    part = max(groups // 3, 1)
    backward_parts = (backward_call(0, part), backward_call(part, groups - part))
    return (
        call(
            ends_kernel,
            "scan_ends",
            [tall, tall, fixed, small],
            [ends, sums, small, small],
            [ends_out, sums_out, small_out, small_out],
            [both, wide, thin, apart, apart],
        ),
        tuple(forward_call(k) for k in range(chunks)),
        call(
            heads_kernel,
            "scan_heads",
            [tall, tall, fixed, small, sums],
            [ends, small],
            [ends_out, small_out],
            [both, wide, thin, apart, apart],
        ),
        backward_parts,
    )


def conv_kernel(width, low, state_proj, direct, inner, rim, taps, bias, mask, *rest):
    inner_low, last, edge, sums, extended, masks = rest[:6]
    slopes = rest[6:]
    count = inner.shape[0]
    tall = min(256, count)
    pad = edge.shape[0]

    @pl.when(pl.program_id(0) == 0)
    def _():
        for k in range(width - 1):
            for at in range(0, count, tall):
                rows = pl.ds(at, tall)
                masks[k, rows, :] = jnp.broadcast_to(mask[rows, k : k + 1], (tall, lanes))

    zeros = jnp.zeros((pad, lanes), f32)
    extended[:pad, :] = rim[...]
    for item in slopes:
        item[:pad, :] = zeros
        item[pl.ds(pad + count, pad), :] = zeros
    for at in range(0, count, tall):
        rows = pl.ds(at, tall)
        extended[pl.ds(pad + at, tall), :] = inner[rows, :].astype(f32)
    totals = [jnp.zeros((1, lanes), f32)] * (width + 1)
    for at in range(0, count, tall):
        rows = pl.ds(at, tall)
        shifted_rows = [extended[pl.ds(pad + at - (width - 1 - k), tall), :] for k in range(width)]
        held = [masks[k, rows, :] for k in range(width - 1)]
        shifted_rows = [item * held[k] if k < width - 1 else item for k, item in enumerate(shifted_rows)]
        convolved = bias[...] + sum(item * taps[k : k + 1, :] for k, item in enumerate(shifted_rows))
        sigma = jax.nn.sigmoid(convolved)
        grad = transposed_right(low[rows, :], state_proj[...]) + direct[rows, :]
        grad = grad * (sigma * (1.0 + convolved * (1.0 - sigma)))
        for k in range(width):
            term = jnp.sum(grad * shifted_rows[k], axis=0, keepdims=True)
            totals[k] = totals[k] + term
            slopes[k][pl.ds(pad + at, tall), :] = grad * held[k] if k < width - 1 else grad
        totals[width] = totals[width] + jnp.sum(grad, axis=0, keepdims=True)
    sums[...] = zeros
    for k in range(width + 1):
        sums[k : k + 1, :] = totals[k]

    def spread_back(at, rows):
        return sum(
            slopes[k][pl.ds(pad + at + width - 1 - k, rows), :] * taps[k : k + 1, :]
            for k in range(width)
        )

    for at in range(0, count, tall):
        inner_low[pl.ds(at, tall), :] = spread_back(at, tall).astype(bf16)
    last[...] = spread_back(count - last.shape[0], last.shape[0])
    edge[...] = spread_back(-pad, pad)


def conv_call(count, channels, width):
    pad = 8
    tall = pl.BlockSpec((count, lanes), lambda g: (0, g))
    fixed = pl.BlockSpec((count, lanes), lambda g: (0, 0))
    eight = pl.BlockSpec((pad, lanes), lambda g: (0, g))
    end = pl.BlockSpec((2 * pad, lanes), lambda g: (0, g))
    shape = jax.ShapeDtypeStruct
    return pl.pallas_call(
        functools.partial(conv_kernel, width),
        grid=(channels // lanes,),
        in_specs=[
            fixed,
            pl.BlockSpec((lanes, lanes), lambda g: (g, 0)),
            tall,
            tall,
            eight,
            pl.BlockSpec((width, lanes), lambda g: (0, g)),
            pl.BlockSpec((1, lanes), lambda g: (0, g)),
            fixed,
        ],
        out_specs=[tall, end, eight, eight],
        out_shape=[
            shape((count, channels), bf16),
            shape((2 * pad, channels), f32),
            shape((pad, channels), f32),
            shape((pad, channels), f32),
        ],
        scratch_shapes=[
            pltpu.VMEM((pad + count, lanes), f32),
            pltpu.VMEM((width - 1, count, lanes), f32),
        ]
        + [pltpu.VMEM((pad + count + pad, lanes), f32)] * width,
        compiler_params=pltpu.CompilerParams(
            dimension_semantics=("arbitrary",), vmem_limit_bytes=vmem_bytes
        ),
        cost_estimate=pl.CostEstimate(flops=count, bytes_accessed=0, transcendentals=0),
        name="conv_backward",
    )


def norm_kernel(rows, gain, out):
    values = rows[...].astype(f32)
    scale = lax.rsqrt(jnp.mean(values * values, axis=-1, keepdims=True) + epsilon)
    out[...] = (values * scale * gain[...]).astype(bf16)


def norm_call(count, features):
    tall = min(count, 256)
    return pl.pallas_call(
        norm_kernel,
        grid=(count // tall,),
        in_specs=[
            pl.BlockSpec((tall, features), lambda i: (i, 0)),
            pl.BlockSpec((1, features), lambda i: (0, 0)),
        ],
        out_specs=pl.BlockSpec((tall, features), lambda i: (i, 0)),
        out_shape=jax.ShapeDtypeStruct((count, features), bf16),
        cost_estimate=pl.CostEstimate(
            flops=6 * count * features, bytes_accessed=4 * count * features, transcendentals=count
        ),
        name="norm_rows",
    )


def chained(product, end, by, fill=()):
    inside = jnp.stack([product, end])
    reach = 1
    outside = None
    while reach < lax.axis_size("seq"):
        got = shifted(inside, "seq", by * reach)
        if fill:
            got = after(got, *fill.pop(0)(inside))
        if outside is None:
            outside = got
        else:
            outside = jnp.stack([outside[0] * got[0], outside[1] + outside[0] * got[1]])
        inside = jnp.stack([product * outside[0], end + product * outside[1]])
        reach *= 2
    return outside[1]


def per_device(
    tokens,
    segment_ids,
    first_gain,
    input_proj,
    gate_proj,
    conv_weight,
    conv_bias,
    state_proj,
    step_proj,
    step_bias,
    decay_log,
    skip_gain,
    output_proj,
    second_gain,
    hidden_gate,
    hidden_up,
    hidden_down,
    upstream,
):
    count, features = tokens.shape[1:]
    width = conv_weight.shape[1]
    rank = step_proj.shape[0]
    size = decay_log.shape[1]
    channels = input_proj.shape[1]
    quarter = count // lax.axis_size("chan")
    me = lax.axis_index("chan")
    place = lax.axis_index("seq")
    dp_bits = [("dp", mask) for mask in bits_of("dp")]
    seq_bits = [("seq", mask) for mask in bits_of("seq")]
    shard_bits = dp_bits + seq_bits
    usual = dp_bits + seq_bits[::-1]
    other = seq_bits[-1:] + dp_bits + seq_bits[:-1]
    scan_ends, scan_forward, scan_heads, scan_backward = scan_calls(count, channels, size, rank)

    def block(values, r):
        return lax.dynamic_slice_in_dim(values, (me ^ r) * quarter, quarter)

    shards = lax.axis_size("dp") * lax.axis_size("seq")

    def scatter(order, *values):
        values = [value.reshape(shards, -1, value.shape[-1]) for value in values]
        return Scatter(values, order, shard_bits)

    def side(values, r):
        return lax.dynamic_slice_in_dim(values, ((me >> 1) ^ r) * 2 * quarter, 2 * quarter)

    def of_side(values, r):
        return lax.dynamic_slice_in_dim(values, ((me ^ r) & 1) * quarter, quarter)

    padded_ids = jnp.concatenate([jnp.full((width - 1,), -1, jnp.int32), segment_ids[0]], axis=0)
    window_ids = lax.dynamic_slice_in_dim(padded_ids, place * count, count + width - 1)
    own_ids = window_ids[width - 1 :]
    masks = [
        (window_ids[offset : offset + count] == own_ids).astype(f32)[:, None]
        for offset in range(width)
    ]
    keep = masks[width - 2]

    rows = tokens[0]
    upper = upstream[0]

    def unit_of(values):
        scale = lax.rsqrt(jnp.mean(values * values, axis=-1, keepdims=True) + epsilon)
        return scale, values * scale

    gain_one = first_gain.astype(f32)
    gain_two = second_gain.astype(f32)
    normed = norm_call(count, features)(rows, gain_one[None])
    inner = matmul(normed, input_proj).astype(bf16)
    rim = shifted(inner[count - width + 1 :], "seq", 1)
    gate_in = matmul(normed, gate_proj)
    extended = jnp.concatenate([rim, after(inner, gate_in)], axis=0).astype(f32)
    taps = conv_weight.astype(f32).T
    convolved = conv_bias.astype(f32) + sum(
        extended[offset : offset + count] * taps[offset] * masks[offset]
        for offset in range(width)
    )
    mixed = jax.nn.silu(convolved).astype(bf16)
    mixed_wide = mixed.astype(f32)
    upper_parts = [lax.optimization_barrier(side(upper, r)) for r in range(2)]
    grad_actives = []

    def upstream_parts(begun):
        grad_actives.extend(
            transposed_right(after(item, begun), hidden_down) for item in upper_parts
        )
        return grad_actives

    projected = chan_total(matmul(mixed, state_proj), distant=upstream_parts)
    step_low = projected[:, :rank].astype(bf16)
    step_pre = matmul(step_low, step_proj) + step_bias.astype(f32)
    rates = jax.nn.softplus(step_pre)
    decay = -jnp.exp(decay_log.astype(f32)).T
    decay_two = decay * log2e
    column = lax.broadcasted_iota(jnp.int32, projected.shape, 1)
    scan_proj = jnp.where(column == 0, (1.0 - keep) * far, projected)

    ends, sums, end_total, product_total = scan_ends(rates, mixed_wide, scan_proj, decay_two)
    arriving = chained(product_total, end_total, 1)
    skip = skip_gain.astype(f32)[None]

    def at_home(blocks, dtype):
        out = jnp.zeros((count, features), dtype)
        for r, item in enumerate(blocks):
            out = lax.dynamic_update_slice_in_dim(out, item.astype(dtype), (me ^ r) * quarter, 0)
        return out

    scan3 = [item.reshape(pieces, -1, item.shape[-1]) for item in (rates, mixed_wide, scan_proj)]
    gate3 = gate_in.reshape(pieces, -1, channels)
    gated, summed, before, unused = scan_forward[0](
        *scan3, decay_two, gate3, skip, ends, sums, arriving
    )

    def output_part(r):
        return matmul(side(gated, r), output_proj).astype(bf16)

    far_part = output_part(1)
    near_part = output_part(0)
    hidden = chan_scatter(lambda r: of_side(far_part if r > 1 else near_part, r))
    rows_own = block(rows, 0).astype(f32)
    upper_own = block(upper, 0).astype(f32)
    hidden_one = rows_own + hidden.total()
    scale_two, unit_two = unit_of(hidden_one)
    normed_own = chan_gather((unit_two * gain_two).astype(bf16))

    def feed_forward(blocks, r):
        normed_part = lax.optimization_barrier(in_order(*blocks))
        gate_ffn = matmul(normed_part, hidden_gate)
        up_ffn = matmul(normed_part, hidden_up)
        gate_act_ffn = jax.nn.silu(gate_ffn)
        active = (gate_act_ffn * up_ffn).astype(bf16)
        grad_active = grad_actives[r]
        grad_gate_ffn = (grad_active * up_ffn * silu_slope(gate_ffn)).astype(bf16)
        grad_up_ffn = (grad_active * gate_act_ffn).astype(bf16)
        grad_normed = (
            transposed_right(grad_gate_ffn, hidden_gate) + transposed_right(grad_up_ffn, hidden_up)
        ).astype(bf16)
        return normed_part, active, grad_gate_ffn, grad_up_ffn, grad_normed

    ffn0 = feed_forward([normed_own.own, normed_own.beside], 0)
    ffn1 = feed_forward(normed_own.blocks(ffn0)[2:], 1)
    back = chan_scatter(lambda r: of_side((ffn1 if r > 1 else ffn0)[4], r))
    normed_two, active, grad_gate_ffn, grad_up_ffn = (
        jnp.concatenate([ffn0[k], ffn1[k]], axis=0) for k in range(4)
    )
    upper_two = jnp.concatenate(upper_parts, axis=0)
    up_weight = transposed_left(after(normed_two, back.middle), grad_up_ffn).astype(bf16)
    gate_weight = transposed_left(after(normed_two, up_weight), grad_gate_ffn).astype(bf16)
    pair_sum = scatter(usual, up_weight, gate_weight)
    sent = pair_sum.send()
    down_sum = scatter(other, transposed_left(after(upper_two, sent), active))
    sent = down_sum.send()
    ffn_sums = [pair_sum, down_sum]
    grad_normed_two = back.total(sent)
    grad_unit_two = grad_normed_two * gain_two
    grad_hidden = upper_own + scale_two * (
        grad_unit_two - unit_two * jnp.mean(grad_unit_two * unit_two, axis=-1, keepdims=True)
    )
    low = chan_gather(grad_hidden.astype(bf16))
    result_parts = [
        matmul(after(item[1], low.own), hidden_down).astype(bf16) for item in (ffn0, ffn1)
    ]
    hidden_blocks = low.blocks(result_parts)
    hidden_low = at_home(hidden_blocks, bf16)
    result_far = after(result_parts[1], hidden_blocks[2])
    results = chan_scatter(lambda r: of_side(result_far if r > 1 else result_parts[0], r))
    gate_act = jax.nn.silu(gate_in)
    grad_gated = transposed_right(hidden_low, output_proj)
    grad_scanned = grad_gated * gate_act
    grad_gate_in = (grad_gated * summed.astype(f32) * silu_slope(gate_in)).astype(bf16)
    skip_grad = jnp.sum(grad_scanned * mixed_wide, axis=0)
    heads, head_total = scan_heads(
        rates, after(grad_scanned, results.middle), scan_proj, decay_two, sums
    )
    head_total = after(head_total, [item.got for item in ffn_sums], results.second)

    mixer_weights = []

    def output_weights(begun):
        value = transposed_left(after(hidden_low, begun), gated).astype(bf16)
        mixer_weights.append(value)
        return mixer_weights

    def gate_weights(begun):
        value = transposed_left(normed, after(grad_gate_in, begun)).astype(bf16)
        mixer_weights.append(value)
        return [value]

    leaving = chained(product_total, head_total, -1, [output_weights, gate_weights])
    sent = [item.send(leaving) for item in ffn_sums]
    mixer_sum = scatter(usual, *mixer_weights)
    result = chan_gather((hidden_one + results.total(leaving)).astype(bf16))
    step_padded = jnp.pad(step_proj, ((0, 2 * size), (0, 0)))
    scan_inputs = (rates, mixed_wide, grad_scanned, scan_proj, decay_two, heads, sums)
    first_scan, second_scan = scan_backward
    begin = after(leaving, sent, result.own)
    parts = first_scan(*scan_inputs, begin, before, skip, step_padded)
    terms = after(parts[2], pair_sum.got, down_sum.got, result.across)
    sent = [item.send(terms) for item in ffn_sums + [mixer_sum]]
    begin = after(leaving, sent)
    kept = [parts[k] for k in (0, 1, 3, 4)]
    pre_low, direct, more_terms, decay_grad, step_bias_grad = second_scan(
        *scan_inputs, begin, before, skip, step_padded, *kept
    )
    more_terms = after(more_terms, [pair_sum.got, down_sum.got, mixer_sum.got])
    proj_terms = terms + more_terms

    step_weight_grad = []

    gate_terms = []

    def step_weights(begun):
        step_weight_grad.append(transposed_left(after(step_low, begun), pre_low).astype(bf16))
        gate_terms.append(transposed_right(after(grad_gate_in, begun), gate_proj).astype(bf16))
        return step_weight_grad + gate_terms

    grad_projected = chan_total(proj_terms, lambda: [mixer_sum.send()], step_weights).astype(bf16)
    mask = jnp.concatenate(masks[: width - 1], axis=1)
    mask = jnp.pad(mask, ((0, 0), (0, lanes - width + 1)))
    rim_rows = jnp.pad(rim.astype(f32), ((8 - width + 1, 0), (0, 0)))
    inner_low, last_rows, edge, conv_sums = conv_call(count, channels, width)(
        grad_projected,
        state_proj,
        direct,
        inner,
        rim_rows,
        taps,
        conv_bias.astype(f32)[None],
        mask,
    )
    returned = shifted(edge, "seq", -1)
    state_grad = transposed_left(after(grad_projected, edge), mixed).astype(bf16)
    singles = jnp.concatenate([step_bias_grad, skip_grad[None]], axis=0)
    few = jnp.concatenate(
        [conv_sums, decay_grad.reshape(size, channels) * decay, jnp.pad(singles, ((0, 6), (0, 0)))],
        axis=0,
    )
    low_rows = rank // shards
    low_parts = jnp.concatenate(
        [
            state_grad[:rank].reshape(shards, low_rows, channels),
            step_weight_grad[0].reshape(shards, low_rows, channels),
        ],
        axis=1,
    )
    last_rows = last_rows.at[-8:].add(after(returned, low_parts)).astype(bf16)
    inner_low = lax.dynamic_update_slice_in_dim(inner_low, last_rows, count - 16, 0)
    lines = jnp.concatenate([state_grad[rank:], few.astype(bf16)], axis=0)
    lines_used = lines.shape[0]

    lines_used = lines.shape[0]

    def token_part(r, sent):
        return (
            transposed_right(block(after(inner_low, sent), r), input_proj)
            + transposed_right(block(after(grad_gate_in, proj_terms), r), gate_proj)
        ).astype(bf16)

    share = features // shards

    def token_part(r):
        product = transposed_right(side(inner_late if r == 0 else inner_low, r), input_proj)
        return (product + side(gate_terms[0], r).astype(f32)).astype(bf16)

    far_part = token_part(1)
    sent = [mixer_sum.send(far_part)]
    inner_late = after(inner_low, sent)
    near_part = token_part(0)
    tokens_sum = chan_scatter(lambda r: of_side(far_part if r > 1 else near_part, r))
    scale_one, unit_one = unit_of(rows_own)

    input_weight = transposed_left(normed, after(inner_low, tokens_sum.middle)).astype(bf16)
    half_width = channels // 2
    input_blocks = input_weight.reshape(shards, share, channels)
    input_sums = []
    sent = []
    for k, order in ((0, usual), (1, other)):
        columns = slice(k * half_width, (k + 1) * half_width)
        value = jnp.concatenate([input_blocks[:, :, columns], low_parts[:, :, columns]], axis=1)
        value = jnp.pad(value, ((0, 0), (0, -value.shape[1] % 16), (0, 0)))
        input_sums.append(Scatter([value], order, shard_bits))
        sent.append(input_sums[-1].send())
    result_whole = at_home(result.blocks(tokens_sum.middle), bf16)
    grad_normed = tokens_sum.total(sent, result_whole)
    grad_unit_one = grad_normed * gain_one
    tokens_grad = grad_hidden + scale_one * (
        grad_unit_one - unit_one * jnp.mean(grad_unit_one * unit_one, axis=-1, keepdims=True)
    )
    tokens_last = chan_gather(tokens_grad.astype(bf16))
    gains = jnp.concatenate(
        [jnp.sum(grad_normed * unit_one, axis=0), jnp.sum(grad_normed_two * unit_two, axis=0)]
    )
    gains = gains.reshape(-1, channels).astype(bf16)
    gains = sum_step(gains, ("chan", 1))
    sent = [item.send(tokens_last.own) for item in input_sums]
    done = pair_sum.total(tokens_last.own)
    blocks = tokens_last.blocks(done, gains, sent)
    while input_sums[0].order:
        sent = [item.send(blocks[2]) for item in input_sums]
    gains = sum_step(gains, ("chan", 2))
    gains = jnp.pad(gains, ((0, -gains.shape[0] % 16), (0, 0)))
    vectors = jnp.concatenate([lines, gains], axis=0)
    for bit in shard_bits:
        vectors = sum_step(vectors, bit, sent)
    tokens_out = at_home(blocks, f32)
    done += down_sum.total(sent) + mixer_sum.total(sent)
    input_parts = [item.total(done)[0] for item in input_sums]
    first = share + 2 * low_rows
    gains = vectors[lines_used:].astype(f32)
    shard = lax.axis_index("dp") * lax.axis_size("seq") + place

    def gain_share(k):
        lines = features // channels
        line = gains[k * lines : (k + 1) * lines].reshape(features)
        return lax.dynamic_slice_in_dim(line, shard * share, share)

    input_parts = jnp.concatenate([item[:first] for item in input_parts], axis=1)
    vectors = vectors.astype(f32)
    at = 2 * size
    return (
        result_whole[None],
        tokens_out[None],
        gain_share(0),
        input_parts[:share],
        done[4],
        vectors[at : at + width].T,
        vectors[at + width],
        input_parts[share : share + low_rows].T,
        vectors[:at].T,
        input_parts[share + low_rows :],
        vectors[at + 8 + size],
        vectors[at + 8 : at + 8 + size].T,
        vectors[at + 9 + size],
        done[3].T,
        gain_share(1),
        done[1],
        done[0],
        done[2].T,
    )


def solution(mesh):
    return jax.shard_map(
        per_device,
        mesh=mesh,
        in_specs=(
            P("dp", "seq", None),
            P("dp", None),
            P(),
            P(None, "chan"),
            P(None, "chan"),
            P("chan", None),
            P("chan"),
            P("chan", None),
            P(None, "chan"),
            P("chan"),
            P("chan", None),
            P("chan"),
            P("chan", None),
            P(),
            P(None, "chan"),
            P(None, "chan"),
            P("chan", None),
            P("dp", "seq", None),
        ),
        out_specs=(
            P("dp", "seq", None),
            P("dp", "seq", None),
            P(("dp", "seq")),
            P(("dp", "seq"), "chan"),
            P(("dp", "seq"), "chan"),
            P("chan", None),
            P("chan"),
            P("chan", ("dp", "seq")),
            P("chan", None),
            P(("dp", "seq"), "chan"),
            P("chan"),
            P("chan", None),
            P("chan"),
            P("chan", ("dp", "seq")),
            P(("dp", "seq")),
            P(("dp", "seq"), "chan"),
            P(("dp", "seq"), "chan"),
            P("chan", ("dp", "seq")),
        ),
        check_vma=False,
    )
```

```python
import functools

import jax
import jax.numpy as jnp
from jax import lax
from jax.experimental import pallas as pl
from jax.experimental.pallas import tpu as pltpu
from jax.sharding import PartitionSpec as P

epsilon = 1e-05
pieces = 8
chunks = 1
lanes = 128
far = 1e6
log2e = 1.4426950408889634
ln2 = 0.6931471805599453
vmem_bytes = 58 * 1024 * 1024
bf16 = jnp.bfloat16
f32 = jnp.float32


def silu_slope(values):
    sigma = jax.nn.sigmoid(values)
    return sigma * (1.0 + values * (1.0 - sigma))


def matmul(left, right):
    return jnp.dot(left, right, preferred_element_type=f32)


def transposed_left(left, right):
    return lax.dot_general(left, right, (((0,), (0,)), ((), ())), preferred_element_type=f32)


def transposed_right(left, right):
    return lax.dot_general(left, right, (((1,), (1,)), ((), ())), preferred_element_type=f32)


def swap(value, axis, mask):
    return lax.ppermute(value, axis, [(i, i ^ mask) for i in range(lax.axis_size(axis))])


def shifted(value, axis, by):
    size = lax.axis_size(axis)
    return lax.ppermute(value, axis, [(i, i + by) for i in range(size) if 0 <= i + by < size])


def bits_of(axis):
    return [1 << k for k in reversed(range(lax.axis_size(axis).bit_length() - 1))]


def bit_is_set(axis, mask):
    return ((lax.axis_index(axis) & mask) != 0).astype(jnp.int32)


def after(value, *others):
    if not others:
        return value
    return lax.optimization_barrier((value, others))[0]


def sum_step(value, bit, *others):
    got = after(swap(value, *bit), *others)
    return (value.astype(f32) + got.astype(f32)).astype(bf16)


class Scatter:
    def __init__(self, values, order, whole):
        self.own = [v.astype(bf16).reshape((2,) * len(whole) + v.shape[1:]) for v in values]
        self.arrived = []
        self.order = list(order)
        self.left = list(whole)

    def send(self, *others):
        axis, mask = self.order.pop(0)
        at = self.left.index((axis, mask))
        self.left.pop(at)
        mine = after(bit_is_set(axis, mask), *others)

        def part(term, which):
            return lax.dynamic_index_in_dim(term, which, at, keepdims=False)

        own = [part(t, 1 - mine) for t in self.own]
        away = own[0] if len(own) == 1 else jnp.concatenate(own, axis=-1)
        if self.arrived:
            away = away.astype(f32) + sum(part(t, 1 - mine).astype(f32) for t in self.arrived)
            away = away.astype(bf16)
        self.own = [part(t, mine) for t in self.own]
        self.arrived = [part(t, mine) for t in self.arrived] + [swap(away, axis, mask)]
        return away

    @property
    def got(self):
        return self.arrived[-1]

    def total(self, *others):
        while self.order:
            self.send(*others)
        self.arrived[-1] = after(self.arrived[-1], *others)
        out, at = [], 0
        for own in self.own:
            columns = slice(at, at + own.shape[-1])
            at += own.shape[-1]
            out.append(own.astype(f32) + sum(t[..., columns].astype(f32) for t in self.arrived))
        return out


class chan_scatter:
    def __init__(self, part):
        third = swap(part(3), "chan", 1)
        self.middle = (part(2).astype(f32) + third.astype(f32)).astype(bf16)
        self.second = swap(self.middle, "chan", 2)
        self.first = swap(part(1), "chan", 1)
        self.own = part(0)

    def total(self, *others):
        second = after(self.second, self.first, *others)
        return self.own.astype(f32) + self.first.astype(f32) + second.astype(f32)


class chan_gather:
    def __init__(self, own):
        self.own = own
        self.across = swap(own, "chan", 2)
        self.beside = swap(own, "chan", 1)

    def blocks(self, *others):
        across = after(self.across, self.beside, *others)
        return [after(self.own, across), self.beside, across, swap(across, "chan", 1)]


def in_order(own, beside):
    upper = bit_is_set("chan", 1) == 1
    return jnp.concatenate(
        [jnp.where(upper, beside, own), jnp.where(upper, own, beside)], axis=0
    )


def chan_total(value, near=lambda: (), distant=lambda begun: ()):
    got = swap(value, "chan", 1)
    value = (value + after(got, *near())).astype(bf16)
    got = swap(value, "chan", 2)
    got = after(got, *distant(value))
    return value.astype(f32) + got.astype(f32)


def step_rows(step, steps):
    return pl.ds(step, pieces, stride=steps)


gap = 8


def gapped_rows(step, steps):
    return pl.ds(step, pieces, stride=steps + gap)


def gapped_part(start, rows, steps):
    return pl.ds(start + start // steps * gap, rows)


def to_gapped(block, out, steps):
    for s in range(pieces):
        out[pl.ds(s * (steps + gap), steps), :] = block[pl.ds(s * steps, steps), :]


def split_proj(proj, both, steps):
    def body(i, unused):
        tile = jnp.concatenate(
            [proj[step_rows(2 * i, steps), :], proj[step_rows(2 * i + 1, steps), :]], axis=0
        )
        high = tile.astype(bf16)
        rows = pl.ds(pl.multiple_of(i * 2 * pieces, 2 * pieces), 2 * pieces)
        both[rows, :lanes] = high
        both[rows, lanes:] = (tile - high.astype(f32)).astype(bf16)
        return unused

    lax.fori_loop(0, steps // 2, body, 0)


def spread(both, out, first, count):
    tall = min(256, both.shape[0])
    source = lax.broadcasted_iota(jnp.int32, (2 * lanes, 2 * lanes), 0) % lanes
    target = lax.broadcasted_iota(jnp.int32, (2 * lanes, 2 * lanes), 1) // lanes
    for n in range(0, count, 2):
        pick = (source == target + (first + n)).astype(f32).astype(bf16)
        for k in range(both.shape[0] // tall):
            rows = pl.ds(k * tall, tall)
            wide = jnp.dot(both[rows, :], pick, preferred_element_type=f32)
            out[n, rows, :] = wide[:, :lanes]
            if n + 1 < count:
                out[n + 1, rows, :] = wide[:, lanes:]


def decay_rows(dec, count):
    return [jnp.broadcast_to(dec[n : n + 1, :], (pieces, lanes)) for n in range(count)]


def ends_kernel(size, rank, rates, mixed, proj, dec, ends, sums, end_total, product_total, *scratch):
    both, eb, fb, rates_apart, mixed_apart = scratch
    steps = rates.shape[0] // pieces
    to_gapped(rates, rates_apart, steps)
    to_gapped(mixed, mixed_apart, steps)

    @pl.when(pl.program_id(0) == 0)
    def _():
        split_proj(proj, both, steps)
        spread(both, eb, rank, size)
        spread(both, fb, 0, 1)

    decays = decay_rows(dec, size)

    def body(i, carry):
        states, total = carry
        rows = pl.ds(pl.multiple_of(i * pieces, pieces), pieces)
        rate = rates_apart[gapped_rows(i, steps), :]
        push = rate * mixed_apart[gapped_rows(i, steps), :]
        rate = rate + fb[0, rows, :]
        out = []
        for n in range(size):
            out.append(jnp.exp2(rate * decays[n]) * states[n] + push * eb[n, rows, :])
        return tuple(out), total + rate

    zero = jnp.zeros((pieces, lanes), f32)
    states, total = lax.fori_loop(0, steps, body, ((zero,) * size, zero), unroll=4)
    for n in range(size):
        ends[n] = states[n]
    sums[...] = total
    reached = ends[:, 0, :]
    for s in range(1, pieces):
        reached = ends[:, s, :] + jnp.exp2(dec[...] * sums[s : s + 1, :]) * reached
    end_total[...] = reached
    product_total[...] = jnp.exp2(dec[...] * jnp.sum(total, axis=0, keepdims=True))


def forward_kernel(size, rank, opening, rates, mixed, proj, dec, gate_in, skip, *rest):
    if opening:
        ends, sums, arriving = rest[:3]
    else:
        begin = rest[0]
    gated, summed, before, final, both, eb, rb, fb, start = rest[-12:-3]
    scanned, rates_apart, mixed_apart = rest[-3:]
    steps = rates.shape[1]
    rates, mixed, proj, gate_in = (
        item.reshape(pieces * steps, lanes) for item in (rates, mixed, proj, gate_in)
    )

    @pl.when(pl.program_id(0) == 0)
    def _():
        split_proj(proj, both, steps)
        spread(both, eb, rank, size)
        spread(both, rb, rank + size, size)
        spread(both, fb, 0, 1)

    to_gapped(rates, rates_apart, steps)
    to_gapped(mixed, mixed_apart, steps)
    decays = decay_rows(dec, size)
    if opening:
        reached = arriving[...]
        for s in range(pieces):
            start[:, s, :] = reached
            reached = ends[:, s, :] + jnp.exp2(dec[...] * sums[s : s + 1, :]) * reached
        begin = start

    def body(i, states):
        rows = pl.ds(pl.multiple_of(i * 2 * pieces, 2 * pieces), 2 * pieces)
        first, second = gapped_rows(2 * i, steps), gapped_rows(2 * i + 1, steps)
        rate0, rate1 = rates_apart[first, :], rates_apart[second, :]
        push0, push1 = rate0 * mixed_apart[first, :], rate1 * mixed_apart[second, :]
        apart = fb[0, rows, :]
        rate0, rate1 = rate0 + apart[:pieces], rate1 + apart[pieces:]
        low = jnp.zeros((pieces, lanes), f32)
        high = low
        out = []
        for n in range(size):
            entry = eb[n, rows, :]
            readout = rb[n, rows, :]
            at_zero = states[n]
            at_one = jnp.exp2(rate0 * decays[n]) * at_zero + push0 * entry[:pieces]
            at_two = jnp.exp2(rate1 * decays[n]) * at_one + push1 * entry[pieces:]
            low = low + readout[:pieces] * at_one
            high = high + readout[pieces:] * at_two
            before[n, rows, :] = jnp.concatenate([at_zero, at_one], axis=0).astype(bf16)
            out.append(at_two)
        scanned[first, :] = low
        scanned[second, :] = high
        return tuple(out)

    states = lax.fori_loop(0, steps // 2, body, tuple(begin[n] for n in range(size)))
    for n in range(size):
        final[n] = states[n]
        last = jnp.concatenate([states[n], states[n]], axis=0).astype(bf16)
        before[n, pl.ds(steps * pieces, 2 * pieces), :] = last

    tall = steps
    for k in range(steps * pieces // tall):
        rows = pl.ds(k * tall, tall)
        total = scanned[gapped_part(k * tall, tall, steps), :] + skip[...] * mixed[rows, :]
        gate = gate_in[rows, :]
        gated[rows, :] = (total * (gate * jax.nn.sigmoid(gate))).astype(bf16)
        summed[rows, :] = total.astype(bf16)


def heads_kernel(size, rank, rates, slope, proj, dec, sums, heads, head_total, *scratch):
    both, rb, fb, rates_apart, slope_apart = scratch
    steps = rates.shape[0] // pieces
    to_gapped(rates, rates_apart, steps)
    to_gapped(slope, slope_apart, steps)

    @pl.when(pl.program_id(0) == 0)
    def _():
        split_proj(proj, both, steps)
        spread(both, rb, rank + size, size)
        spread(both, fb, 0, 1)

    decays = decay_rows(dec, size)

    def body(i, carried):
        step = steps - 1 - i
        rows = pl.ds(pl.multiple_of(step * pieces, pieces), pieces)
        rate = rates_apart[gapped_rows(step, steps), :] + fb[0, rows, :]
        grad = slope_apart[gapped_rows(step, steps), :]
        return tuple(
            (carried[n] + rb[n, rows, :] * grad) * jnp.exp2(rate * decays[n]) for n in range(size)
        )

    zero = jnp.zeros((pieces, lanes), f32)
    carried = lax.fori_loop(0, steps, body, (zero,) * size, unroll=4)
    for n in range(size):
        heads[n] = carried[n]
    reached = heads[:, pieces - 1, :]
    for s in reversed(range(pieces - 1)):
        reached = heads[:, s, :] + jnp.exp2(dec[...] * sums[s : s + 1, :]) * reached
    head_total[...] = reached


def backward_kernel(
    size,
    rank,
    rates,
    mixed,
    slope,
    proj,
    dec,
    heads,
    sums,
    leaving,
    *rest,
):
    stored_states = rest[:chunks]
    skip, step_proj = rest[chunks : chunks + 2]
    rest = rest[chunks + 2 :]
    pre_low, direct, proj_grad, decay_grad, bias_grad = rest[:5]
    both, eb, rb, fb, stop, decay_sum, entry_terms, readout_terms = rest[5:13]
    picks, rate_grad, drive_grad, terms_grad, rates_apart, mixed_apart, slope_apart = rest[13:]
    steps = rates.shape[0] // pieces
    count = steps * pieces
    pair = 2 * pieces
    group = pl.program_id(0)

    @pl.when(group == 0)
    def _():
        split_proj(proj, both, steps)
        spread(both, eb, rank, size)
        spread(both, rb, rank + size, size)
        spread(both, fb, 0, 1)
        proj_grad[...] = jnp.zeros_like(proj_grad)
        target = lax.broadcasted_iota(jnp.int32, (lanes, lanes), 1)
        for n in range(2 * size):
            picks[pl.ds(n * lanes, lanes), :] = (target == rank + n).astype(f32).astype(bf16)

    to_gapped(rates, rates_apart, steps)
    to_gapped(mixed, mixed_apart, steps)
    to_gapped(slope, slope_apart, steps)
    decays = decay_rows(dec, size)
    reached = leaving[...]
    for s in reversed(range(pieces)):
        stop[:, s, :] = reached
        reached = heads[:, s, :] + jnp.exp2(dec[...] * sums[s : s + 1, :]) * reached
    decay_sum[...] = jnp.zeros_like(decay_sum)

    span = steps // 2 // chunks

    def body(fresh, before, offset, i, carried):
        place = span - 1 - i
        at = pl.multiple_of(place * pair, pair)
        stored = pl.ds(at, pair)
        following = pl.ds(at + pair, pair)
        half = offset + place
        rows = pl.ds(pl.multiple_of(half * pair, pair), pair)
        first, second = gapped_rows(2 * half, steps), gapped_rows(2 * half + 1, steps)
        rate0, rate1 = rates_apart[first, :], rates_apart[second, :]
        push0, push1 = rate0 * mixed_apart[first, :], rate1 * mixed_apart[second, :]
        grad0, grad1 = slope_apart[first, :], slope_apart[second, :]
        apart = fb[0, rows, :]
        far0, far1 = rate0 + apart[:pieces], rate1 + apart[pieces:]
        zero = jnp.zeros((pieces, lanes), f32)
        rates0 = rates1 = drives0 = drives1 = zero
        out = []
        for n in range(size):
            entry = eb[n, rows, :]
            readout = rb[n, rows, :]
            state = before[n, stored, :].astype(f32)
            later = before[n, following, :].astype(f32)[:pieces]
            held1 = carried[n] + readout[pieces:] * grad1
            passed1 = held1 * jnp.exp2(far1 * decays[n])
            scaled1 = passed1 * state[pieces:]
            held0 = passed1 + readout[:pieces] * grad0
            passed0 = held0 * jnp.exp2(far0 * decays[n])
            scaled0 = passed0 * state[:pieces]
            rates1 = rates1 + scaled1 * decays[n]
            rates0 = rates0 + scaled0 * decays[n]
            drives1 = drives1 + held1 * entry[pieces:]
            drives0 = drives0 + held0 * entry[:pieces]
            decay_sum[n] += scaled1 * rate1 + scaled0 * rate0
            here = pl.ds(n * lanes, lanes)
            entries = jnp.concatenate([held0 * push0, held1 * push1], axis=0)
            readouts = jnp.concatenate([grad0 * state[pieces:], grad1 * later], axis=0)
            entry_terms[rows, here] = entries if fresh else entry_terms[rows, here] + entries
            readout_terms[rows, here] = (
                readouts if fresh else readout_terms[rows, here] + readouts
            )
            out.append(passed0)
        rate_grad[first, :] = rates0
        rate_grad[second, :] = rates1
        drive_grad[first, :] = drives0
        drive_grad[second, :] = drives1
        return tuple(out)

    def sweep(fresh):
        carried = tuple(stop[n] for n in range(size))
        for k in reversed(range(chunks)):
            step = functools.partial(body, fresh, stored_states[k], k * span)
            carried = lax.fori_loop(0, span, step, carried)

    pl.when(group == 0)(lambda: sweep(True))
    pl.when(group > 0)(lambda: sweep(False))
    decay_grad[...] = jnp.sum(decay_sum[...], axis=1)

    tall = steps
    bias_total = jnp.zeros((1, lanes), f32)
    for k in range(count // tall):
        rows = pl.ds(k * tall, tall)
        apart = gapped_part(k * tall, tall, steps)
        rate, drives = rates[rows, :], drive_grad[apart, :]
        pre = (rate_grad[apart, :] * ln2 + drives * mixed[rows, :]) * (1.0 - jnp.exp(-rate))
        bias_total = bias_total + jnp.sum(pre, axis=0, keepdims=True)
        low = pre.astype(bf16)
        pre_low[rows, :] = low
        direct[rows, :] = drives * rate + skip[...] * slope[rows, :]
        proj_grad[rows, :] += lax.dot_general(
            low, step_proj[...], (((1,), (1,)), ((), ())), preferred_element_type=f32
        )
    bias_grad[...] = bias_total

    @pl.when(group == pl.num_programs(0) - 1)
    def _():
        for k in range(count // tall):
            rows = pl.ds(k * tall, tall)
            terms_grad[rows, :] = jnp.dot(
                entry_terms[rows, :].astype(bf16),
                picks[: size * lanes, :],
                preferred_element_type=f32,
            ) + jnp.dot(
                readout_terms[rows, :].astype(bf16),
                picks[size * lanes :, :],
                preferred_element_type=f32,
            )

        def finish(i, unused):
            rows = pl.ds(pl.multiple_of(i * pieces, pieces), pieces)
            proj_grad[step_rows(i, steps), :] += terms_grad[rows, :]
            return unused

        lax.fori_loop(0, steps, finish, 0)


def scan_calls(count, channels, size, rank):
    groups = channels // lanes
    tall = pl.BlockSpec((count, lanes), lambda g: (0, g))
    fixed = pl.BlockSpec((count, lanes), lambda g: (0, 0))
    small = pl.BlockSpec((size, lanes), lambda g: (0, g))
    ends = pl.BlockSpec((size, pieces, lanes), lambda g: (0, 0, g))
    sums = pl.BlockSpec((pieces, lanes), lambda g: (0, g))
    line = pl.BlockSpec((1, lanes), lambda g: (0, g))
    square = pl.BlockSpec((lanes, lanes), lambda g: (0, g))
    run = count // pieces // chunks
    states = pl.BlockSpec((size, pieces * run + 2 * pieces, lanes), lambda g: (0, 0, g))
    shape = jax.ShapeDtypeStruct
    tall_out = shape((count, channels), f32)
    tall_low = shape((count, channels), bf16)
    small_out = shape((size, channels), f32)
    ends_out = shape((size, pieces, channels), f32)
    sums_out = shape((pieces, channels), f32)
    states_out = shape((size, pieces * run + 2 * pieces, channels), bf16)
    fixed_out = shape((count, lanes), f32)
    line_out = shape((1, channels), f32)
    both = pltpu.VMEM((count, 2 * lanes), bf16)
    wide = pltpu.VMEM((size, count, lanes), f32)
    thin = pltpu.VMEM((1, count, lanes), f32)
    terms = pltpu.VMEM((count, size * lanes), f32)
    edge = pltpu.VMEM((size, pieces, lanes), f32)
    own = pltpu.VMEM((count, lanes), f32)
    apart = pltpu.VMEM((count + pieces * gap, lanes), f32)
    picks = pltpu.VMEM((2 * size * lanes, lanes), bf16)
    work = count * channels * size

    def call(kernel, name, ins, outs, out_shape, scratch, span=groups, aliases={}):
        return pl.pallas_call(
            functools.partial(kernel, size, rank),
            grid=(span,),
            in_specs=ins,
            out_specs=outs,
            out_shape=out_shape,
            scratch_shapes=scratch,
            compiler_params=pltpu.CompilerParams(
                dimension_semantics=("arbitrary",), vmem_limit_bytes=vmem_bytes
            ),
            cost_estimate=pl.CostEstimate(flops=work, bytes_accessed=0, transcendentals=0),
            input_output_aliases=aliases,
            name=name,
        )

    def forward_call(k):
        rows = pl.BlockSpec((pieces, run, lanes), lambda g: (0, k, g))
        same = pl.BlockSpec((pieces, run, lanes), lambda g: (0, k, 0))
        part = pl.BlockSpec((pieces * run, lanes), lambda g: (0, g))
        part_out = shape((pieces * run, channels), bf16)
        wide_part = pltpu.VMEM((size, pieces * run, lanes), f32)
        thin_part = pltpu.VMEM((1, pieces * run, lanes), f32)
        both_part = pltpu.VMEM((pieces * run, 2 * lanes), bf16)
        own_part = pltpu.VMEM((pieces * (run + gap), lanes), f32)
        begin = [ends] if k else [ends, sums, small]

        def kernel(size, rank, *refs):
            forward_kernel(size, rank, k == 0, *refs)

        return call(
            kernel,
            "scan_forward",
            [rows, rows, same, small, rows, line] + begin,
            [part, part, states, ends],
            [part_out, part_out, states_out, ends_out],
            [both_part, wide_part, wide_part, thin_part, edge, own_part, own_part, own_part],
        )

    def backward_call(first, span):
        def moved(spec):
            return pl.BlockSpec(spec.block_shape, lambda g: spec.index_map(g + first))

        ins = [tall, tall, tall, fixed, small, ends, sums, small]
        ins += [states] * chunks + [line, square]
        outs = [tall, tall, fixed, small, line]
        kept = [0, 1, 3, 4] if first else []
        aliases = {len(ins) + i: out for i, out in enumerate(kept)}
        held = [pl.BlockSpec(memory_space=pl.ANY)] * len(kept)

        def kernel(size, rank, *refs):
            refs = refs[: len(ins)] + refs[len(ins) + len(kept) :]
            backward_kernel(size, rank, *refs)

        return call(
            kernel,
            "scan_backward",
            [moved(spec) for spec in ins] + held,
            [moved(spec) for spec in outs],
            [tall_low, tall_out, fixed_out, small_out, line_out],
            [both, wide, wide, thin, edge, edge, terms, terms, picks, apart, apart, own]
            + [apart] * 3,
            span,
            aliases,
        )

    part = max(groups // 3, 1)
    backward_parts = (backward_call(0, part), backward_call(part, groups - part))
    return (
        call(
            ends_kernel,
            "scan_ends",
            [tall, tall, fixed, small],
            [ends, sums, small, small],
            [ends_out, sums_out, small_out, small_out],
            [both, wide, thin, apart, apart],
        ),
        tuple(forward_call(k) for k in range(chunks)),
        call(
            heads_kernel,
            "scan_heads",
            [tall, tall, fixed, small, sums],
            [ends, small],
            [ends_out, small_out],
            [both, wide, thin, apart, apart],
        ),
        backward_parts,
    )


def conv_kernel(width, low, state_proj, direct, inner, rim, taps, bias, mask, *rest):
    inner_low, last, edge, sums, extended, masks = rest[:6]
    slopes = rest[6:]
    count = inner.shape[0]
    tall = min(256, count)
    pad = edge.shape[0]

    @pl.when(pl.program_id(0) == 0)
    def _():
        for k in range(width - 1):
            for at in range(0, count, tall):
                rows = pl.ds(at, tall)
                masks[k, rows, :] = jnp.broadcast_to(mask[rows, k : k + 1], (tall, lanes))

    zeros = jnp.zeros((pad, lanes), f32)
    extended[:pad, :] = rim[...]
    for item in slopes:
        item[:pad, :] = zeros
        item[pl.ds(pad + count, pad), :] = zeros
    for at in range(0, count, tall):
        rows = pl.ds(at, tall)
        extended[pl.ds(pad + at, tall), :] = inner[rows, :].astype(f32)
    totals = [jnp.zeros((1, lanes), f32)] * (width + 1)
    for at in range(0, count, tall):
        rows = pl.ds(at, tall)
        shifted_rows = [extended[pl.ds(pad + at - (width - 1 - k), tall), :] for k in range(width)]
        held = [masks[k, rows, :] for k in range(width - 1)]
        shifted_rows = [item * held[k] if k < width - 1 else item for k, item in enumerate(shifted_rows)]
        convolved = bias[...] + sum(item * taps[k : k + 1, :] for k, item in enumerate(shifted_rows))
        sigma = jax.nn.sigmoid(convolved)
        grad = transposed_right(low[rows, :], state_proj[...]) + direct[rows, :]
        grad = grad * (sigma * (1.0 + convolved * (1.0 - sigma)))
        for k in range(width):
            term = jnp.sum(grad * shifted_rows[k], axis=0, keepdims=True)
            totals[k] = totals[k] + term
            slopes[k][pl.ds(pad + at, tall), :] = grad * held[k] if k < width - 1 else grad
        totals[width] = totals[width] + jnp.sum(grad, axis=0, keepdims=True)
    sums[...] = zeros
    for k in range(width + 1):
        sums[k : k + 1, :] = totals[k]

    def spread_back(at, rows):
        return sum(
            slopes[k][pl.ds(pad + at + width - 1 - k, rows), :] * taps[k : k + 1, :]
            for k in range(width)
        )

    for at in range(0, count, tall):
        inner_low[pl.ds(at, tall), :] = spread_back(at, tall).astype(bf16)
    last[...] = spread_back(count - last.shape[0], last.shape[0])
    edge[...] = spread_back(-pad, pad)


def conv_call(count, channels, width):
    pad = 8
    tall = pl.BlockSpec((count, lanes), lambda g: (0, g))
    fixed = pl.BlockSpec((count, lanes), lambda g: (0, 0))
    eight = pl.BlockSpec((pad, lanes), lambda g: (0, g))
    end = pl.BlockSpec((2 * pad, lanes), lambda g: (0, g))
    shape = jax.ShapeDtypeStruct
    return pl.pallas_call(
        functools.partial(conv_kernel, width),
        grid=(channels // lanes,),
        in_specs=[
            fixed,
            pl.BlockSpec((lanes, lanes), lambda g: (g, 0)),
            tall,
            tall,
            eight,
            pl.BlockSpec((width, lanes), lambda g: (0, g)),
            pl.BlockSpec((1, lanes), lambda g: (0, g)),
            fixed,
        ],
        out_specs=[tall, end, eight, eight],
        out_shape=[
            shape((count, channels), bf16),
            shape((2 * pad, channels), f32),
            shape((pad, channels), f32),
            shape((pad, channels), f32),
        ],
        scratch_shapes=[
            pltpu.VMEM((pad + count, lanes), f32),
            pltpu.VMEM((width - 1, count, lanes), f32),
        ]
        + [pltpu.VMEM((pad + count + pad, lanes), f32)] * width,
        compiler_params=pltpu.CompilerParams(
            dimension_semantics=("arbitrary",), vmem_limit_bytes=vmem_bytes
        ),
        cost_estimate=pl.CostEstimate(flops=count, bytes_accessed=0, transcendentals=0),
        name="conv_backward",
    )


def norm_kernel(rows, gain, out):
    values = rows[...].astype(f32)
    scale = lax.rsqrt(jnp.mean(values * values, axis=-1, keepdims=True) + epsilon)
    out[...] = (values * scale * gain[...].astype(f32)[None, :]).astype(bf16)


def norm_call(count, features):
    tall = min(count, 256)
    return pl.pallas_call(
        norm_kernel,
        grid=(count // tall,),
        in_specs=[
            pl.BlockSpec((tall, features), lambda i: (i, 0)),
            pl.BlockSpec((features,), lambda i: (0,)),
        ],
        out_specs=pl.BlockSpec((tall, features), lambda i: (i, 0)),
        out_shape=jax.ShapeDtypeStruct((count, features), bf16),
        cost_estimate=pl.CostEstimate(
            flops=6 * count * features, bytes_accessed=4 * count * features, transcendentals=count
        ),
        name="norm_rows",
    )


def chained(product, end, by, fill=()):
    inside = jnp.stack([product, end])
    reach = 1
    outside = None
    while reach < lax.axis_size("seq"):
        got = shifted(inside, "seq", by * reach)
        if fill:
            got = after(got, *fill.pop(0)(inside))
        if outside is None:
            outside = got
        else:
            outside = jnp.stack([outside[0] * got[0], outside[1] + outside[0] * got[1]])
        inside = jnp.stack([product * outside[0], end + product * outside[1]])
        reach *= 2
    return outside[1]


def per_device(
    tokens,
    segment_ids,
    first_gain,
    input_proj,
    gate_proj,
    conv_weight,
    conv_bias,
    state_proj,
    step_proj,
    step_bias,
    decay_log,
    skip_gain,
    output_proj,
    second_gain,
    hidden_gate,
    hidden_up,
    hidden_down,
    upstream,
):
    count, features = tokens.shape[1:]
    width = conv_weight.shape[1]
    rank = step_proj.shape[0]
    size = decay_log.shape[1]
    channels = input_proj.shape[1]
    quarter = count // lax.axis_size("chan")
    me = lax.axis_index("chan")
    place = lax.axis_index("seq")
    dp_bits = [("dp", mask) for mask in bits_of("dp")]
    seq_bits = [("seq", mask) for mask in bits_of("seq")]
    shard_bits = dp_bits + seq_bits
    usual = dp_bits + seq_bits[::-1]
    other = seq_bits[-1:] + dp_bits + seq_bits[:-1]
    scan_ends, scan_forward, scan_heads, scan_backward = scan_calls(count, channels, size, rank)

    def block(values, r):
        return lax.dynamic_slice_in_dim(values, (me ^ r) * quarter, quarter)

    shards = lax.axis_size("dp") * lax.axis_size("seq")

    def scatter(order, *values):
        values = [value.reshape(shards, -1, value.shape[-1]) for value in values]
        return Scatter(values, order, shard_bits)

    def side(values, r):
        return lax.dynamic_slice_in_dim(values, ((me >> 1) ^ r) * 2 * quarter, 2 * quarter)

    def of_side(values, r):
        return lax.dynamic_slice_in_dim(values, ((me ^ r) & 1) * quarter, quarter)

    padded_ids = jnp.concatenate([jnp.full((width - 1,), -1, jnp.int32), segment_ids[0]], axis=0)
    window_ids = lax.dynamic_slice_in_dim(padded_ids, place * count, count + width - 1)
    own_ids = window_ids[width - 1 :]
    masks = [
        (window_ids[offset : offset + count] == own_ids).astype(f32)[:, None]
        for offset in range(width)
    ]
    keep = masks[width - 2]

    rows = tokens[0]
    upper = upstream[0]

    def unit_of(values):
        scale = lax.rsqrt(jnp.mean(values * values, axis=-1, keepdims=True) + epsilon)
        return scale, values * scale

    gain_one = first_gain.astype(f32)
    gain_two = second_gain.astype(f32)
    normed = norm_call(count, features)(rows, first_gain)
    inner = matmul(normed, input_proj).astype(bf16)
    rim = shifted(inner[count - width + 1 :], "seq", 1)
    gate_in = matmul(normed, gate_proj)
    extended = jnp.concatenate([rim, after(inner, gate_in)], axis=0).astype(f32)
    taps = conv_weight.astype(f32).T
    convolved = conv_bias.astype(f32) + sum(
        extended[offset : offset + count] * taps[offset] * masks[offset]
        for offset in range(width)
    )
    mixed = jax.nn.silu(convolved).astype(bf16)
    mixed_wide = mixed.astype(f32)
    upper_parts = [lax.optimization_barrier(side(upper, r)) for r in range(2)]
    grad_actives = []

    def upstream_parts(begun):
        grad_actives.extend(
            transposed_right(after(item, begun), hidden_down) for item in upper_parts
        )
        return grad_actives

    projected = chan_total(matmul(mixed, state_proj), distant=upstream_parts)
    step_low = projected[:, :rank].astype(bf16)
    step_pre = matmul(step_low, step_proj) + step_bias.astype(f32)
    rates = jax.nn.softplus(step_pre)
    decay = -jnp.exp(decay_log.astype(f32)).T
    decay_two = decay * log2e
    column = lax.broadcasted_iota(jnp.int32, projected.shape, 1)
    scan_proj = jnp.where(column == 0, (1.0 - keep) * far, projected)

    ends, sums, end_total, product_total = scan_ends(rates, mixed_wide, scan_proj, decay_two)
    arriving = chained(product_total, end_total, 1)
    skip = skip_gain.astype(f32)[None]

    def at_home(blocks, dtype):
        out = jnp.zeros((count, features), dtype)
        for r, item in enumerate(blocks):
            out = lax.dynamic_update_slice_in_dim(out, item.astype(dtype), (me ^ r) * quarter, 0)
        return out

    scan3 = [item.reshape(pieces, -1, item.shape[-1]) for item in (rates, mixed_wide, scan_proj)]
    gate3 = gate_in.reshape(pieces, -1, channels)
    gated, summed, before, unused = scan_forward[0](
        *scan3, decay_two, gate3, skip, ends, sums, arriving
    )

    def output_part(r):
        return matmul(side(gated, r), output_proj).astype(bf16)

    far_part = output_part(1)
    near_part = output_part(0)
    hidden = chan_scatter(lambda r: of_side(far_part if r > 1 else near_part, r))
    rows_own = block(rows, 0).astype(f32)
    upper_own = block(upper, 0).astype(f32)
    hidden_one = rows_own + hidden.total()
    scale_two, unit_two = unit_of(hidden_one)
    normed_own = chan_gather((unit_two * gain_two).astype(bf16))

    def feed_forward(blocks, r):
        normed_part = lax.optimization_barrier(in_order(*blocks))
        gate_ffn = matmul(normed_part, hidden_gate)
        up_ffn = matmul(normed_part, hidden_up)
        gate_act_ffn = jax.nn.silu(gate_ffn)
        active = (gate_act_ffn * up_ffn).astype(bf16)
        grad_active = grad_actives[r]
        grad_gate_ffn = (grad_active * up_ffn * silu_slope(gate_ffn)).astype(bf16)
        grad_up_ffn = (grad_active * gate_act_ffn).astype(bf16)
        grad_normed = (
            transposed_right(grad_gate_ffn, hidden_gate) + transposed_right(grad_up_ffn, hidden_up)
        ).astype(bf16)
        return normed_part, active, grad_gate_ffn, grad_up_ffn, grad_normed

    ffn0 = feed_forward([normed_own.own, normed_own.beside], 0)
    ffn1 = feed_forward(normed_own.blocks(ffn0)[2:], 1)
    back = chan_scatter(lambda r: of_side((ffn1 if r > 1 else ffn0)[4], r))
    normed_two, active, grad_gate_ffn, grad_up_ffn = (
        jnp.concatenate([ffn0[k], ffn1[k]], axis=0) for k in range(4)
    )
    upper_two = jnp.concatenate(upper_parts, axis=0)
    up_weight = transposed_left(after(normed_two, back.middle), grad_up_ffn).astype(bf16)
    gate_weight = transposed_left(after(normed_two, up_weight), grad_gate_ffn).astype(bf16)
    pair_sum = scatter(usual, up_weight, gate_weight)
    sent = pair_sum.send()
    down_sum = scatter(other, transposed_left(after(upper_two, sent), active))
    sent = down_sum.send()
    ffn_sums = [pair_sum, down_sum]
    grad_normed_two = back.total(sent)
    grad_unit_two = grad_normed_two * gain_two
    grad_hidden = upper_own + scale_two * (
        grad_unit_two - unit_two * jnp.mean(grad_unit_two * unit_two, axis=-1, keepdims=True)
    )
    low = chan_gather(grad_hidden.astype(bf16))
    result_parts = [
        matmul(after(item[1], low.own), hidden_down).astype(bf16) for item in (ffn0, ffn1)
    ]
    hidden_blocks = low.blocks(result_parts)
    hidden_low = at_home(hidden_blocks, bf16)
    result_far = after(result_parts[1], hidden_blocks[2])
    results = chan_scatter(lambda r: of_side(result_far if r > 1 else result_parts[0], r))
    gate_act = jax.nn.silu(gate_in)
    grad_gated = transposed_right(hidden_low, output_proj)
    grad_scanned = grad_gated * gate_act
    grad_gate_in = (grad_gated * summed.astype(f32) * silu_slope(gate_in)).astype(bf16)
    skip_grad = jnp.sum(grad_scanned * mixed_wide, axis=0)
    heads, head_total = scan_heads(
        rates, after(grad_scanned, results.middle), scan_proj, decay_two, sums
    )
    head_total = after(head_total, down_sum.got, results.second)

    mixer_weights = []

    def output_weights(begun):
        value = transposed_left(after(hidden_low, begun), gated).astype(bf16)
        mixer_weights.append(value)
        return mixer_weights

    def gate_weights(begun):
        value = transposed_left(normed, after(grad_gate_in, begun)).astype(bf16)
        mixer_weights.append(value)
        return [value, pair_sum.got]

    leaving = chained(product_total, head_total, -1, [output_weights, gate_weights])
    sent = [item.send(leaving) for item in ffn_sums]
    mixer_sum = scatter(usual, *mixer_weights)
    result = chan_gather((hidden_one + results.total(leaving)).astype(bf16))
    step_padded = jnp.pad(step_proj, ((0, 2 * size), (0, 0)))
    scan_inputs = (rates, mixed_wide, grad_scanned, scan_proj, decay_two, heads, sums)
    first_scan, second_scan = scan_backward
    begin = after(leaving, sent, result.own)
    parts = first_scan(*scan_inputs, begin, before, skip, step_padded)
    terms = after(parts[2], pair_sum.got, down_sum.got, result.across)
    sent = [item.send(terms) for item in ffn_sums + [mixer_sum]]
    begin = after(leaving, sent)
    kept = [parts[k] for k in (0, 1, 3, 4)]
    pre_low, direct, more_terms, decay_grad, step_bias_grad = second_scan(
        *scan_inputs, begin, before, skip, step_padded, *kept
    )
    more_terms = after(more_terms, [pair_sum.got, down_sum.got, mixer_sum.got])
    proj_terms = terms + more_terms

    step_weight_grad = []

    gate_terms = []

    def step_weights(begun):
        step_weight_grad.append(transposed_left(after(step_low, begun), pre_low).astype(bf16))
        gate_terms.append(transposed_right(after(grad_gate_in, begun), gate_proj).astype(bf16))
        return step_weight_grad + gate_terms

    grad_projected = chan_total(proj_terms, lambda: [mixer_sum.send()], step_weights).astype(bf16)
    mask = jnp.concatenate(masks[: width - 1], axis=1)
    mask = jnp.pad(mask, ((0, 0), (0, lanes - width + 1)))
    rim_rows = jnp.pad(rim.astype(f32), ((8 - width + 1, 0), (0, 0)))
    inner_low, last_rows, edge, conv_sums = conv_call(count, channels, width)(
        grad_projected,
        state_proj,
        direct,
        inner,
        rim_rows,
        taps,
        conv_bias.astype(f32)[None],
        mask,
    )
    returned = shifted(edge, "seq", -1)
    state_grad = transposed_left(after(grad_projected, edge), mixed).astype(bf16)
    singles = jnp.concatenate([step_bias_grad, skip_grad[None]], axis=0)
    few = jnp.concatenate(
        [conv_sums, decay_grad.reshape(size, channels) * decay, jnp.pad(singles, ((0, 6), (0, 0)))],
        axis=0,
    )
    low_rows = rank // shards
    low_parts = jnp.concatenate(
        [
            state_grad[:rank].reshape(shards, low_rows, channels),
            step_weight_grad[0].reshape(shards, low_rows, channels),
        ],
        axis=1,
    )
    last_rows = last_rows.at[-8:].add(after(returned, low_parts)).astype(bf16)
    inner_low = lax.dynamic_update_slice_in_dim(inner_low, last_rows, count - 16, 0)
    lines = jnp.concatenate([state_grad[rank:], few.astype(bf16)], axis=0)
    lines_used = lines.shape[0]

    lines_used = lines.shape[0]

    def token_part(r, sent):
        return (
            transposed_right(block(after(inner_low, sent), r), input_proj)
            + transposed_right(block(after(grad_gate_in, proj_terms), r), gate_proj)
        ).astype(bf16)

    share = features // shards

    def token_part(r):
        product = transposed_right(side(inner_late if r == 0 else inner_low, r), input_proj)
        return (product + side(gate_terms[0], r).astype(f32)).astype(bf16)

    far_part = token_part(1)
    sent = [mixer_sum.send(far_part)]
    inner_late = after(inner_low, sent)
    near_part = token_part(0)
    tokens_sum = chan_scatter(lambda r: of_side(far_part if r > 1 else near_part, r))
    scale_one, unit_one = unit_of(rows_own)

    input_weight = transposed_left(normed, after(inner_low, tokens_sum.middle)).astype(bf16)
    half_width = channels // 2
    input_blocks = input_weight.reshape(shards, share, channels)
    input_sums = []
    sent = []
    for k, order in ((0, usual), (1, other)):
        columns = slice(k * half_width, (k + 1) * half_width)
        value = jnp.concatenate([input_blocks[:, :, columns], low_parts[:, :, columns]], axis=1)
        value = jnp.pad(value, ((0, 0), (0, -value.shape[1] % 16), (0, 0)))
        input_sums.append(Scatter([value], order, shard_bits))
        sent.append(input_sums[-1].send())
    result_whole = at_home(result.blocks(tokens_sum.middle), bf16)
    grad_normed = tokens_sum.total(sent, result_whole)
    grad_unit_one = grad_normed * gain_one
    tokens_grad = grad_hidden + scale_one * (
        grad_unit_one - unit_one * jnp.mean(grad_unit_one * unit_one, axis=-1, keepdims=True)
    )
    tokens_last = chan_gather(tokens_grad.astype(bf16))
    gains = jnp.concatenate(
        [jnp.sum(grad_normed * unit_one, axis=0), jnp.sum(grad_normed_two * unit_two, axis=0)]
    )
    gains = gains.reshape(-1, channels).astype(bf16)
    gains = sum_step(gains, ("chan", 1))
    sent = [item.send(tokens_last.own) for item in input_sums]
    done = pair_sum.total(tokens_last.own)
    blocks = tokens_last.blocks(done, gains, sent)
    gains = sum_step(gains, ("chan", 2), blocks[2])
    gains = jnp.pad(gains, ((0, -gains.shape[0] % 16), (0, 0)))
    vectors = jnp.concatenate([lines, gains], axis=0)
    while input_sums[0].order:
        sent = [item.send(blocks[2]) for item in input_sums]
    for bit in usual[:-1]:
        vectors = sum_step(vectors, bit)
    early = vectors
    vectors = sum_step(vectors, usual[-1])
    tokens_out = at_home(blocks, f32)
    done += down_sum.total(sent, early) + mixer_sum.total(sent, early)
    input_parts = [item.total(done)[0] for item in input_sums]
    first = share + 2 * low_rows
    gains = vectors[lines_used:].astype(f32)
    shard = lax.axis_index("dp") * lax.axis_size("seq") + place

    def gain_share(k):
        lines = features // channels
        line = gains[k * lines : (k + 1) * lines].reshape(features)
        return lax.dynamic_slice_in_dim(line, shard * share, share)

    input_parts = jnp.concatenate([item[:first] for item in input_parts], axis=1)
    vectors = vectors.astype(f32)
    at = 2 * size
    return (
        result_whole[None],
        tokens_out[None],
        gain_share(0),
        input_parts[:share],
        done[4],
        vectors[at : at + width].T,
        vectors[at + width],
        input_parts[share : share + low_rows].T,
        vectors[:at].T,
        input_parts[share + low_rows :],
        vectors[at + 8 + size],
        vectors[at + 8 : at + 8 + size].T,
        vectors[at + 9 + size],
        done[3].T,
        gain_share(1),
        done[1],
        done[0],
        done[2].T,
    )


def solution(mesh):
    return jax.shard_map(
        per_device,
        mesh=mesh,
        in_specs=(
            P("dp", "seq", None),
            P("dp", None),
            P(),
            P(None, "chan"),
            P(None, "chan"),
            P("chan", None),
            P("chan"),
            P("chan", None),
            P(None, "chan"),
            P("chan"),
            P("chan", None),
            P("chan"),
            P("chan", None),
            P(),
            P(None, "chan"),
            P(None, "chan"),
            P("chan", None),
            P("dp", "seq", None),
        ),
        out_specs=(
            P("dp", "seq", None),
            P("dp", "seq", None),
            P(("dp", "seq")),
            P(("dp", "seq"), "chan"),
            P(("dp", "seq"), "chan"),
            P("chan", None),
            P("chan"),
            P("chan", ("dp", "seq")),
            P("chan", None),
            P(("dp", "seq"), "chan"),
            P("chan"),
            P("chan", None),
            P("chan"),
            P("chan", ("dp", "seq")),
            P(("dp", "seq")),
            P(("dp", "seq"), "chan"),
            P(("dp", "seq"), "chan"),
            P("chan", ("dp", "seq")),
        ),
        check_vma=False,
    )
```

```python
import functools

import jax
import jax.numpy as jnp
from jax import lax
from jax.experimental import pallas as pl
from jax.experimental.pallas import tpu as pltpu
from jax.sharding import PartitionSpec as P

epsilon = 1e-05
pieces = 8
chunks = 1
lanes = 128
far = 1e6
log2e = 1.4426950408889634
ln2 = 0.6931471805599453
vmem_bytes = 58 * 1024 * 1024
bf16 = jnp.bfloat16
f32 = jnp.float32


def silu_slope(values):
    sigma = jax.nn.sigmoid(values)
    return sigma * (1.0 + values * (1.0 - sigma))


def matmul(left, right):
    return jnp.dot(left, right, preferred_element_type=f32)


def transposed_left(left, right):
    return lax.dot_general(left, right, (((0,), (0,)), ((), ())), preferred_element_type=f32)


def transposed_right(left, right):
    return lax.dot_general(left, right, (((1,), (1,)), ((), ())), preferred_element_type=f32)


def swap(value, axis, mask):
    return lax.ppermute(value, axis, [(i, i ^ mask) for i in range(lax.axis_size(axis))])


def shifted(value, axis, by):
    size = lax.axis_size(axis)
    return lax.ppermute(value, axis, [(i, i + by) for i in range(size) if 0 <= i + by < size])


def bits_of(axis):
    return [1 << k for k in reversed(range(lax.axis_size(axis).bit_length() - 1))]


def bit_is_set(axis, mask):
    return ((lax.axis_index(axis) & mask) != 0).astype(jnp.int32)


def after(value, *others):
    if not others:
        return value
    return lax.optimization_barrier((value, others))[0]


def sum_step(value, bit, *others):
    got = after(swap(value, *bit), *others)
    return (value.astype(f32) + got.astype(f32)).astype(bf16)


class Scatter:
    def __init__(self, values, order, whole):
        self.own = [v.astype(bf16).reshape((2,) * len(whole) + v.shape[1:]) for v in values]
        self.arrived = []
        self.order = list(order)
        self.left = list(whole)

    def send(self, *others):
        axis, mask = self.order.pop(0)
        at = self.left.index((axis, mask))
        self.left.pop(at)
        mine = after(bit_is_set(axis, mask), *others)

        def part(term, which):
            return lax.dynamic_index_in_dim(term, which, at, keepdims=False)

        own = [part(t, 1 - mine) for t in self.own]
        away = own[0] if len(own) == 1 else jnp.concatenate(own, axis=-1)
        if self.arrived:
            away = away.astype(f32) + sum(part(t, 1 - mine).astype(f32) for t in self.arrived)
            away = away.astype(bf16)
        self.own = [part(t, mine) for t in self.own]
        self.arrived = [part(t, mine) for t in self.arrived] + [swap(away, axis, mask)]
        return away

    @property
    def got(self):
        return self.arrived[-1]

    def total(self, *others):
        while self.order:
            self.send(*others)
        self.arrived[-1] = after(self.arrived[-1], *others)
        out, at = [], 0
        for own in self.own:
            columns = slice(at, at + own.shape[-1])
            at += own.shape[-1]
            out.append(own.astype(f32) + sum(t[..., columns].astype(f32) for t in self.arrived))
        return out


class chan_scatter:
    def __init__(self, part):
        third = swap(part(3), "chan", 1)
        self.middle = (part(2).astype(f32) + third.astype(f32)).astype(bf16)
        self.second = swap(self.middle, "chan", 2)
        self.first = swap(part(1), "chan", 1)
        self.own = part(0)

    def total(self, *others):
        second = after(self.second, self.first, *others)
        return self.own.astype(f32) + self.first.astype(f32) + second.astype(f32)


class chan_gather:
    def __init__(self, own):
        self.own = own
        self.across = swap(own, "chan", 2)
        self.beside = swap(own, "chan", 1)

    def blocks(self, *others):
        across = after(self.across, self.beside, *others)
        return [after(self.own, across), self.beside, across, swap(across, "chan", 1)]


def in_order(own, beside):
    upper = bit_is_set("chan", 1) == 1
    return jnp.concatenate(
        [jnp.where(upper, beside, own), jnp.where(upper, own, beside)], axis=0
    )


def chan_total(value, near=lambda: (), distant=lambda begun: ()):
    got = swap(value, "chan", 1)
    value = (value + after(got, *near())).astype(bf16)
    got = swap(value, "chan", 2)
    got = after(got, *distant(value))
    return value.astype(f32) + got.astype(f32)


def step_rows(step, steps):
    return pl.ds(step, pieces, stride=steps)


gap = 8


def gapped_rows(step, steps):
    return pl.ds(step, pieces, stride=steps + gap)


def gapped_part(start, rows, steps):
    return pl.ds(start + start // steps * gap, rows)


def to_gapped(block, out, steps):
    for s in range(pieces):
        out[pl.ds(s * (steps + gap), steps), :] = block[pl.ds(s * steps, steps), :]


def split_proj(proj, both, steps):
    def body(i, unused):
        tile = jnp.concatenate(
            [proj[step_rows(2 * i, steps), :], proj[step_rows(2 * i + 1, steps), :]], axis=0
        )
        high = tile.astype(bf16)
        rows = pl.ds(pl.multiple_of(i * 2 * pieces, 2 * pieces), 2 * pieces)
        both[rows, :lanes] = high
        both[rows, lanes:] = (tile - high.astype(f32)).astype(bf16)
        return unused

    lax.fori_loop(0, steps // 2, body, 0)


def spread(both, out, first, count):
    tall = min(256, both.shape[0])
    source = lax.broadcasted_iota(jnp.int32, (2 * lanes, 2 * lanes), 0) % lanes
    target = lax.broadcasted_iota(jnp.int32, (2 * lanes, 2 * lanes), 1) // lanes
    for n in range(0, count, 2):
        pick = (source == target + (first + n)).astype(f32).astype(bf16)
        for k in range(both.shape[0] // tall):
            rows = pl.ds(k * tall, tall)
            wide = jnp.dot(both[rows, :], pick, preferred_element_type=f32)
            out[n, rows, :] = wide[:, :lanes]
            if n + 1 < count:
                out[n + 1, rows, :] = wide[:, lanes:]


def decay_rows(dec, count):
    return [jnp.broadcast_to(dec[n : n + 1, :], (pieces, lanes)) for n in range(count)]


def ends_kernel(size, rank, rates, mixed, proj, dec, ends, sums, end_total, product_total, *scratch):
    both, eb, fb, rates_apart, mixed_apart = scratch
    steps = rates.shape[0] // pieces
    to_gapped(rates, rates_apart, steps)
    to_gapped(mixed, mixed_apart, steps)

    @pl.when(pl.program_id(0) == 0)
    def _():
        split_proj(proj, both, steps)
        spread(both, eb, rank, size)
        spread(both, fb, 0, 1)

    decays = decay_rows(dec, size)

    def body(i, carry):
        states, total = carry
        rows = pl.ds(pl.multiple_of(i * pieces, pieces), pieces)
        rate = rates_apart[gapped_rows(i, steps), :]
        push = rate * mixed_apart[gapped_rows(i, steps), :]
        rate = rate + fb[0, rows, :]
        out = []
        for n in range(size):
            out.append(jnp.exp2(rate * decays[n]) * states[n] + push * eb[n, rows, :])
        return tuple(out), total + rate

    zero = jnp.zeros((pieces, lanes), f32)
    states, total = lax.fori_loop(0, steps, body, ((zero,) * size, zero), unroll=8)
    for n in range(size):
        ends[n] = states[n]
    sums[...] = total
    reached = ends[:, 0, :]
    for s in range(1, pieces):
        reached = ends[:, s, :] + jnp.exp2(dec[...] * sums[s : s + 1, :]) * reached
    end_total[...] = reached
    product_total[...] = jnp.exp2(dec[...] * jnp.sum(total, axis=0, keepdims=True))


def forward_kernel(size, rank, opening, rates, mixed, proj, dec, gate_in, skip, *rest):
    if opening:
        ends, sums, arriving = rest[:3]
    else:
        begin = rest[0]
    gated, summed, before, final, both, eb, rb, fb, start = rest[-12:-3]
    scanned, rates_apart, mixed_apart = rest[-3:]
    steps = rates.shape[1]
    rates, mixed, proj, gate_in = (
        item.reshape(pieces * steps, lanes) for item in (rates, mixed, proj, gate_in)
    )

    @pl.when(pl.program_id(0) == 0)
    def _():
        split_proj(proj, both, steps)
        spread(both, eb, rank, size)
        spread(both, rb, rank + size, size)
        spread(both, fb, 0, 1)

    to_gapped(rates, rates_apart, steps)
    to_gapped(mixed, mixed_apart, steps)
    decays = decay_rows(dec, size)
    if opening:
        reached = arriving[...]
        for s in range(pieces):
            start[:, s, :] = reached
            reached = ends[:, s, :] + jnp.exp2(dec[...] * sums[s : s + 1, :]) * reached
        begin = start

    def body(i, states):
        rows = pl.ds(pl.multiple_of(i * 2 * pieces, 2 * pieces), 2 * pieces)
        first, second = gapped_rows(2 * i, steps), gapped_rows(2 * i + 1, steps)
        rate0, rate1 = rates_apart[first, :], rates_apart[second, :]
        push0, push1 = rate0 * mixed_apart[first, :], rate1 * mixed_apart[second, :]
        apart = fb[0, rows, :]
        rate0, rate1 = rate0 + apart[:pieces], rate1 + apart[pieces:]
        low = jnp.zeros((pieces, lanes), f32)
        high = low
        out = []
        for n in range(size):
            entry = eb[n, rows, :]
            readout = rb[n, rows, :]
            at_zero = states[n]
            at_one = jnp.exp2(rate0 * decays[n]) * at_zero + push0 * entry[:pieces]
            at_two = jnp.exp2(rate1 * decays[n]) * at_one + push1 * entry[pieces:]
            low = low + readout[:pieces] * at_one
            high = high + readout[pieces:] * at_two
            before[n, rows, :] = jnp.concatenate([at_zero, at_one], axis=0).astype(bf16)
            out.append(at_two)
        scanned[first, :] = low
        scanned[second, :] = high
        return tuple(out)

    states = lax.fori_loop(0, steps // 2, body, tuple(begin[n] for n in range(size)), unroll=2)
    for n in range(size):
        final[n] = states[n]
        last = jnp.concatenate([states[n], states[n]], axis=0).astype(bf16)
        before[n, pl.ds(steps * pieces, 2 * pieces), :] = last

    tall = steps
    for k in range(steps * pieces // tall):
        rows = pl.ds(k * tall, tall)
        total = scanned[gapped_part(k * tall, tall, steps), :] + skip[...] * mixed[rows, :]
        gate = gate_in[rows, :]
        gated[rows, :] = (total * (gate * jax.nn.sigmoid(gate))).astype(bf16)
        summed[rows, :] = total.astype(bf16)


def heads_kernel(size, rank, rates, slope, proj, dec, sums, heads, head_total, *scratch):
    both, rb, fb, rates_apart, slope_apart = scratch
    steps = rates.shape[0] // pieces
    to_gapped(rates, rates_apart, steps)
    to_gapped(slope, slope_apart, steps)

    @pl.when(pl.program_id(0) == 0)
    def _():
        split_proj(proj, both, steps)
        spread(both, rb, rank + size, size)
        spread(both, fb, 0, 1)

    decays = decay_rows(dec, size)

    def body(i, carried):
        step = steps - 1 - i
        rows = pl.ds(pl.multiple_of(step * pieces, pieces), pieces)
        rate = rates_apart[gapped_rows(step, steps), :] + fb[0, rows, :]
        grad = slope_apart[gapped_rows(step, steps), :]
        return tuple(
            (carried[n] + rb[n, rows, :] * grad) * jnp.exp2(rate * decays[n]) for n in range(size)
        )

    zero = jnp.zeros((pieces, lanes), f32)
    carried = lax.fori_loop(0, steps, body, (zero,) * size, unroll=8)
    for n in range(size):
        heads[n] = carried[n]
    reached = heads[:, pieces - 1, :]
    for s in reversed(range(pieces - 1)):
        reached = heads[:, s, :] + jnp.exp2(dec[...] * sums[s : s + 1, :]) * reached
    head_total[...] = reached


def backward_kernel(
    size,
    rank,
    rates,
    mixed,
    slope,
    proj,
    dec,
    heads,
    sums,
    leaving,
    *rest,
):
    stored_states = rest[:chunks]
    skip, step_proj = rest[chunks : chunks + 2]
    rest = rest[chunks + 2 :]
    pre_low, direct, proj_grad, decay_grad, bias_grad = rest[:5]
    both, eb, rb, fb, stop, decay_sum, entry_terms, readout_terms = rest[5:13]
    picks, rate_grad, drive_grad, terms_grad, rates_apart, mixed_apart, slope_apart = rest[13:]
    steps = rates.shape[0] // pieces
    count = steps * pieces
    pair = 2 * pieces
    group = pl.program_id(0)

    @pl.when(group == 0)
    def _():
        split_proj(proj, both, steps)
        spread(both, eb, rank, size)
        spread(both, rb, rank + size, size)
        spread(both, fb, 0, 1)
        proj_grad[...] = jnp.zeros_like(proj_grad)
        target = lax.broadcasted_iota(jnp.int32, (lanes, lanes), 1)
        for n in range(2 * size):
            picks[pl.ds(n * lanes, lanes), :] = (target == rank + n).astype(f32).astype(bf16)

    to_gapped(rates, rates_apart, steps)
    to_gapped(mixed, mixed_apart, steps)
    to_gapped(slope, slope_apart, steps)
    decays = decay_rows(dec, size)
    reached = leaving[...]
    for s in reversed(range(pieces)):
        stop[:, s, :] = reached
        reached = heads[:, s, :] + jnp.exp2(dec[...] * sums[s : s + 1, :]) * reached
    decay_sum[...] = jnp.zeros_like(decay_sum)

    span = steps // 2 // chunks

    def body(fresh, before, offset, i, carried):
        place = span - 1 - i
        at = pl.multiple_of(place * pair, pair)
        stored = pl.ds(at, pair)
        following = pl.ds(at + pair, pair)
        half = offset + place
        rows = pl.ds(pl.multiple_of(half * pair, pair), pair)
        first, second = gapped_rows(2 * half, steps), gapped_rows(2 * half + 1, steps)
        rate0, rate1 = rates_apart[first, :], rates_apart[second, :]
        push0, push1 = rate0 * mixed_apart[first, :], rate1 * mixed_apart[second, :]
        grad0, grad1 = slope_apart[first, :], slope_apart[second, :]
        apart = fb[0, rows, :]
        far0, far1 = rate0 + apart[:pieces], rate1 + apart[pieces:]
        zero = jnp.zeros((pieces, lanes), f32)
        rates0 = rates1 = drives0 = drives1 = zero
        out = []
        for n in range(size):
            entry = eb[n, rows, :]
            readout = rb[n, rows, :]
            state = before[n, stored, :].astype(f32)
            later = before[n, following, :].astype(f32)[:pieces]
            held1 = carried[n] + readout[pieces:] * grad1
            passed1 = held1 * jnp.exp2(far1 * decays[n])
            scaled1 = passed1 * state[pieces:]
            held0 = passed1 + readout[:pieces] * grad0
            passed0 = held0 * jnp.exp2(far0 * decays[n])
            scaled0 = passed0 * state[:pieces]
            rates1 = rates1 + scaled1 * decays[n]
            rates0 = rates0 + scaled0 * decays[n]
            drives1 = drives1 + held1 * entry[pieces:]
            drives0 = drives0 + held0 * entry[:pieces]
            decay_sum[n] += scaled1 * rate1 + scaled0 * rate0
            here = pl.ds(n * lanes, lanes)
            entries = jnp.concatenate([held0 * push0, held1 * push1], axis=0)
            readouts = jnp.concatenate([grad0 * state[pieces:], grad1 * later], axis=0)
            entry_terms[rows, here] = entries if fresh else entry_terms[rows, here] + entries
            readout_terms[rows, here] = (
                readouts if fresh else readout_terms[rows, here] + readouts
            )
            out.append(passed0)
        rate_grad[first, :] = rates0
        rate_grad[second, :] = rates1
        drive_grad[first, :] = drives0
        drive_grad[second, :] = drives1
        return tuple(out)

    def sweep(fresh):
        carried = tuple(stop[n] for n in range(size))
        for k in reversed(range(chunks)):
            step = functools.partial(body, fresh, stored_states[k], k * span)
            carried = lax.fori_loop(0, span, step, carried, unroll=2)

    pl.when(group == 0)(lambda: sweep(True))
    pl.when(group > 0)(lambda: sweep(False))
    decay_grad[...] = jnp.sum(decay_sum[...], axis=1)

    tall = steps
    bias_total = jnp.zeros((1, lanes), f32)
    for k in range(count // tall):
        rows = pl.ds(k * tall, tall)
        apart = gapped_part(k * tall, tall, steps)
        rate, drives = rates[rows, :], drive_grad[apart, :]
        pre = (rate_grad[apart, :] * ln2 + drives * mixed[rows, :]) * (1.0 - jnp.exp(-rate))
        bias_total = bias_total + jnp.sum(pre, axis=0, keepdims=True)
        low = pre.astype(bf16)
        pre_low[rows, :] = low
        direct[rows, :] = drives * rate + skip[...] * slope[rows, :]
        proj_grad[rows, :] += lax.dot_general(
            low, step_proj[...], (((1,), (1,)), ((), ())), preferred_element_type=f32
        )
    bias_grad[...] = bias_total

    @pl.when(group == pl.num_programs(0) - 1)
    def _():
        for k in range(count // tall):
            rows = pl.ds(k * tall, tall)
            terms_grad[rows, :] = jnp.dot(
                entry_terms[rows, :].astype(bf16),
                picks[: size * lanes, :],
                preferred_element_type=f32,
            ) + jnp.dot(
                readout_terms[rows, :].astype(bf16),
                picks[size * lanes :, :],
                preferred_element_type=f32,
            )

        def finish(i, unused):
            rows = pl.ds(pl.multiple_of(i * pieces, pieces), pieces)
            proj_grad[step_rows(i, steps), :] += terms_grad[rows, :]
            return unused

        lax.fori_loop(0, steps, finish, 0)


def scan_calls(count, channels, size, rank):
    groups = channels // lanes
    tall = pl.BlockSpec((count, lanes), lambda g: (0, g))
    fixed = pl.BlockSpec((count, lanes), lambda g: (0, 0))
    small = pl.BlockSpec((size, lanes), lambda g: (0, g))
    ends = pl.BlockSpec((size, pieces, lanes), lambda g: (0, 0, g))
    sums = pl.BlockSpec((pieces, lanes), lambda g: (0, g))
    line = pl.BlockSpec((1, lanes), lambda g: (0, g))
    square = pl.BlockSpec((lanes, lanes), lambda g: (0, g))
    run = count // pieces // chunks
    states = pl.BlockSpec((size, pieces * run + 2 * pieces, lanes), lambda g: (0, 0, g))
    shape = jax.ShapeDtypeStruct
    tall_out = shape((count, channels), f32)
    tall_low = shape((count, channels), bf16)
    small_out = shape((size, channels), f32)
    ends_out = shape((size, pieces, channels), f32)
    sums_out = shape((pieces, channels), f32)
    states_out = shape((size, pieces * run + 2 * pieces, channels), bf16)
    fixed_out = shape((count, lanes), f32)
    line_out = shape((1, channels), f32)
    both = pltpu.VMEM((count, 2 * lanes), bf16)
    wide = pltpu.VMEM((size, count, lanes), f32)
    thin = pltpu.VMEM((1, count, lanes), f32)
    terms = pltpu.VMEM((count, size * lanes), f32)
    edge = pltpu.VMEM((size, pieces, lanes), f32)
    own = pltpu.VMEM((count, lanes), f32)
    apart = pltpu.VMEM((count + pieces * gap, lanes), f32)
    picks = pltpu.VMEM((2 * size * lanes, lanes), bf16)
    work = count * channels * size

    def call(kernel, name, ins, outs, out_shape, scratch, span=groups, aliases={}):
        return pl.pallas_call(
            functools.partial(kernel, size, rank),
            grid=(span,),
            in_specs=ins,
            out_specs=outs,
            out_shape=out_shape,
            scratch_shapes=scratch,
            compiler_params=pltpu.CompilerParams(
                dimension_semantics=("arbitrary",), vmem_limit_bytes=vmem_bytes
            ),
            cost_estimate=pl.CostEstimate(flops=work, bytes_accessed=0, transcendentals=0),
            input_output_aliases=aliases,
            name=name,
        )

    def forward_call(k):
        rows = pl.BlockSpec((pieces, run, lanes), lambda g: (0, k, g))
        same = pl.BlockSpec((pieces, run, lanes), lambda g: (0, k, 0))
        part = pl.BlockSpec((pieces * run, lanes), lambda g: (0, g))
        part_out = shape((pieces * run, channels), bf16)
        wide_part = pltpu.VMEM((size, pieces * run, lanes), f32)
        thin_part = pltpu.VMEM((1, pieces * run, lanes), f32)
        both_part = pltpu.VMEM((pieces * run, 2 * lanes), bf16)
        own_part = pltpu.VMEM((pieces * (run + gap), lanes), f32)
        begin = [ends] if k else [ends, sums, small]

        def kernel(size, rank, *refs):
            forward_kernel(size, rank, k == 0, *refs)

        return call(
            kernel,
            "scan_forward",
            [rows, rows, same, small, rows, line] + begin,
            [part, part, states, ends],
            [part_out, part_out, states_out, ends_out],
            [both_part, wide_part, wide_part, thin_part, edge, own_part, own_part, own_part],
        )

    def backward_call(first, span):
        def moved(spec):
            return pl.BlockSpec(spec.block_shape, lambda g: spec.index_map(g + first))

        ins = [tall, tall, tall, fixed, small, ends, sums, small]
        ins += [states] * chunks + [line, square]
        outs = [tall, tall, fixed, small, line]
        kept = [0, 1, 3, 4] if first else []
        aliases = {len(ins) + i: out for i, out in enumerate(kept)}
        held = [pl.BlockSpec(memory_space=pl.ANY)] * len(kept)

        def kernel(size, rank, *refs):
            refs = refs[: len(ins)] + refs[len(ins) + len(kept) :]
            backward_kernel(size, rank, *refs)

        return call(
            kernel,
            "scan_backward",
            [moved(spec) for spec in ins] + held,
            [moved(spec) for spec in outs],
            [tall_low, tall_out, fixed_out, small_out, line_out],
            [both, wide, wide, thin, edge, edge, terms, terms, picks, apart, apart, own]
            + [apart] * 3,
            span,
            aliases,
        )

    part = max(groups // 3, 1)
    backward_parts = (backward_call(0, part), backward_call(part, groups - part))
    return (
        call(
            ends_kernel,
            "scan_ends",
            [tall, tall, fixed, small],
            [ends, sums, small, small],
            [ends_out, sums_out, small_out, small_out],
            [both, wide, thin, apart, apart],
        ),
        tuple(forward_call(k) for k in range(chunks)),
        call(
            heads_kernel,
            "scan_heads",
            [tall, tall, fixed, small, sums],
            [ends, small],
            [ends_out, small_out],
            [both, wide, thin, apart, apart],
        ),
        backward_parts,
    )


def conv_kernel(width, low, state_proj, direct, inner, rim, taps, bias, mask, *rest):
    inner_low, last, edge, sums, extended, masks = rest[:6]
    slopes = rest[6:]
    count = inner.shape[0]
    tall = min(256, count)
    pad = edge.shape[0]

    @pl.when(pl.program_id(0) == 0)
    def _():
        for k in range(width - 1):
            for at in range(0, count, tall):
                rows = pl.ds(at, tall)
                masks[k, rows, :] = jnp.broadcast_to(mask[rows, k : k + 1], (tall, lanes))

    zeros = jnp.zeros((pad, lanes), f32)
    extended[:pad, :] = rim[...]
    for item in slopes:
        item[:pad, :] = zeros
        item[pl.ds(pad + count, pad), :] = zeros
    for at in range(0, count, tall):
        rows = pl.ds(at, tall)
        extended[pl.ds(pad + at, tall), :] = inner[rows, :].astype(f32)
    totals = [jnp.zeros((1, lanes), f32)] * (width + 1)
    for at in range(0, count, tall):
        rows = pl.ds(at, tall)
        shifted_rows = [extended[pl.ds(pad + at - (width - 1 - k), tall), :] for k in range(width)]
        held = [masks[k, rows, :] for k in range(width - 1)]
        shifted_rows = [item * held[k] if k < width - 1 else item for k, item in enumerate(shifted_rows)]
        convolved = bias[...] + sum(item * taps[k : k + 1, :] for k, item in enumerate(shifted_rows))
        sigma = jax.nn.sigmoid(convolved)
        grad = transposed_right(low[rows, :], state_proj[...]) + direct[rows, :]
        grad = grad * (sigma * (1.0 + convolved * (1.0 - sigma)))
        for k in range(width):
            term = jnp.sum(grad * shifted_rows[k], axis=0, keepdims=True)
            totals[k] = totals[k] + term
            slopes[k][pl.ds(pad + at, tall), :] = grad * held[k] if k < width - 1 else grad
        totals[width] = totals[width] + jnp.sum(grad, axis=0, keepdims=True)
    sums[...] = zeros
    for k in range(width + 1):
        sums[k : k + 1, :] = totals[k]

    def spread_back(at, rows):
        return sum(
            slopes[k][pl.ds(pad + at + width - 1 - k, rows), :] * taps[k : k + 1, :]
            for k in range(width)
        )

    for at in range(0, count, tall):
        inner_low[pl.ds(at, tall), :] = spread_back(at, tall).astype(bf16)
    last[...] = spread_back(count - last.shape[0], last.shape[0])
    edge[...] = spread_back(-pad, pad)


def conv_call(count, channels, width):
    pad = 8
    tall = pl.BlockSpec((count, lanes), lambda g: (0, g))
    fixed = pl.BlockSpec((count, lanes), lambda g: (0, 0))
    eight = pl.BlockSpec((pad, lanes), lambda g: (0, g))
    end = pl.BlockSpec((2 * pad, lanes), lambda g: (0, g))
    shape = jax.ShapeDtypeStruct
    return pl.pallas_call(
        functools.partial(conv_kernel, width),
        grid=(channels // lanes,),
        in_specs=[
            fixed,
            pl.BlockSpec((lanes, lanes), lambda g: (g, 0)),
            tall,
            tall,
            eight,
            pl.BlockSpec((width, lanes), lambda g: (0, g)),
            pl.BlockSpec((1, lanes), lambda g: (0, g)),
            fixed,
        ],
        out_specs=[tall, end, eight, eight],
        out_shape=[
            shape((count, channels), bf16),
            shape((2 * pad, channels), f32),
            shape((pad, channels), f32),
            shape((pad, channels), f32),
        ],
        scratch_shapes=[
            pltpu.VMEM((pad + count, lanes), f32),
            pltpu.VMEM((width - 1, count, lanes), f32),
        ]
        + [pltpu.VMEM((pad + count + pad, lanes), f32)] * width,
        compiler_params=pltpu.CompilerParams(
            dimension_semantics=("arbitrary",), vmem_limit_bytes=vmem_bytes
        ),
        cost_estimate=pl.CostEstimate(flops=count, bytes_accessed=0, transcendentals=0),
        name="conv_backward",
    )


def norm_kernel(rows, gain, out):
    values = rows[...].astype(f32)
    scale = lax.rsqrt(jnp.mean(values * values, axis=-1, keepdims=True) + epsilon)
    out[...] = (values * scale * gain[...].astype(f32)[None, :]).astype(bf16)


def norm_call(count, features):
    tall = min(count, 256)
    return pl.pallas_call(
        norm_kernel,
        grid=(count // tall,),
        in_specs=[
            pl.BlockSpec((tall, features), lambda i: (i, 0)),
            pl.BlockSpec((features,), lambda i: (0,)),
        ],
        out_specs=pl.BlockSpec((tall, features), lambda i: (i, 0)),
        out_shape=jax.ShapeDtypeStruct((count, features), bf16),
        cost_estimate=pl.CostEstimate(
            flops=6 * count * features, bytes_accessed=4 * count * features, transcendentals=count
        ),
        name="norm_rows",
    )


def chained(product, end, by, fill=()):
    inside = jnp.stack([product, end])
    reach = 1
    outside = None
    while reach < lax.axis_size("seq"):
        got = shifted(inside, "seq", by * reach)
        if fill:
            got = after(got, *fill.pop(0)(inside))
        if outside is None:
            outside = got
        else:
            outside = jnp.stack([outside[0] * got[0], outside[1] + outside[0] * got[1]])
        inside = jnp.stack([product * outside[0], end + product * outside[1]])
        reach *= 2
    return outside[1]


def per_device(
    tokens,
    segment_ids,
    first_gain,
    input_proj,
    gate_proj,
    conv_weight,
    conv_bias,
    state_proj,
    step_proj,
    step_bias,
    decay_log,
    skip_gain,
    output_proj,
    second_gain,
    hidden_gate,
    hidden_up,
    hidden_down,
    upstream,
):
    count, features = tokens.shape[1:]
    width = conv_weight.shape[1]
    rank = step_proj.shape[0]
    size = decay_log.shape[1]
    channels = input_proj.shape[1]
    quarter = count // lax.axis_size("chan")
    me = lax.axis_index("chan")
    place = lax.axis_index("seq")
    dp_bits = [("dp", mask) for mask in bits_of("dp")]
    seq_bits = [("seq", mask) for mask in bits_of("seq")]
    shard_bits = dp_bits + seq_bits
    usual = dp_bits + seq_bits[::-1]
    other = seq_bits[-1:] + dp_bits + seq_bits[:-1]
    scan_ends, scan_forward, scan_heads, scan_backward = scan_calls(count, channels, size, rank)

    def block(values, r):
        return lax.dynamic_slice_in_dim(values, (me ^ r) * quarter, quarter)

    shards = lax.axis_size("dp") * lax.axis_size("seq")

    def scatter(order, *values):
        values = [value.reshape(shards, -1, value.shape[-1]) for value in values]
        return Scatter(values, order, shard_bits)

    def side(values, r):
        return lax.dynamic_slice_in_dim(values, ((me >> 1) ^ r) * 2 * quarter, 2 * quarter)

    def of_side(values, r):
        return lax.dynamic_slice_in_dim(values, ((me ^ r) & 1) * quarter, quarter)

    padded_ids = jnp.concatenate([jnp.full((width - 1,), -1, jnp.int32), segment_ids[0]], axis=0)
    window_ids = lax.dynamic_slice_in_dim(padded_ids, place * count, count + width - 1)
    own_ids = window_ids[width - 1 :]
    masks = [
        (window_ids[offset : offset + count] == own_ids).astype(f32)[:, None]
        for offset in range(width)
    ]
    keep = masks[width - 2]

    rows = tokens[0]
    upper = upstream[0]

    def unit_of(values):
        scale = lax.rsqrt(jnp.mean(values * values, axis=-1, keepdims=True) + epsilon)
        return scale, values * scale

    gain_one = first_gain.astype(f32)
    gain_two = second_gain.astype(f32)
    normed = norm_call(count, features)(rows, first_gain)
    inner = matmul(normed, input_proj).astype(bf16)
    rim = shifted(inner[count - width + 1 :], "seq", 1)
    gate_in = matmul(normed, gate_proj)
    extended = jnp.concatenate([rim, after(inner, gate_in)], axis=0).astype(f32)
    taps = conv_weight.astype(f32).T
    convolved = conv_bias.astype(f32) + sum(
        extended[offset : offset + count] * taps[offset] * masks[offset]
        for offset in range(width)
    )
    mixed = jax.nn.silu(convolved).astype(bf16)
    mixed_wide = mixed.astype(f32)
    upper_parts = [lax.optimization_barrier(side(upper, r)) for r in range(2)]
    grad_actives = []

    def upstream_parts(begun):
        grad_actives.extend(
            transposed_right(after(item, begun), hidden_down) for item in upper_parts
        )
        return grad_actives

    projected = chan_total(matmul(mixed, state_proj), distant=upstream_parts)
    step_low = projected[:, :rank].astype(bf16)
    step_pre = matmul(step_low, step_proj) + step_bias.astype(f32)
    rates = jax.nn.softplus(step_pre)
    decay = -jnp.exp(decay_log.astype(f32)).T
    decay_two = decay * log2e
    column = lax.broadcasted_iota(jnp.int32, projected.shape, 1)
    scan_proj = jnp.where(column == 0, (1.0 - keep) * far, projected)

    ends, sums, end_total, product_total = scan_ends(rates, mixed_wide, scan_proj, decay_two)
    arriving = chained(product_total, end_total, 1)
    skip = skip_gain.astype(f32)[None]

    def at_home(blocks, dtype):
        out = jnp.zeros((count, features), dtype)
        for r, item in enumerate(blocks):
            out = lax.dynamic_update_slice_in_dim(out, item.astype(dtype), (me ^ r) * quarter, 0)
        return out

    scan3 = [item.reshape(pieces, -1, item.shape[-1]) for item in (rates, mixed_wide, scan_proj)]
    gate3 = gate_in.reshape(pieces, -1, channels)
    gated, summed, before, unused = scan_forward[0](
        *scan3, decay_two, gate3, skip, ends, sums, arriving
    )

    def output_part(r):
        return matmul(side(gated, r), output_proj).astype(bf16)

    far_part = output_part(1)
    near_part = output_part(0)
    hidden = chan_scatter(lambda r: of_side(far_part if r > 1 else near_part, r))
    rows_own = block(rows, 0).astype(f32)
    upper_own = block(upper, 0).astype(f32)
    hidden_one = rows_own + hidden.total()
    scale_two, unit_two = unit_of(hidden_one)
    normed_own = chan_gather((unit_two * gain_two).astype(bf16))

    def feed_forward(blocks, r):
        normed_part = lax.optimization_barrier(in_order(*blocks))
        gate_ffn = matmul(normed_part, hidden_gate)
        up_ffn = matmul(normed_part, hidden_up)
        gate_act_ffn = jax.nn.silu(gate_ffn)
        active = (gate_act_ffn * up_ffn).astype(bf16)
        grad_active = grad_actives[r]
        grad_gate_ffn = (grad_active * up_ffn * silu_slope(gate_ffn)).astype(bf16)
        grad_up_ffn = (grad_active * gate_act_ffn).astype(bf16)
        grad_normed = (
            transposed_right(grad_gate_ffn, hidden_gate) + transposed_right(grad_up_ffn, hidden_up)
        ).astype(bf16)
        return normed_part, active, grad_gate_ffn, grad_up_ffn, grad_normed

    ffn0 = feed_forward([normed_own.own, normed_own.beside], 0)
    ffn1 = feed_forward(normed_own.blocks(ffn0)[2:], 1)
    back = chan_scatter(lambda r: of_side((ffn1 if r > 1 else ffn0)[4], r))
    normed_two, active, grad_gate_ffn, grad_up_ffn = (
        jnp.concatenate([ffn0[k], ffn1[k]], axis=0) for k in range(4)
    )
    upper_two = jnp.concatenate(upper_parts, axis=0)
    up_weight = transposed_left(after(normed_two, back.middle), grad_up_ffn).astype(bf16)
    gate_weight = transposed_left(after(normed_two, up_weight), grad_gate_ffn).astype(bf16)
    pair_sum = scatter(usual, up_weight, gate_weight)
    sent = pair_sum.send()
    down_sum = scatter(other, transposed_left(after(upper_two, sent), active))
    sent = down_sum.send()
    ffn_sums = [pair_sum, down_sum]
    grad_normed_two = back.total(sent)
    grad_unit_two = grad_normed_two * gain_two
    grad_hidden = upper_own + scale_two * (
        grad_unit_two - unit_two * jnp.mean(grad_unit_two * unit_two, axis=-1, keepdims=True)
    )
    low = chan_gather(grad_hidden.astype(bf16))
    result_parts = [
        matmul(after(item[1], low.own), hidden_down).astype(bf16) for item in (ffn0, ffn1)
    ]
    hidden_blocks = low.blocks(result_parts)
    hidden_low = at_home(hidden_blocks, bf16)
    result_far = after(result_parts[1], hidden_blocks[2])
    results = chan_scatter(lambda r: of_side(result_far if r > 1 else result_parts[0], r))
    gate_act = jax.nn.silu(gate_in)
    grad_gated = transposed_right(hidden_low, output_proj)
    grad_scanned = grad_gated * gate_act
    grad_gate_in = (grad_gated * summed.astype(f32) * silu_slope(gate_in)).astype(bf16)
    skip_grad = jnp.sum(grad_scanned * mixed_wide, axis=0)
    heads, head_total = scan_heads(
        rates, after(grad_scanned, results.middle), scan_proj, decay_two, sums
    )
    head_total = after(head_total, down_sum.got, results.second)

    mixer_weights = []

    def output_weights(begun):
        value = transposed_left(after(hidden_low, begun), gated).astype(bf16)
        mixer_weights.append(value)
        return mixer_weights

    def gate_weights(begun):
        value = transposed_left(normed, after(grad_gate_in, begun)).astype(bf16)
        mixer_weights.append(value)
        return [value, pair_sum.got]

    leaving = chained(product_total, head_total, -1, [output_weights, gate_weights])
    sent = [item.send(leaving) for item in ffn_sums]
    mixer_sum = scatter(usual, *mixer_weights)
    result = chan_gather((hidden_one + results.total(leaving)).astype(bf16))
    step_padded = jnp.pad(step_proj, ((0, 2 * size), (0, 0)))
    scan_inputs = (rates, mixed_wide, grad_scanned, scan_proj, decay_two, heads, sums)
    first_scan, second_scan = scan_backward
    begin = after(leaving, sent, result.own)
    parts = first_scan(*scan_inputs, begin, before, skip, step_padded)
    terms = after(parts[2], pair_sum.got, down_sum.got, result.across)
    sent = [item.send(terms) for item in ffn_sums + [mixer_sum]]
    begin = after(leaving, sent)
    kept = [parts[k] for k in (0, 1, 3, 4)]
    pre_low, direct, more_terms, decay_grad, step_bias_grad = second_scan(
        *scan_inputs, begin, before, skip, step_padded, *kept
    )
    more_terms = after(more_terms, [pair_sum.got, down_sum.got, mixer_sum.got])
    proj_terms = terms + more_terms

    step_weight_grad = []

    gate_terms = []

    def step_weights(begun):
        step_weight_grad.append(transposed_left(after(step_low, begun), pre_low).astype(bf16))
        gate_terms.append(transposed_right(after(grad_gate_in, begun), gate_proj).astype(bf16))
        return step_weight_grad + gate_terms

    grad_projected = chan_total(proj_terms, lambda: [mixer_sum.send()], step_weights).astype(bf16)
    mask = jnp.concatenate(masks[: width - 1], axis=1)
    mask = jnp.pad(mask, ((0, 0), (0, lanes - width + 1)))
    rim_rows = jnp.pad(rim.astype(f32), ((8 - width + 1, 0), (0, 0)))
    inner_low, last_rows, edge, conv_sums = conv_call(count, channels, width)(
        grad_projected,
        state_proj,
        direct,
        inner,
        rim_rows,
        taps,
        conv_bias.astype(f32)[None],
        mask,
    )
    returned = shifted(edge, "seq", -1)
    state_grad = transposed_left(after(grad_projected, edge), mixed).astype(bf16)
    singles = jnp.concatenate([step_bias_grad, skip_grad[None]], axis=0)
    few = jnp.concatenate(
        [conv_sums, decay_grad.reshape(size, channels) * decay, jnp.pad(singles, ((0, 6), (0, 0)))],
        axis=0,
    )
    low_rows = rank // shards
    low_parts = jnp.concatenate(
        [
            state_grad[:rank].reshape(shards, low_rows, channels),
            step_weight_grad[0].reshape(shards, low_rows, channels),
        ],
        axis=1,
    )
    last_rows = last_rows.at[-8:].add(after(returned, low_parts)).astype(bf16)
    inner_low = lax.dynamic_update_slice_in_dim(inner_low, last_rows, count - 16, 0)
    lines = jnp.concatenate([state_grad[rank:], few.astype(bf16)], axis=0)
    lines_used = lines.shape[0]

    lines_used = lines.shape[0]

    def token_part(r, sent):
        return (
            transposed_right(block(after(inner_low, sent), r), input_proj)
            + transposed_right(block(after(grad_gate_in, proj_terms), r), gate_proj)
        ).astype(bf16)

    share = features // shards

    def token_part(r):
        product = transposed_right(side(inner_late if r == 0 else inner_low, r), input_proj)
        return (product + side(gate_terms[0], r).astype(f32)).astype(bf16)

    far_part = token_part(1)
    sent = [mixer_sum.send(far_part)]
    inner_late = after(inner_low, sent)
    near_part = token_part(0)
    tokens_sum = chan_scatter(lambda r: of_side(far_part if r > 1 else near_part, r))
    scale_one, unit_one = unit_of(rows_own)

    input_weight = transposed_left(normed, after(inner_low, tokens_sum.middle)).astype(bf16)
    half_width = channels // 2
    input_blocks = input_weight.reshape(shards, share, channels)
    input_sums = []
    sent = []
    for k, order in ((0, usual), (1, other)):
        columns = slice(k * half_width, (k + 1) * half_width)
        value = jnp.concatenate([input_blocks[:, :, columns], low_parts[:, :, columns]], axis=1)
        value = jnp.pad(value, ((0, 0), (0, -value.shape[1] % 16), (0, 0)))
        input_sums.append(Scatter([value], order, shard_bits))
        sent.append(input_sums[-1].send())
    result_whole = at_home(result.blocks(tokens_sum.middle), bf16)
    grad_normed = tokens_sum.total(sent, result_whole)
    grad_unit_one = grad_normed * gain_one
    tokens_grad = grad_hidden + scale_one * (
        grad_unit_one - unit_one * jnp.mean(grad_unit_one * unit_one, axis=-1, keepdims=True)
    )
    tokens_last = chan_gather(tokens_grad.astype(bf16))
    gains = jnp.concatenate(
        [jnp.sum(grad_normed * unit_one, axis=0), jnp.sum(grad_normed_two * unit_two, axis=0)]
    )
    gains = gains.reshape(-1, channels).astype(bf16)
    gains = sum_step(gains, ("chan", 1))
    sent = [item.send(tokens_last.own) for item in input_sums]
    done = pair_sum.total(tokens_last.own)
    blocks = tokens_last.blocks(done, gains, sent)
    gains = sum_step(gains, ("chan", 2), blocks[2])
    gains = jnp.pad(gains, ((0, -gains.shape[0] % 16), (0, 0)))
    vectors = jnp.concatenate([lines, gains], axis=0)
    while input_sums[0].order:
        sent = [item.send(blocks[2]) for item in input_sums]
    for bit in usual[:-1]:
        vectors = sum_step(vectors, bit)
    early = vectors
    vectors = sum_step(vectors, usual[-1])
    tokens_out = at_home(blocks, f32)
    done += down_sum.total(sent, early) + mixer_sum.total(sent, early)
    input_parts = [item.total(done)[0] for item in input_sums]
    first = share + 2 * low_rows
    gains = vectors[lines_used:].astype(f32)
    shard = lax.axis_index("dp") * lax.axis_size("seq") + place

    def gain_share(k):
        lines = features // channels
        line = gains[k * lines : (k + 1) * lines].reshape(features)
        return lax.dynamic_slice_in_dim(line, shard * share, share)

    input_parts = jnp.concatenate([item[:first] for item in input_parts], axis=1)
    vectors = vectors.astype(f32)
    at = 2 * size
    return (
        result_whole[None],
        tokens_out[None],
        gain_share(0),
        input_parts[:share],
        done[4],
        vectors[at : at + width].T,
        vectors[at + width],
        input_parts[share : share + low_rows].T,
        vectors[:at].T,
        input_parts[share + low_rows :],
        vectors[at + 8 + size],
        vectors[at + 8 : at + 8 + size].T,
        vectors[at + 9 + size],
        done[3].T,
        gain_share(1),
        done[1],
        done[0],
        done[2].T,
    )


def solution(mesh):
    return jax.shard_map(
        per_device,
        mesh=mesh,
        in_specs=(
            P("dp", "seq", None),
            P("dp", None),
            P(),
            P(None, "chan"),
            P(None, "chan"),
            P("chan", None),
            P("chan"),
            P("chan", None),
            P(None, "chan"),
            P("chan"),
            P("chan", None),
            P("chan"),
            P("chan", None),
            P(),
            P(None, "chan"),
            P(None, "chan"),
            P("chan", None),
            P("dp", "seq", None),
        ),
        out_specs=(
            P("dp", "seq", None),
            P("dp", "seq", None),
            P(("dp", "seq")),
            P(("dp", "seq"), "chan"),
            P(("dp", "seq"), "chan"),
            P("chan", None),
            P("chan"),
            P("chan", ("dp", "seq")),
            P("chan", None),
            P(("dp", "seq"), "chan"),
            P("chan"),
            P("chan", None),
            P("chan"),
            P("chan", ("dp", "seq")),
            P(("dp", "seq")),
            P(("dp", "seq"), "chan"),
            P(("dp", "seq"), "chan"),
            P("chan", ("dp", "seq")),
        ),
        check_vma=False,
    )
```
